128 devices in a mesh: band: 2 (over x_hi), dom: 64 (over z, y, x_lo, core).
Axes of the slice: x: 4 (x_hi: 2, x_lo: 2; x = x_hi * 2 + x_lo), y: 4, z: 4, core: 2. Of those that a mesh axis runs over, the one named last changes fastest.
Arguments:
- orbitals: float32 [16, 64, 8, 3072], P('band', 'dom'), may hold values from -6 to 6
- occupation: float32 [16], P('band'), may hold values from 0.2 to 2
- potential: float32 [64, 8, 3072], P('dom'), may hold values from -4 to 1
- projectors: float32 [64, 4, 448, 128], P('dom'), may hold values from -0.2 to 0.2
- energies: float32 [64, 4, 128], P('dom'), may hold values from -10 to 10
- piece_column: int32 [64, 448], P('dom'), may hold values from 0 to 127
- piece_shift: int32 [64, 448], P('dom'), may hold values from 0 to 64
- piece_owner: int32 [64, 448], P('dom'), may hold values from 0 to 8
- piece_atom: int32 [64, 448], P('dom'), may hold values from 0 to 127
- lower_edge: float32 [1], replicated, may hold values from -1 to 1
- upper_edge: float32 [1], replicated, may hold values from 80 to 100
Outputs:
- filtered: float32 [16, 64, 8, 3072], P('band', 'dom')
- density: float32 [64, 8, 3072], P('dom', None, 'band')
The draws below stay inside these ranges and needn't reach their ends.
All inputs are finite; a program needn't handle non-finite values.
Results may differ from the reference program's by a relative error of at most 0.00012.
Values sent between devices are 32-bit elements; how exact they have to be, the bound alone decides.
No kernel may reach another device: no remote copies, remote signals or barrier semaphores. Data moves between devices by JAX's collectives and lax.ppermute only.
A program may use at most 128 MiB of HBM per device.

```python
import math
import jax
import jax.numpy as jnp
import numpy as np
from jax import lax

CX = 8
CY = 16
NZ = 192
OWN_MAX = 128
PIECES = 448
PTS = 128
NPJ = 4
HALO = 6
DEG = 4
PY = 8
PX = 8
DOMAINS = 64
NX = 64
NY = 128
ORBS = 16


def set_ends(result, key, smallest, high):
    spot = [jax.random.randint(jax.random.fold_in(key, axis), (), 0, length) for axis, length in enumerate(result.shape)]
    longest = result.shape.index(max(result.shape))
    beside = spot[:longest] + [(spot[longest] + 1) % result.shape[longest]] + spot[longest + 1:]
    return result.at[tuple(spot)].set(smallest).at[tuple(beside)].set(high)


def steps_of(key, dims, pieces, least, largest):
    level, own = 1.0, jax.random.fold_in(key, 6)
    for position, shards_of in pieces:
        steps = jnp.exp(jax.random.uniform(jax.random.fold_in(own, position), (shards_of,), jnp.float32, least / len(pieces), largest / len(pieces)))
        level = level * jnp.repeat(steps, dims[position] // shards_of).reshape([-1 if axis == position else 1 for axis in range(len(dims))])
    return level


def cumulative_ranks(amount, slope):
    weights = [(1 << 20) // math.isqrt(standing ** slope) + 1 for standing in range(1, amount + 1)]
    scale = 1 + sum(weights) // (1 << 30)
    return np.cumsum(np.array([max(1, weight // scale) for weight in weights]))


def skewed_ids(own_key, shape, count, slope):
    table = cumulative_ranks(count, slope)
    ticket = jax.random.randint(jax.random.fold_in(own_key, 1), shape, 0, int(table[count - 1]))
    standing = jnp.searchsorted(jnp.asarray(table, jnp.int32), ticket, side="right")
    return jax.random.permutation(jax.random.fold_in(own_key, 2), count)[standing].astype(jnp.int32)


def centred(rng, extent, deviation, bound, shards=(), kind=jnp.bfloat16):
    level = steps_of(rng, extent, shards, -0.22, 0.18) if shards else 1.0
    entries = jax.random.normal(rng, extent, jnp.float32) * deviation * level
    return jnp.minimum(jnp.maximum(entries, -bound), bound).astype(kind)


def setup_inputs(seed: int = 0) -> dict:
    key_list = jax.random.split(jax.random.key(seed), 12)
    return {
        "orbitals": centred(key_list[0], (ORBS, DOMAINS, CX, CY * NZ), 1.0, 6.0, ((0, 2), (1, 64)), jnp.float32),
        "occupation": jnp.clip(0.2 + 1.8 * jax.random.uniform(key_list[1], (ORBS,), jnp.float32) ** steps_of(key_list[1], (ORBS,), ((0, 2),), -0.2, 0.2), 0.2, 2.0),
        "potential": jnp.clip(-4.0 + 5.0 * jax.random.uniform(key_list[2], (DOMAINS, CX, CY * NZ), jnp.float32) ** steps_of(key_list[2], (DOMAINS, CX, CY * NZ), ((0, 64),), -0.2, 0.2), -4.0, 1.0),
        "projectors": centred(key_list[3], (DOMAINS, NPJ, PIECES, PTS), 0.033, 0.2, ((0, 64),), jnp.float32),
        "energies": jnp.clip(jax.random.uniform(key_list[4], (DOMAINS, NPJ, OWN_MAX), jnp.float32, -10.0, 10.0) * steps_of(key_list[4], (DOMAINS, NPJ, OWN_MAX), ((0, 64),), -0.4, 0.0), -10.0, 10.0),
        "piece_column": set_ends(jax.random.randint(key_list[5], (DOMAINS, PIECES), 0, CX * CY), jax.random.fold_in(key_list[5], 1), 0, (CX * CY) - 1).astype(jnp.int32),
        "piece_shift": set_ends(jax.random.randint(key_list[6], (DOMAINS, PIECES), 0, NZ - PTS + 1), jax.random.fold_in(key_list[6], 1), 0, NZ - PTS).astype(jnp.int32),
        "piece_owner": set_ends(jax.random.randint(key_list[7], (DOMAINS, PIECES), 0, 9), jax.random.fold_in(key_list[7], 1), 0, 8).astype(jnp.int32),
        "piece_atom": set_ends(skewed_ids(key_list[8], (DOMAINS, PIECES), OWN_MAX, 2), jax.random.fold_in(key_list[8], 3), 0, OWN_MAX - 1).astype(jnp.int32),
        "lower_edge": jnp.clip(jax.random.uniform(key_list[9], (1,), jnp.float32, -1.0, 1.0), -1.0, 1.0),
        "upper_edge": jnp.clip(jax.random.uniform(key_list[10], (1,), jnp.float32, 80.0, 100.0), 80.0, 100.0),
    }


WEIGHTS = (-5369.0 / 1800.0, 12.0 / 7.0, -15.0 / 56.0, 10.0 / 189.0, -1.0 / 112.0, 2.0 / 1925.0, -1.0 / 16632.0)
KINETIC = -0.5 / 0.16


def to_grid(block):
    return block.reshape(PX, PY, CX, CY, NZ).transpose(0, 2, 1, 3, 4).reshape(NX, NY, NZ)


def to_blocks(grid):
    return grid.reshape(PX, CX, PY, CY, NZ).transpose(0, 2, 1, 3, 4).reshape(DOMAINS, CX, CY * NZ)


def reference(orbitals, occupation, potential, projectors, energies, piece_column, piece_shift, piece_owner, piece_atom, lower_edge, upper_edge):
    domain_ids = jnp.arange(DOMAINS, dtype=jnp.int32)
    place_x = domain_ids // PY
    place_y = domain_ids % PY
    step_x = piece_owner // 3 - 1
    step_y = piece_owner % 3 - 1
    owner = ((place_x[:, None] + step_x) % PX) * PY + (place_y[:, None] + step_y) % PY
    atom_ids = (owner * OWN_MAX + piece_atom).reshape(-1).astype(jnp.int32)
    energy_all = jnp.transpose(energies, (1, 0, 2)).reshape(NPJ, DOMAINS * OWN_MAX)
    depth_ids = jnp.arange(NZ, dtype=jnp.int32)
    offsets = depth_ids[None, None, :] - piece_shift[:, :, None]
    valid = (offsets >= 0) & (offsets < PTS)
    safe = jnp.clip(offsets, 0, PTS - 1).astype(jnp.int32)
    placed = jnp.take_along_axis(projectors, jnp.broadcast_to(safe[:, None], (DOMAINS, NPJ, PIECES, NZ)), axis=3)
    expanded = jnp.where(valid[:, None], placed, jnp.float32(0.0))
    column_ids = piece_column.astype(jnp.int32)
    row_ids = jnp.broadcast_to(domain_ids[:, None], (DOMAINS, PIECES))
    center = (upper_edge[0] + lower_edge[0]) / 2.0
    half = (upper_edge[0] - lower_edge[0]) / 2.0

    def apply(block):
        grid = to_grid(block)
        lap = 3.0 * WEIGHTS[0] * grid
        for offset in range(1, HALO + 1):
            for axis_id in range(3):
                lap = lap + WEIGHTS[offset] * (jnp.roll(grid, -offset, axis_id) + jnp.roll(grid, offset, axis_id))
        columns = block.reshape(DOMAINS, CX * CY, NZ)
        picked = jnp.take_along_axis(columns, column_ids[:, :, None], axis=1)
        partial_value = jnp.einsum("dpz,djpz->jdp", picked, expanded, precision=lax.Precision.HIGHEST).reshape(NPJ, DOMAINS * PIECES)
        coef = jnp.zeros((NPJ, DOMAINS * OWN_MAX), jnp.float32).at[:, atom_ids].add(partial_value)
        scaled = (coef * energy_all)[:, atom_ids].reshape(NPJ, DOMAINS, PIECES)
        spread = jnp.einsum("jdp,djpz->dpz", scaled, expanded, precision=lax.Precision.HIGHEST)
        beyond = jnp.zeros((DOMAINS, CX * CY, NZ), jnp.float32).at[row_ids, column_ids].add(spread).reshape(DOMAINS, CX, CY * NZ)
        return KINETIC * to_blocks(lap) + potential * block + beyond

    def one_orbital(total, inputs):
        block, weight = inputs
        before = block
        after = (apply(block) - center * block) / half
        for level in range(1, DEG):
            upcoming = 2.0 * (apply(after) - center * after) / half - before
            before, after = after, upcoming
        return total + weight * after * after, after

    density, filtered = lax.scan(one_orbital, jnp.zeros((DOMAINS, CX, CY * NZ), jnp.float32), (orbitals, occupation))
    return filtered, density
```

```python
import functools

import jax
import jax.numpy as jnp
import numpy as np
from jax import lax
from jax.experimental import pallas as pl
from jax.experimental.pallas import tpu as pltpu
from jax.sharding import PartitionSpec as P

NZ = 192
HALO = 6
DEG = 4
CX = 8
CY = 16
WX = 2 * CX
COLS = WX * CY
ORB = 4
NPJ = 4
PIECES = 448
ALL = 2 * PIECES
PTS = 128
SLOTS = 128
ROWS = ORB * NPJ
PACKED = 144
TAIL = NZ - PACKED
LANES = 128
EDGE = HALO * 16
EDGES = ORB * PACKED
CODES = 16
HALF = CODES * ROWS // 2
CHUNKS = ((0, 256), (256, 256), (512, 256), (768, 128))

WEIGHTS = (
    -5369.0 / 1800.0,
    12.0 / 7.0,
    -15.0 / 56.0,
    10.0 / 189.0,
    -1.0 / 112.0,
    2.0 / 1925.0,
    -1.0 / 16632.0,
)
KINETIC = -0.5 / 0.16
F32 = jnp.float32
BF16 = jnp.bfloat16


def coupling(steps):
    reach = np.abs(steps)
    near = (reach >= 1) & (reach <= HALO)
    table = np.array(WEIGHTS) * KINETIC
    return np.where(near, table[np.minimum(reach, HALO)], 0.0)


def stencil_matrices():
    col = np.arange(COLS)
    x, y = col // CY, col % CY
    same_x = x[:, None] == x[None, :]
    same_y = y[:, None] == y[None, :]
    own = np.where(same_y, coupling(x[None, :] - x[:, None]), 0.0)
    own = own + np.where(same_x, coupling(y[None, :] - y[:, None]), 0.0)
    lane = np.arange(LANES)
    used = (lane < EDGE)[:, None]
    parts = []
    for start in (-HALO, WX):
        hx, hy = start + lane // CY, lane % CY
        parts.append(np.where(used & (hy[:, None] == y[None, :]), coupling(x[None, :] - hx[:, None]), 0.0))
    for start in (-HALO, CY):
        hy, hx = start + lane // WX, lane % WX
        parts.append(np.where(used & (hx[:, None] == x[None, :]), coupling(y[None, :] - hy[:, None]), 0.0))
    halo = np.concatenate(parts, axis=0)
    depth = np.arange(NZ)
    apart = (depth[None, :] - depth[:, None] + NZ // 2) % NZ - NZ // 2
    ring = coupling(apart)
    picks = []
    for start in (0, CY - HALO):
        hy, hx = start + lane // WX, lane % WX
        picks.append(np.where(used.T & (col[:, None] == (hx * CY + hy)[None, :]), 1.0, 0.0))
    edge = np.concatenate(picks, axis=1)
    return own, halo, ring, edge


def two_parts(matrix):
    high = np.asarray(matrix, np.float32).astype(jnp.bfloat16)
    low = (np.asarray(matrix, np.float64) - high.astype(np.float64)).astype(np.float32).astype(jnp.bfloat16)
    return high, low


def split(value):
    high = value.astype(BF16)
    low = (value - high.astype(F32)).astype(BF16)
    return high, low


def mul(left, right):
    return jnp.dot(left, right, preferred_element_type=F32)


def mul_t(left, right):
    return lax.dot_general(left, right, (((1,), (1,)), ((), ())), preferred_element_type=F32)


def pack_edge(value):
    main = value[:PACKED]
    lane = lax.broadcasted_iota(jnp.int32, (TAIL, LANES), 1)
    rows = []
    for k in range(3):
        tail = pltpu.roll(value[PACKED:], (EDGE - 32 * k) % LANES, 1)
        rows.append(jnp.where(lane < EDGE, main[k * TAIL : (k + 1) * TAIL], tail))
    return jnp.concatenate(rows, axis=0)


def unpack_edge(value):
    lane = lax.broadcasted_iota(jnp.int32, (TAIL, LANES), 1)
    tail = jnp.zeros((TAIL, LANES), F32)
    for k in range(3):
        moved = pltpu.roll(value[k * TAIL : (k + 1) * TAIL], (32 * k - EDGE) % LANES, 1)
        tail = jnp.where((lane >= 32 * k) & (lane < 32 * k + 32), moved, tail)
    return jnp.concatenate([value, tail], axis=0)


def emit_edges(fields, below_inner, edge_ref, xl_ref, xh_ref, inner_ref, outer_ref):
    for o in range(ORB):
        value = fields[o]
        high, low = split(value)
        picked = mul(high, edge_ref[...]) + mul(low, edge_ref[...])
        xl_ref[o] = pack_edge(value[:, :LANES])
        xh_ref[o] = pack_edge(pltpu.roll(value[:, LANES:], LANES - 32, 1))
        bottom, top = pack_edge(picked[:, :LANES]), pack_edge(picked[:, LANES:])
        inner_ref[o] = jnp.where(below_inner, bottom, top)
        outer_ref[o] = jnp.where(below_inner, top, bottom)


def to_columns(source, near, far):
    for y in range(CY):
        at = y * NZ
        near[pl.ds(y, CX, stride=CY), :] = source[:, at : at + LANES]
        tail = source[:, at + LANES : at + NZ]
        far[pl.ds(y, CX, stride=CY), :] = jnp.concatenate([tail, jnp.zeros((CX, 2 * LANES - NZ), F32)], axis=1)
    return jnp.concatenate([jnp.transpose(near[...]), jnp.transpose(far[...])[: NZ - LANES]], axis=0)


def from_columns(value, near, far):
    near[...] = jnp.transpose(value[:LANES])
    far[...] = jnp.transpose(jnp.concatenate([value[LANES:], jnp.zeros((2 * LANES - NZ, LANES), F32)], axis=0))
    for y in range(0, CY, 2):
        lines = []
        for at in (y, y + 1):
            lines.append(near[pl.ds(at, CX, stride=CY), :])
            lines.append(far[pl.ds(at, CX, stride=CY), :][:, : NZ - LANES])
        yield y * NZ, jnp.concatenate(lines, axis=1)


def turn_kernel(place, raw, local, energy, keep, going, misc, near, far):
    for o in range(ORB):
        keep[o] = to_columns(raw.at[place[0] * ORB + o], near, far)
        going[o] = to_columns(raw.at[(1 - place[0]) * ORB + o], near, far)
    misc[:NZ] = to_columns(local, near, far)
    misc[NZ : NZ + NPJ] = energy[...]
    misc[NZ + NPJ :] = jnp.zeros((4, LANES), F32)


def start_kernel(place, keep, came, misc, misc_came, edge, field, pot, xl, xh, inner, outer):
    mine = pl.multiple_of(place[0] * LANES, LANES)
    other = pl.multiple_of((1 - place[0]) * LANES, LANES)
    for at, source, local in ((mine, keep, misc), (other, came, misc_came)):
        for o in range(ORB):
            field[o, :, pl.ds(at, LANES)] = source[o]
        pot[:, pl.ds(at, LANES)] = local[:NZ]
    emit_edges([field[o] for o in range(ORB)], place[1] == 1, edge, xl, xh, inner, outer)


def prepare_kernel(index, own, came, placed):
    for j in range(NPJ):
        both = jnp.concatenate([own[j], came[j]], axis=0)
        for k in range(ALL // LANES):
            block = jnp.transpose(both[k * LANES : (k + 1) * LANES])
            block = jnp.concatenate([block, jnp.zeros((NZ - PTS, LANES), F32)], axis=0)
            shift = index[1:2, k * LANES : (k + 1) * LANES]
            for bit in (64, 32, 16, 8, 4, 2, 1):
                block = jnp.where((shift & bit) != 0, pltpu.roll(block, bit, 0), block)
            placed[j, :, k * LANES : (k + 1) * LANES] = block


def column_hot(index, at, wide):
    where = lax.broadcasted_iota(jnp.int32, (COLS, wide), 0) == index[0:1, at : at + wide]
    return where.astype(F32).astype(BF16)


def atom_hot(index):
    where = lax.broadcasted_iota(jnp.int32, (SLOTS, ALL), 0) == index[3:4, :]
    return where.astype(F32).astype(BF16)


def table_kernel(index, field, placed, inner, message, partial):
    for o in range(ORB):
        message[o * PACKED : (o + 1) * PACKED] = inner[o]
    parts = [split(field[o]) for o in range(ORB)]
    both = jnp.concatenate([jnp.concatenate(p, axis=1) for p in parts], axis=0)
    for at, wide in CHUNKS:
        hot = column_hot(index, at, wide)
        picked = mul(both, jnp.concatenate([hot, hot], axis=0))
        for j in range(NPJ):
            values = placed[j, :, at : at + wide]
            for o in range(ORB):
                term = picked[o * NZ : (o + 1) * NZ] * values
                partial[o * NPJ + j : o * NPJ + j + 1, at : at + wide] = jnp.sum(term, axis=0, keepdims=True)
    value = partial[...]
    codes = index[2:3, :]
    spread = jnp.concatenate([jnp.where(codes == code, value, 0.0) for code in range(CODES)], axis=0)
    high, low = split(spread)
    atoms = atom_hot(index)
    message[EDGES:] = mul_t(high, atoms) + mul_t(low, atoms)


def pair_kernel(place, first, came, outer, xl, xh, message, xl_out, xh_out):
    for o in range(ORB):
        message[o * PACKED : (o + 1) * PACKED] = outer[o]
    at = pl.multiple_of(EDGES + place[1] * HALF, 8)
    message[EDGES:] = first[pl.ds(at, HALF)] + came[pl.ds(at, HALF)]


def sum_kernel(mine, came, low, high):
    total = mine[EDGES:] + came[EDGES:]
    step = 2 * ROWS
    for q in range(2):
        low[q * step : (q + 1) * step] = total[2 * q * step : (2 * q + 1) * step]
        high[q * step : (q + 1) * step] = total[(2 * q + 1) * step : (2 * q + 2) * step]


def scale_of(first, edges):
    width = jnp.full((8, LANES), (edges[0] - edges[1]) / 2.0, F32)
    return ((1.0 if first else 2.0) / width)[0:1, 0:1]


def total_kernel(first, edges, low, high, below, above, energy, out):
    step = 2 * ROWS
    blocks = []
    for q in range(2):
        at = slice(q * step, (q + 1) * step)
        blocks.append(low[at] + below[at])
        blocks.append(high[at] + above[at])
    out[...] = jnp.concatenate(blocks, axis=0) * energy[...] * scale_of(first, edges)


def local_kernel(first, edges, field, before, pot, own_w, ring_w, out):
    center = (edges[0] + edges[1]) / 2.0
    scale = scale_of(first, edges)
    diagonal = pot[...] + (3.0 * WEIGHTS[0] * KINETIC - center)
    for o in range(ORB):
        value = field[o]
        high, low = split(value)
        across = mul(jnp.concatenate([high, low, high], axis=1), own_w[...])
        along = mul(ring_w[...], jnp.concatenate([high, low, high], axis=0))
        total = scale * (across + along + diagonal * value)
        out[o] = total if first else total - before[o]


def halo_kernel(first, place, edges, acc, xl, xh, inner, outer, halo_w, out):
    scale = scale_of(first, edges)
    below_inner = place[1] == 1
    for o in range(ORB):
        inside = unpack_edge(inner[o * PACKED : (o + 1) * PACKED])
        outside = unpack_edge(outer[o * PACKED : (o + 1) * PACKED])
        bottom = jnp.where(below_inner, inside, outside)
        top = jnp.where(below_inner, outside, inside)
        line = jnp.concatenate([unpack_edge(xl[o]), unpack_edge(xh[o]), bottom, top], axis=1)
        high, low = split(line)
        out[o] = acc[o] + scale * mul(jnp.concatenate([high, low, high], axis=1), halo_w[...])


def update_kernel(last, place, index, acc, mine, came, placed, *rest):
    second = place[1] == 1
    total = jnp.concatenate(
        [jnp.where(second, came[...], mine[...]), jnp.where(second, mine[...], came[...])], axis=0
    )
    atoms = atom_hot(index)
    spread = mul(jnp.concatenate(split(total), axis=1), jnp.concatenate([atoms, atoms], axis=0))
    codes = index[2:3, :]
    coefs = jnp.zeros((ROWS, ALL), F32)
    for code in range(CODES):
        coefs = jnp.where(codes == code, spread[code * ROWS : (code + 1) * ROWS], coefs)
    total = jnp.zeros((ORB * NZ, COLS), F32)
    for at, wide in CHUNKS:
        hot = column_hot(index, at, wide)
        lines = []
        for o in range(ORB):
            line = coefs[o * NPJ : o * NPJ + 1, at : at + wide] * placed[0, :, at : at + wide]
            for j in range(1, NPJ):
                row = o * NPJ + j
                line = line + coefs[row : row + 1, at : at + wide] * placed[j, :, at : at + wide]
            lines.append(jnp.concatenate(split(line), axis=1))
        total = total + mul_t(jnp.concatenate(lines, axis=0), jnp.concatenate([hot, hot], axis=1))
    fields = [acc[o] + total[o * NZ : (o + 1) * NZ] for o in range(ORB)]
    if not last:
        edge, field, xl, xh, inner, outer = rest
        for o in range(ORB):
            field[o] = fields[o]
        emit_edges(fields, second, edge, xl, xh, inner, outer)
        return
    weights, kept, sent, quarter, across_x, across_band, across_both, near, far, hold, plane = rest
    dens = jnp.zeros((NZ, COLS), F32)
    for o in range(ORB):
        hold[o] = fields[o]
        dens = dens + weights[place[0] * ORB + o] * fields[o] * fields[o]
    hold[ORB] = dens
    mine_at = pl.multiple_of(place[0] * LANES, LANES)
    other_at = pl.multiple_of((1 - place[0]) * LANES, LANES)
    span = CY * NZ // 2
    here = pl.multiple_of(place[2] * span, LANES)
    there = pl.multiple_of((1 - place[2]) * span, LANES)
    for at, out, same, opposite in (
        (other_at, sent, across_x, across_both),
        (mine_at, kept, quarter, across_band),
    ):
        for o in range(ORB + 1):
            for spot, pair in from_columns(hold[o, :, pl.ds(at, LANES)], near, far):
                if o < ORB:
                    out[o, :, spot : spot + 2 * NZ] = pair
                else:
                    plane[:, spot : spot + 2 * NZ] = pair
        same[...] = plane[:, pl.ds(here, span)]
        opposite[...] = plane[:, pl.ds(there, span)]


VM = pl.BlockSpec(memory_space=pltpu.VMEM)
SM = pl.BlockSpec(memory_space=pltpu.SMEM)
ANY = pl.BlockSpec(memory_space=pl.ANY)


def call(kernel, in_specs, shapes, args, scratch=(), flops=10**8, name=None, passed=0):
    single = isinstance(shapes, tuple)
    outs = [shapes] if single else list(shapes)
    plain = len(outs) - passed
    result = pl.pallas_call(
        kernel,
        out_shape=[jax.ShapeDtypeStruct(s, F32) for s in outs],
        in_specs=in_specs,
        out_specs=[VM] * plain + [ANY] * passed,
        scratch_shapes=list(scratch),
        input_output_aliases={len(args) - passed + k: plain + k for k in range(passed)},
        compiler_params=pltpu.CompilerParams(vmem_limit_bytes=48 * 1024 * 1024),
        cost_estimate=pl.CostEstimate(flops=flops, bytes_accessed=4 * 10**6, transcendentals=0),
        name=name,
    )(*args)
    return result[0] if single else result


def send(value, pairs):
    return lax.ppermute(value, "dom", pairs)


def along_z(step):
    return [(d, (d + 16 * step) % 64) for d in range(64)]


def outward(d):
    y = d % 8
    return d // 8 * 8 + ((y - 1) % 8 if y % 2 == 0 else (y + 1) % 8)


SWAP = [(d, d ^ 8) for d in range(64)]
CORES = [(d, d ^ 1) for d in range(64)]
OUTER = [(d, outward(d)) for d in range(64)]


def body(
    orbitals,
    occupation,
    potential,
    projectors,
    energies,
    piece_column,
    piece_shift,
    piece_owner,
    piece_atom,
    lower_edge,
    upper_edge,
):
    own_m, halo_m, ring_m, edge_m = stencil_matrices()
    a, b = two_parts(own_m)
    own_w = jnp.asarray(np.concatenate([a, a, b], axis=0))
    a, b = two_parts(halo_m)
    halo_w = jnp.asarray(np.concatenate([a, a, b], axis=0))
    a, b = two_parts(ring_m)
    ring_w = jnp.asarray(np.concatenate([a, a, b], axis=1))
    edge_w = jnp.asarray(edge_m.astype(np.float32).astype(jnp.bfloat16))

    here = lax.axis_index("dom")
    side = (here // 8 % 2).astype(jnp.int32)
    core = (here % 2).astype(jnp.int32)
    place = jnp.stack([side, core, lax.axis_index("band").astype(jnp.int32)])
    edges = jnp.concatenate([upper_edge, lower_edge])
    packed = (ORB, PACKED, LANES)
    grid = (ORB, NZ, COLS)
    stage = [pltpu.VMEM((LANES, LANES), F32)] * 2

    keep, going, misc = call(
        turn_kernel,
        [SM] + [VM] * 3,
        [(ORB, NZ, LANES)] * 2 + [(NZ + 8, LANES)],
        (place, orbitals[:, 0], potential[0], energies[0]),
        stage,
        name="turn",
    )
    came = send(going, SWAP)
    misc_came = send(misc, SWAP)
    ints = jnp.stack([piece_column[0], piece_shift[0], piece_owner[0], piece_atom[0]])
    ints_came = send(ints, SWAP)
    proj_came = send(projectors[0], SWAP)

    raw = jnp.concatenate([ints, ints_came], axis=1)
    sub = jnp.where(jnp.arange(ALL) < PIECES, side, 1 - side).astype(jnp.int32)
    step_x = raw[2] // 3 - 1
    step_y = raw[2] % 3 - 1
    codes = (step_y + 1 + core) * 4 + sub + step_x + 1
    index = jnp.stack([sub * LANES + raw[0], raw[1], codes, raw[3]])

    pair = jnp.stack([energies[0], misc_came[NZ : NZ + NPJ]])
    pair = jnp.where(side == 0, pair, pair[::-1])
    outer_pair = send(pair, OUTER)
    two = jnp.where(core == 0, jnp.stack([outer_pair, pair]), jnp.stack([pair, outer_pair]))
    below_e = send(two[:, 1], along_z(1))
    above_e = send(two[:, 0], along_z(-1))
    around = jnp.concatenate([below_e[:, None], two, above_e[:, None]], axis=1)
    energy = jnp.broadcast_to(around[:, :, None], (2, 4, ORB, NPJ, LANES)).reshape(HALF, LANES)

    field, pot, xl, xh, inner, outer = call(
        start_kernel,
        [SM] + [VM] * 5,
        [grid, (NZ, COLS)] + [packed] * 4,
        (place, keep, came, misc, misc_came, edge_w),
        name="start",
    )
    placed = call(prepare_kernel, [VM] * 3, (NPJ, NZ, ALL), (index, projectors[0], proj_came), name="prepare")

    before = field
    for level in range(DEG):
        first, last = level == 0, level == DEG - 1
        message = call(
            table_kernel,
            [VM] * 4,
            (EDGES + CODES * ROWS, LANES),
            (index, field, placed, inner),
            [pltpu.VMEM((ROWS, ALL), F32)],
            name="table",
        )
        message_came = send(message, CORES)
        second, xl, xh = call(
            pair_kernel,
            [SM, VM, VM, VM, ANY, ANY],
            [(EDGES + HALF, LANES), packed, packed],
            (place, message, message_came, outer, xl, xh),
            flops=10**6,
            name="pair",
            passed=2,
        )
        second_came = send(second, OUTER)
        xl_came = send(xh, along_z(1))
        xh_came = send(xl, along_z(-1))
        acc = call(
            functools.partial(local_kernel, first),
            [SM] + [VM] * 5,
            grid,
            (edges, field, before, pot, own_w, ring_w),
            name="local",
        )
        low, high = call(
            sum_kernel, [VM] * 2, [(HALF // 2, LANES)] * 2, (second, second_came), flops=10**6, name="sums"
        )
        below = send(high, along_z(1))
        above = send(low, along_z(-1))
        acc = call(
            functools.partial(halo_kernel, first),
            [SM, SM] + [VM] * 6,
            grid,
            (place, edges, acc, xl_came, xh_came, message_came, second_came, halo_w),
            name="halo",
        )
        total = call(
            functools.partial(total_kernel, first),
            [SM] + [VM] * 5,
            (HALF, LANES),
            (edges, low, high, below, above, energy),
            flops=10**6,
            name="totals",
        )
        total_came = send(total, CORES)
        args = (place, index, acc, total, total_came, placed)
        if not last:
            before, (field, xl, xh, inner, outer) = field, call(
                functools.partial(update_kernel, last),
                [SM] + [VM] * 6,
                [grid] + [packed] * 4,
                args + (edge_w,),
                name="update",
            )
        else:
            flat = (ORB, CX, CY * NZ)
            part = (CX, CY * NZ // 2)
            mine, other, quarter, across_x, across_band, across_both = call(
                functools.partial(update_kernel, last),
                [SM] + [VM] * 5 + [SM],
                [flat, flat] + [part] * 4,
                args + (occupation,),
                stage + [pltpu.VMEM((ORB + 1, NZ, COLS), F32), pltpu.VMEM((CX, CY * NZ), F32)],
                name="finish",
            )
    swapped = send(other, SWAP)
    both = [(d, d ^ 72) for d in range(128)]
    density = (
        quarter
        + send(across_x, SWAP)
        + lax.ppermute(across_band, "band", [(0, 1), (1, 0)])
        + lax.ppermute(across_both, ("band", "dom"), both)
    )
    filtered = jnp.where(
        side == 0, jnp.concatenate([mine, swapped], axis=0), jnp.concatenate([swapped, mine], axis=0)
    )
    return filtered[:, None], density[None]


def solution(mesh):
    in_specs = (
        P("band", "dom", None, None),
        P("band"),
        P("dom", None, None),
        P("dom", None, None, None),
        P("dom", None, None),
        P("dom", None),
        P("dom", None),
        P("dom", None),
        P("dom", None),
        P(),
        P(),
    )
    out_specs = (P("band", "dom", None, None), P("dom", None, "band"))
    return jax.shard_map(body, mesh=mesh, in_specs=in_specs, out_specs=out_specs, check_vma=False)
```

```python
import functools

import jax
import jax.numpy as jnp
import numpy as np
from jax import lax
from jax.experimental import pallas as pl
from jax.experimental.pallas import tpu as pltpu
from jax.sharding import PartitionSpec as P

NZ = 192
HALO = 6
DEG = 4
CX = 8
CY = 16
WX = 2 * CX
COLS = WX * CY
ORB = 4
NPJ = 4
PIECES = 448
ALL = 2 * PIECES
PTS = 128
SLOTS = 128
ROWS = ORB * NPJ
PACKED = 144
TAIL = NZ - PACKED
LANES = 128
EDGE = HALO * 16
OWN = 512
CODES = 16
HALF = CODES * ROWS // 2
CHUNKS = ((0, 256), (256, 256), (512, 256), (768, 128))

WEIGHTS = (
    -5369.0 / 1800.0,
    12.0 / 7.0,
    -15.0 / 56.0,
    10.0 / 189.0,
    -1.0 / 112.0,
    2.0 / 1925.0,
    -1.0 / 16632.0,
)
KINETIC = -0.5 / 0.16
F32 = jnp.float32
BF16 = jnp.bfloat16


def coupling(steps):
    reach = np.abs(steps)
    near = (reach >= 1) & (reach <= HALO)
    table = np.array(WEIGHTS) * KINETIC
    return np.where(near, table[np.minimum(reach, HALO)], 0.0)


def stencil_matrices():
    col = np.arange(COLS)
    x, y = col // CY, col % CY
    same_x = x[:, None] == x[None, :]
    same_y = y[:, None] == y[None, :]
    own = np.where(same_y, coupling(x[None, :] - x[:, None]), 0.0)
    own = own + np.where(same_x, coupling(y[None, :] - y[:, None]), 0.0)
    lane = np.arange(LANES)
    used = (lane < EDGE)[:, None]
    parts = []
    for start in (-HALO, WX):
        hx, hy = start + lane // CY, lane % CY
        parts.append(np.where(used & (hy[:, None] == y[None, :]), coupling(x[None, :] - hx[:, None]), 0.0))
    for start in (-HALO, CY):
        hy, hx = start + lane // WX, lane % WX
        parts.append(np.where(used & (hx[:, None] == x[None, :]), coupling(y[None, :] - hy[:, None]), 0.0))
    halo = np.concatenate(parts, axis=0)
    depth = np.arange(NZ)
    apart = (depth[None, :] - depth[:, None] + NZ // 2) % NZ - NZ // 2
    ring = coupling(apart)
    picks = []
    for start in (0, CY - HALO):
        hy, hx = start + lane // WX, lane % WX
        picks.append(np.where(used.T & (col[:, None] == (hx * CY + hy)[None, :]), 1.0, 0.0))
    edge = np.concatenate(picks, axis=1)
    return own, halo, ring, edge


def two_parts(matrix):
    high = np.asarray(matrix, np.float32).astype(jnp.bfloat16)
    low = (np.asarray(matrix, np.float64) - high.astype(np.float64)).astype(np.float32).astype(jnp.bfloat16)
    return high, low


def split(value):
    high = value.astype(BF16)
    low = (value - high.astype(F32)).astype(BF16)
    return high, low


def mul(left, right):
    return jnp.dot(left, right, preferred_element_type=F32)


def mul_t(left, right):
    return lax.dot_general(left, right, (((1,), (1,)), ((), ())), preferred_element_type=F32)


def pack_edge(value):
    main = value[:PACKED]
    lane = lax.broadcasted_iota(jnp.int32, (TAIL, LANES), 1)
    rows = []
    for k in range(3):
        tail = pltpu.roll(value[PACKED:], (EDGE - 32 * k) % LANES, 1)
        rows.append(jnp.where(lane < EDGE, main[k * TAIL : (k + 1) * TAIL], tail))
    return jnp.concatenate(rows, axis=0)


def unpack_edge(value):
    lane = lax.broadcasted_iota(jnp.int32, (TAIL, LANES), 1)
    tail = jnp.zeros((TAIL, LANES), F32)
    for k in range(3):
        moved = pltpu.roll(value[k * TAIL : (k + 1) * TAIL], (32 * k - EDGE) % LANES, 1)
        tail = jnp.where((lane >= 32 * k) & (lane < 32 * k + 32), moved, tail)
    return jnp.concatenate([value, tail], axis=0)


def emit_edges(fields, below_inner, edge_ref, xl_ref, xh_ref, inner_ref, outer_ref):
    for o in range(ORB):
        value = fields[o]
        high, low = split(value)
        picked = mul(high, edge_ref[...]) + mul(low, edge_ref[...])
        xl_ref[o] = pack_edge(value[:, :LANES])
        xh_ref[o] = pack_edge(pltpu.roll(value[:, LANES:], LANES - 32, 1))
        bottom, top = pack_edge(picked[:, :LANES]), pack_edge(picked[:, LANES:])
        inner_ref[o] = jnp.where(below_inner, bottom, top)
        outer_ref[o] = jnp.where(below_inner, top, bottom)


def to_columns(source, near, far):
    for y in range(CY):
        at = y * NZ
        line = source(at)
        near[pl.ds(y, CX, stride=CY), :] = line[:, :LANES]
        tail = line[:, LANES:]
        far[pl.ds(y, CX, stride=CY), :] = jnp.concatenate([tail, jnp.zeros((CX, 2 * LANES - NZ), F32)], axis=1)
    return jnp.concatenate([jnp.transpose(near[...]), jnp.transpose(far[...])[: NZ - LANES]], axis=0)


def from_columns(value, near, far):
    near[...] = jnp.transpose(value[:LANES])
    far[...] = jnp.transpose(jnp.concatenate([value[LANES:], jnp.zeros((2 * LANES - NZ, LANES), F32)], axis=0))
    for y in range(0, CY, 2):
        lines = []
        for at in (y, y + 1):
            lines.append(near[pl.ds(at, CX, stride=CY), :])
            lines.append(far[pl.ds(at, CX, stride=CY), :][:, : NZ - LANES])
        yield y * NZ, jnp.concatenate(lines, axis=1)


def flag(params, row):
    return params[row : row + 1, :] == 1.0


def turn_kernel(params, raw, local, energy, index, keep, going, misc, near, far):
    upper = params[0:1, 0:1] == 1.0
    for o in range(ORB):
        def kept(at, o=o):
            return jnp.where(upper, raw[ORB + o, :, at : at + NZ], raw[o, :, at : at + NZ])

        def sent(at, o=o):
            return jnp.where(upper, raw[o, :, at : at + NZ], raw[ORB + o, :, at : at + NZ])

        going[o] = to_columns(sent, near, far)
        keep[o] = to_columns(kept, near, far)
    misc[:NZ] = to_columns(lambda at: local[:, at : at + NZ], near, far)
    misc[NZ : NZ + NPJ] = energy[...]
    misc[NZ + NPJ : NZ + 8] = jnp.zeros((4, LANES), F32)
    numbers = index[:4].astype(F32)
    for k in range(OWN // LANES):
        misc[NZ + 8 + 4 * k : NZ + 12 + 4 * k] = numbers[:, k * LANES : (k + 1) * LANES]


def start_kernel(params, keep, came, misc, misc_came, edge, field, pot, xl, xh, inner, outer):
    upper = flag(params, 0)
    for o in range(ORB):
        field[o, :, :LANES] = jnp.where(upper, came[o], keep[o])
        field[o, :, LANES:] = jnp.where(upper, keep[o], came[o])
    pot[:, :LANES] = jnp.where(upper, misc_came[:NZ], misc[:NZ])
    pot[:, LANES:] = jnp.where(upper, misc[:NZ], misc_came[:NZ])
    emit_edges([field[o] for o in range(ORB)], flag(params, 1), edge, xl, xh, inner, outer)


def prepare_kernel(ints, misc_came, own, came, placed, index):
    lines = [misc_came[NZ + 8 + 4 * k : NZ + 12 + 4 * k] for k in range(OWN // LANES)]
    other = jnp.concatenate(lines, axis=1)[:, :PIECES].astype(jnp.int32)
    index[...] = jnp.concatenate([ints[:4, :PIECES], other], axis=1)
    for j in range(NPJ):
        both = jnp.concatenate([own[j], came[j]], axis=0)
        for k in range(ALL // LANES):
            at = slice(k * LANES, (k + 1) * LANES)
            placed[j, :, at] = shifted(both[at], index[1:2, at])


def column_hot(index, at, wide):
    where = lax.broadcasted_iota(jnp.int32, (COLS, wide), 0) == index[0:1, at : at + wide]
    return where.astype(F32).astype(BF16)


def atom_hot(index):
    codes = index[3:4, :]
    return (lax.broadcasted_iota(jnp.int32, (SLOTS, codes.shape[1]), 0) == codes).astype(F32).astype(BF16)


def shifted(block, shift):
    block = jnp.concatenate([jnp.transpose(block), jnp.zeros((NZ - PTS, LANES), F32)], axis=0)
    for bit in (64, 32, 16, 8, 4, 2, 1):
        block = jnp.where((shift & bit) != 0, pltpu.roll(block, bit, 0), block)
    return block


def gather_table(index, spread):
    codes = index[2:3, :]
    rows = jnp.concatenate([jnp.where(codes == code, spread, 0.0) for code in range(CODES)], axis=0)
    high, low = split(rows)
    atoms = atom_hot(index)
    return mul_t(high, atoms) + mul_t(low, atoms)


def first_table_kernel(index, keep, going, proj, table, table_going, proj_out, placed, partial):
    blocks = OWN // LANES
    for j in range(NPJ):
        proj_out[j] = proj[j]
        for k in range(blocks):
            block = proj[j, k * LANES : min((k + 1) * LANES, PIECES)]
            if k == blocks - 1:
                block = jnp.concatenate([block, jnp.zeros((OWN - PIECES, LANES), F32)], axis=0)
            placed[j, :, k * LANES : (k + 1) * LANES] = shifted(block, index[1:2, k * LANES : (k + 1) * LANES])
    hot = (lax.broadcasted_iota(jnp.int32, (LANES, OWN), 0) == index[4:5, :]).astype(F32).astype(BF16)
    hot = jnp.concatenate([hot, hot], axis=0)
    for source, out in ((keep, table), (going, table_going)):
        both = jnp.concatenate([jnp.concatenate(split(source[o]), axis=1) for o in range(ORB)], axis=0)
        for at in range(0, OWN, 256):
            picked = mul(both, hot[:, at : at + 256])
            for j in range(NPJ):
                values = placed[j, :, at : at + 256]
                for o in range(ORB):
                    term = picked[o * NZ : (o + 1) * NZ] * values
                    partial[o * NPJ + j : o * NPJ + j + 1, at : at + 256] = jnp.sum(term, axis=0, keepdims=True)
        out[...] = gather_table(index, partial[...])


def table_kernel(index, field, placed, table, partial):
    parts = [split(field[o]) for o in range(ORB)]
    both = jnp.concatenate([jnp.concatenate(p, axis=1) for p in parts], axis=0)
    for at, wide in CHUNKS:
        hot = column_hot(index, at, wide)
        picked = mul(both, jnp.concatenate([hot, hot], axis=0))
        for j in range(NPJ):
            values = placed[j, :, at : at + wide]
            for o in range(ORB):
                term = picked[o * NZ : (o + 1) * NZ] * values
                partial[o * NPJ + j : o * NPJ + j + 1, at : at + wide] = jnp.sum(term, axis=0, keepdims=True)
    table[...] = gather_table(index, partial[...])


def pair_kernel(params, table, came, half):
    second = flag(params, 1)
    half[...] = jnp.where(second, table[HALF:] + came[HALF:], table[:HALF] + came[:HALF])


def sum_kernel(mine, came, acc, low, high, acc_out):
    total = mine[...] + came[...]
    step = 2 * ROWS
    for q in range(2):
        low[q * step : (q + 1) * step] = total[2 * q * step : (2 * q + 1) * step]
        high[q * step : (q + 1) * step] = total[(2 * q + 1) * step : (2 * q + 2) * step]


def scale_of(first, params):
    row = 3 if first else 4
    return params[row : row + 1, 0:1]


def total_kernel(first, params, low, high, below, above, energy, acc, out, acc_out):
    step = 2 * ROWS
    scale = params[3 if first else 4 : 4 if first else 5, :]
    for q in range(2):
        at = slice(q * step, (q + 1) * step)
        row = 2 * q * step
        out[row : row + step] = (low[at] + below[at]) * energy[row : row + step] * scale
        row = row + step
        out[row : row + step] = (high[at] + above[at]) * energy[row : row + step] * scale


def local_kernel(first, params, half, field, before, pot, own_w, ring_w, out):
    center = params[2:3, 0:1]
    scale = scale_of(first, params)
    diagonal = pot[...] + (3.0 * WEIGHTS[0] * KINETIC - center)
    for o in range(ORB):
        value = field[o]
        high, low = split(value)
        across = mul(jnp.concatenate([high, low, high], axis=1), own_w[...])
        along = mul(ring_w[...], jnp.concatenate([high, low, high], axis=0))
        total = scale * (across + along + diagonal * value)
        out[o] = total if first else total - before[o]


def halo_kernel(first, params, acc, xl, xh, inner, outer, halo_w, out):
    scale = scale_of(first, params)
    below_inner = flag(params, 1)
    for o in range(ORB):
        inside, outside = unpack_edge(inner[o]), unpack_edge(outer[o])
        bottom = jnp.where(below_inner, inside, outside)
        top = jnp.where(below_inner, outside, inside)
        line = jnp.concatenate([unpack_edge(xl[o]), unpack_edge(xh[o]), bottom, top], axis=1)
        high, low = split(line)
        out[o] = acc[o] + scale * mul(jnp.concatenate([high, low, high], axis=1), halo_w[...])


def update_kernel(last, params, index, acc, mine, came, placed, *rest):
    second = flag(params, 1)
    total = jnp.concatenate(
        [jnp.where(second, came[...], mine[...]), jnp.where(second, mine[...], came[...])], axis=0
    )
    atoms = atom_hot(index)
    spread = mul(jnp.concatenate(split(total), axis=1), jnp.concatenate([atoms, atoms], axis=0))
    codes = index[2:3, :]
    coefs = jnp.zeros((ROWS, ALL), F32)
    for code in range(CODES):
        coefs = jnp.where(codes == code, spread[code * ROWS : (code + 1) * ROWS], coefs)
    total = jnp.zeros((ORB * NZ, COLS), F32)
    for at, wide in CHUNKS:
        hot = column_hot(index, at, wide)
        lines = []
        for o in range(ORB):
            line = coefs[o * NPJ : o * NPJ + 1, at : at + wide] * placed[0, :, at : at + wide]
            for j in range(1, NPJ):
                row = o * NPJ + j
                line = line + coefs[row : row + 1, at : at + wide] * placed[j, :, at : at + wide]
            lines.append(jnp.concatenate(split(line), axis=1))
        total = total + mul_t(jnp.concatenate(lines, axis=0), jnp.concatenate([hot, hot], axis=1))
    fields = [acc[o] + total[o * NZ : (o + 1) * NZ] for o in range(ORB)]
    if not last:
        edge, field, xl, xh, inner, outer = rest
        for o in range(ORB):
            field[o] = fields[o]
        emit_edges(fields, second, edge, xl, xh, inner, outer)
        return
    kept, sent, hold, near, far = rest
    upper = flag(params, 0)
    for o in range(ORB):
        left, right = fields[o][:, :LANES], fields[o][:, LANES:]
        hold[o] = fields[o]
        for spot, pair in from_columns(jnp.where(upper, left, right), near, far):
            sent[o, :, spot : spot + 2 * NZ] = pair
    for o in range(ORB):
        left, right = fields[o][:, :LANES], fields[o][:, LANES:]
        for spot, pair in from_columns(jnp.where(upper, right, left), near, far):
            kept[o, :, spot : spot + 2 * NZ] = pair


def join_kernel(params, mine, came, out):
    upper = params[0:1, 0:1] == 1.0
    for o in range(ORB):
        out[o] = jnp.where(upper, came[o], mine[o])
        out[ORB + o] = jnp.where(upper, mine[o], came[o])


def add_kernel(a, b, c, d, filtered, out, filtered_out):
    out[...] = a[...] + b[...] + c[...] + d[...]


def density_kernel(params, field, quarter, across_x, across_band, across_both, plane, near, far):
    dens = jnp.zeros((NZ, COLS), F32)
    for o in range(ORB):
        dens = dens + params[8 + o : 9 + o, 0:1] * field[o] * field[o]
    left, right = dens[:, :LANES], dens[:, LANES:]
    upper = flag(params, 0)
    second = params[5:6, 0:1] == 1.0
    span = CY * NZ // 2
    for value, same, opposite in (
        (jnp.where(upper, right, left), quarter, across_band),
        (jnp.where(upper, left, right), across_x, across_both),
    ):
        for spot, pair in from_columns(value, near, far):
            plane[:, spot : spot + 2 * NZ] = pair
        same[...] = jnp.where(second, plane[:, span:], plane[:, :span])
        opposite[...] = jnp.where(second, plane[:, :span], plane[:, span:])


VM = pl.BlockSpec(memory_space=pltpu.VMEM)
ANY = pl.BlockSpec(memory_space=pl.ANY)


def call(kernel, in_specs, shapes, args, scratch=(), flops=10**8, name=None, passed=0):
    single = isinstance(shapes, tuple)
    outs = [shapes] if single else list(shapes)
    outs = [shape if isinstance(shape[0], tuple) else (shape, F32) for shape in outs]
    plain = len(outs) - passed
    result = pl.pallas_call(
        kernel,
        out_shape=[jax.ShapeDtypeStruct(*out) for out in outs],
        in_specs=in_specs,
        out_specs=[VM] * plain + [ANY] * passed,
        scratch_shapes=list(scratch),
        input_output_aliases={len(args) - passed + k: plain + k for k in range(passed)},
        compiler_params=pltpu.CompilerParams(vmem_limit_bytes=48 * 1024 * 1024),
        cost_estimate=pl.CostEstimate(flops=flops, bytes_accessed=4 * 10**6, transcendentals=0),
        name=name,
    )(*args)
    return result[0] if single else result


def send(value, pairs):
    return lax.ppermute(value, "dom", pairs)


def along_z(step):
    return [(d, (d + 16 * step) % 64) for d in range(64)]


def outward(d):
    y = d % 8
    return d // 8 * 8 + ((y - 1) % 8 if y % 2 == 0 else (y + 1) % 8)


SWAP = [(d, d ^ 8) for d in range(64)]
CORES = [(d, d ^ 1) for d in range(64)]
OUTER = [(d, outward(d)) for d in range(64)]


def body(
    orbitals,
    occupation,
    potential,
    projectors,
    energies,
    piece_column,
    piece_shift,
    piece_owner,
    piece_atom,
    lower_edge,
    upper_edge,
):
    own_m, halo_m, ring_m, edge_m = stencil_matrices()
    a, b = two_parts(own_m)
    own_w = jnp.asarray(np.concatenate([a, a, b], axis=0))
    a, b = two_parts(halo_m)
    halo_w = jnp.asarray(np.concatenate([a, a, b], axis=0))
    a, b = two_parts(ring_m)
    ring_w = jnp.asarray(np.concatenate([a, a, b], axis=1))
    edge_w = jnp.asarray(edge_m.astype(np.float32).astype(jnp.bfloat16))

    here = lax.axis_index("dom")
    side = (here // 8 % 2).astype(jnp.int32)
    core = (here % 2).astype(jnp.int32)
    band = lax.axis_index("band")
    center = (upper_edge + lower_edge) / 2.0
    half_width = (upper_edge - lower_edge) / 2.0
    weights = lax.dynamic_slice_in_dim(occupation, side * ORB, ORB, 0)
    places = jnp.stack([side, core, band]).astype(F32)
    values = jnp.concatenate(
        [places[:2], center, 1.0 / half_width, 2.0 / half_width, places[2:], jnp.zeros((2,), F32), weights, weights]
    )
    params = jnp.broadcast_to(values[:, None], (16, LANES))
    packed = (ORB, PACKED, LANES)
    grid = (ORB, NZ, COLS)
    stage = [pltpu.VMEM((LANES, LANES), F32)] * 2

    step_x = piece_owner[0] // 3 - 1
    step_y = piece_owner[0] % 3 - 1
    codes = (step_y + 1 + core) * 4 + side + step_x + 1
    rows = [side * LANES + piece_column[0], piece_shift[0], codes, piece_atom[0], piece_column[0]]
    ints = jnp.pad(jnp.stack(rows), ((0, 0), (0, OWN - PIECES)), constant_values=-1)
    keep, going, misc = call(
        turn_kernel,
        [VM] * 5,
        [(ORB, NZ, LANES)] * 2 + [(NZ + 24, LANES)],
        (params, orbitals[:, 0], potential[0], energies[0], ints),
        stage,
        name="turn",
    )
    came = send(going, SWAP)
    table_keep, table_going, proj = call(
        first_table_kernel,
        [VM] * 4,
        [(CODES * ROWS, LANES)] * 2 + [(NPJ, PIECES, LANES)],
        (ints, keep, going, projectors[0]),
        [pltpu.VMEM((NPJ, NZ, OWN), F32), pltpu.VMEM((ROWS, OWN), F32)],
        name="first_table",
    )
    table = table_keep + send(table_going, SWAP)
    misc_came = send(misc, SWAP)
    proj_came = send(proj, SWAP)
    pair = jnp.stack([energies[0], misc_came[NZ : NZ + NPJ]])
    pair = jnp.where(side == 0, pair, pair[::-1])
    outer_pair = send(pair, OUTER)
    two = jnp.where(core == 0, jnp.stack([outer_pair, pair]), jnp.stack([pair, outer_pair]))
    below_e = send(two[:, 1], along_z(1))
    above_e = send(two[:, 0], along_z(-1))
    around = jnp.concatenate([below_e[:, None], two, above_e[:, None]], axis=1)
    energy = jnp.broadcast_to(around[:, :, None], (2, 4, ORB, NPJ, LANES)).reshape(HALF, LANES)

    field, pot, xl, xh, inner, outer = call(
        start_kernel,
        [VM] * 6,
        [grid, (NZ, COLS)] + [packed] * 4,
        (params, keep, came, misc, misc_came, edge_w),
        name="start",
    )
    placed, index = call(
        prepare_kernel,
        [VM] * 4,
        [(NPJ, NZ, ALL), ((4, ALL), jnp.int32)],
        (ints, misc_came, projectors[0], proj_came),
        name="prepare",
    )

    before = field
    for level in range(DEG):
        first, last = level == 0, level == DEG - 1
        if not first:
            table = call(
                table_kernel,
                [VM] * 3,
                (CODES * ROWS, LANES),
                (index, field, placed),
                [pltpu.VMEM((ROWS, ALL), F32)],
                name="table",
            )
        inner_came = send(inner, CORES)
        half = call(
            pair_kernel, [VM] * 3, (HALF, LANES), (params, table, send(table, CORES)), flops=10**6, name="pair"
        )
        half_came = send(half, OUTER)
        xl_came = send(xh, along_z(1))
        xh_came = send(xl, along_z(-1))
        outer_came = send(outer, OUTER)
        acc = call(
            functools.partial(local_kernel, first),
            [VM, ANY] + [VM] * 5,
            grid,
            (params, half, field, before, pot, own_w, ring_w),
            name="local",
        )
        low, high, acc = call(
            sum_kernel,
            [VM, VM, ANY],
            [(HALF // 2, LANES)] * 2 + [grid],
            (half, half_came, acc),
            flops=10**6,
            name="sums",
            passed=1,
        )
        below = send(high, along_z(1))
        above = send(low, along_z(-1))
        acc = call(
            functools.partial(halo_kernel, first),
            [VM] * 7,
            grid,
            (params, acc, xl_came, xh_came, inner_came, outer_came, halo_w),
            name="halo",
        )
        total, acc = call(
            functools.partial(total_kernel, first),
            [VM] * 6 + [ANY],
            [(HALF, LANES), grid],
            (params, low, high, below, above, energy, acc),
            flops=10**6,
            name="totals",
            passed=1,
        )
        total_came = send(total, CORES)
        args = (params, index, acc, total, total_came, placed)
        if not last:
            before, (field, xl, xh, inner, outer) = field, call(
                functools.partial(update_kernel, last),
                [VM] * 7,
                [grid] + [packed] * 4,
                args + (edge_w,),
                name="update",
            )
        else:
            flat = (ORB, CX, CY * NZ)
            mine, other, result = call(
                functools.partial(update_kernel, last),
                [VM] * 6,
                [flat, flat, grid],
                args,
                stage,
                name="finish",
            )
    part = (CX, CY * NZ // 2)
    quarter, across_x, across_band, across_both = call(
        density_kernel,
        [VM] * 2,
        [part] * 4,
        (params, result),
        [pltpu.VMEM((CX, CY * NZ), F32)] + stage,
        name="density",
    )
    swapped = send(other, SWAP)
    both = [(d, d ^ 72) for d in range(128)]
    filtered = call(join_kernel, [VM] * 3, (2 * ORB, CX, CY * NZ), (params, mine, swapped), name="join")
    sums = (
        quarter,
        send(across_x, SWAP),
        lax.ppermute(across_band, "band", [(0, 1), (1, 0)]),
        lax.ppermute(across_both, ("band", "dom"), both),
    )
    density, filtered = call(
        add_kernel, [VM] * 4 + [ANY], [part, filtered.shape], sums + (filtered,), name="add", passed=1
    )
    return filtered[:, None], density[None]


def solution(mesh):
    in_specs = (
        P("band", "dom", None, None),
        P("band"),
        P("dom", None, None),
        P("dom", None, None, None),
        P("dom", None, None),
        P("dom", None),
        P("dom", None),
        P("dom", None),
        P("dom", None),
        P(),
        P(),
    )
    out_specs = (P("band", "dom", None, None), P("dom", None, "band"))
    return jax.shard_map(body, mesh=mesh, in_specs=in_specs, out_specs=out_specs, check_vma=False)
```

```python
import functools

import jax
import jax.numpy as jnp
import numpy as np
from jax import lax
from jax.experimental import pallas as pl
from jax.experimental.pallas import tpu as pltpu
from jax.sharding import PartitionSpec as P

NZ = 192
HALO = 6
DEG = 4
CX = 8
CY = 16
WX = 2 * CX
COLS = WX * CY
ORB = 4
NPJ = 4
PIECES = 448
ALL = 2 * PIECES
PTS = 128
SLOTS = 128
ROWS = ORB * NPJ
PACKED = 144
TAIL = NZ - PACKED
LANES = 128
EDGE = HALO * 16
OWN = 512
CODES = 12
TABLE = CODES * ROWS
THIRD = TABLE // 3
HALF = 2 * THIRD
NOTE = TABLE + NZ
CHUNKS = ((0, 256), (256, 256), (512, 256), (768, 128))

WEIGHTS = (
    -5369.0 / 1800.0,
    12.0 / 7.0,
    -15.0 / 56.0,
    10.0 / 189.0,
    -1.0 / 112.0,
    2.0 / 1925.0,
    -1.0 / 16632.0,
)
KINETIC = -0.5 / 0.16
F32 = jnp.float32
BF16 = jnp.bfloat16


def coupling(steps):
    reach = np.abs(steps)
    near = (reach >= 1) & (reach <= HALO)
    table = np.array(WEIGHTS) * KINETIC
    return np.where(near, table[np.minimum(reach, HALO)], 0.0)


def stencil_matrices():
    col = np.arange(COLS)
    x, y = col // CY, col % CY
    same_x = x[:, None] == x[None, :]
    same_y = y[:, None] == y[None, :]
    own = np.where(same_y, coupling(x[None, :] - x[:, None]), 0.0)
    own = own + np.where(same_x, coupling(y[None, :] - y[:, None]), 0.0)
    lane = np.arange(LANES)
    used = (lane < EDGE)[:, None]
    parts = []
    for start in (-HALO, WX):
        hx, hy = start + lane // CY, lane % CY
        parts.append(np.where(used & (hy[:, None] == y[None, :]), coupling(x[None, :] - hx[:, None]), 0.0))
    for start in (-HALO, CY):
        hy, hx = start + lane // WX, lane % WX
        parts.append(np.where(used & (hx[:, None] == x[None, :]), coupling(y[None, :] - hy[:, None]), 0.0))
    halo = np.concatenate(parts, axis=0)
    depth = np.arange(NZ)
    apart = (depth[None, :] - depth[:, None] + NZ // 2) % NZ - NZ // 2
    ring = coupling(apart)
    picks = []
    for start in (0, CY - HALO):
        hy, hx = start + lane // WX, lane % WX
        picks.append(np.where(used.T & (col[:, None] == (hx * CY + hy)[None, :]), 1.0, 0.0))
    edge = np.concatenate(picks, axis=1)
    return own, halo, ring, edge


def two_parts(matrix):
    high = np.asarray(matrix, np.float32).astype(jnp.bfloat16)
    low = (np.asarray(matrix, np.float64) - high.astype(np.float64)).astype(np.float32).astype(jnp.bfloat16)
    return high, low


def split(value):
    high = value.astype(BF16)
    low = (value - high.astype(F32)).astype(BF16)
    return high, low


def mul(left, right):
    return jnp.dot(left, right, preferred_element_type=F32)


def mul_t(left, right):
    return lax.dot_general(left, right, (((1,), (1,)), ((), ())), preferred_element_type=F32)


def pack_edge(value):
    main = value[:PACKED]
    lane = lax.broadcasted_iota(jnp.int32, (TAIL, LANES), 1)
    rows = []
    for k in range(3):
        tail = pltpu.roll(value[PACKED:], (EDGE - 32 * k) % LANES, 1)
        rows.append(jnp.where(lane < EDGE, main[k * TAIL : (k + 1) * TAIL], tail))
    return jnp.concatenate(rows, axis=0)


def unpack_edge(value):
    lane = lax.broadcasted_iota(jnp.int32, (TAIL, LANES), 1)
    tail = jnp.zeros((TAIL, LANES), F32)
    for k in range(3):
        moved = pltpu.roll(value[k * TAIL : (k + 1) * TAIL], (32 * k - EDGE) % LANES, 1)
        tail = jnp.where((lane >= 32 * k) & (lane < 32 * k + 32), moved, tail)
    return jnp.concatenate([value, tail], axis=0)


def emit_edges(fields, below_inner, edge_ref, xl_ref, xh_ref, inner_ref, outer_ref):
    for o in range(ORB):
        value = fields[o]
        high, low = split(value)
        picked = mul(high, edge_ref[...]) + mul(low, edge_ref[...])
        xl_ref[o] = pack_edge(value[:, :LANES])
        xh_ref[o] = pack_edge(pltpu.roll(value[:, LANES:], LANES - 32, 1))
        bottom, top = pack_edge(picked[:, :LANES]), pack_edge(picked[:, LANES:])
        inner_ref[o] = jnp.where(below_inner, bottom, top)
        outer_ref[o] = jnp.where(below_inner, top, bottom)


def to_columns(source, near, far):
    for y in range(CY):
        at = y * NZ
        line = source(at)
        near[pl.ds(y, CX, stride=CY), :] = line[:, :LANES]
        tail = line[:, LANES:]
        far[pl.ds(y, CX, stride=CY), :] = jnp.concatenate([tail, jnp.zeros((CX, 2 * LANES - NZ), F32)], axis=1)
    return jnp.concatenate([jnp.transpose(near[...]), jnp.transpose(far[...])[: NZ - LANES]], axis=0)


def from_columns(value, near, far):
    near[...] = jnp.transpose(value[:LANES])
    far[...] = jnp.transpose(jnp.concatenate([value[LANES:], jnp.zeros((2 * LANES - NZ, LANES), F32)], axis=0))
    for y in range(0, CY, 2):
        lines = []
        for at in (y, y + 1):
            lines.append(near[pl.ds(at, CX, stride=CY), :])
            lines.append(far[pl.ds(at, CX, stride=CY), :][:, : NZ - LANES])
        yield y * NZ, jnp.concatenate(lines, axis=1)


def flag(params, row):
    return params[row : row + 1, :] == 1.0


def turn_kernel(place, upper_edge, lower_edge, weights, column, shift, owner, atom, raw, keep, going, params, ints, near, far):
    side, core = place[0], place[1]
    upper = jnp.full((1, LANES), side, jnp.int32) == 1
    params[0:1] = jnp.full((1, LANES), side, jnp.int32).astype(F32)
    params[1:2] = jnp.full((1, LANES), core, jnp.int32).astype(F32)
    top = jnp.full((1, LANES), upper_edge[0], F32)
    bottom = jnp.full((1, LANES), lower_edge[0], F32)
    half_width = (top - bottom) / 2.0
    params[2:3] = (top + bottom) / 2.0
    params[3:4] = 1.0 / half_width
    params[4:5] = 2.0 / half_width
    params[5:6] = jnp.full((1, LANES), place[2], jnp.int32).astype(F32)
    params[6:8] = jnp.zeros((2, LANES), F32)
    for o in range(ORB):
        params[8 + o : 9 + o] = jnp.full((1, LANES), weights[side * ORB + o], F32)
    params[8 + ORB :] = jnp.zeros((8 - ORB, LANES), F32)
    sub = jnp.full((1, PIECES), side, jnp.int32)
    step_x = (owner[...] >= 3).astype(jnp.int32) + (owner[...] >= 6).astype(jnp.int32)
    row = owner[...] - 3 * step_x
    lines = [
        sub * LANES + column[...],
        shift[...],
        row * 4 + sub + step_x,
        atom[...],
        column[...],
    ]
    gap = jnp.full((1, OWN - PIECES), -1, jnp.int32)
    for k, line in enumerate(lines):
        ints[k : k + 1] = jnp.concatenate([line, gap], axis=1)
    ints[len(lines) :] = jnp.zeros((8 - len(lines), OWN), jnp.int32)
    for o in range(ORB):
        def kept(at, o=o):
            return jnp.where(upper[:, :1], raw[ORB + o, :, at : at + NZ], raw[o, :, at : at + NZ])

        def sent(at, o=o):
            return jnp.where(upper[:, :1], raw[o, :, at : at + NZ], raw[ORB + o, :, at : at + NZ])

        going[o] = to_columns(sent, near, far)
        keep[o] = to_columns(kept, near, far)


def start_kernel(params, keep, came, local, note_came, edge, field, pot, xl, xh, inner, outer, near, far):
    upper = flag(params, 0)
    for o in range(ORB):
        turned = to_columns(lambda at, o=o: came[o, :, at : at + NZ], near, far)
        field[o, :, :LANES] = jnp.where(upper, turned, keep[o])
        field[o, :, LANES:] = jnp.where(upper, keep[o], turned)
    there = note_came[TABLE : TABLE + NZ]
    pot[:, :LANES] = jnp.where(upper, there, local[...])
    pot[:, LANES:] = jnp.where(upper, local[...], there)
    emit_edges([field[o] for o in range(ORB)], flag(params, 1), edge, xl, xh, inner, outer)


def gate_kernel(came, note_came, proj, out):
    pass


def prepare_kernel(ints, note_came, own, came, placed, index):
    lines = [note_came[NOTE + 8 + 4 * k : NOTE + 12 + 4 * k] for k in range(OWN // LANES)]
    other = jnp.concatenate(lines, axis=1)[:, :PIECES].astype(jnp.int32)
    index[...] = jnp.concatenate([ints[:4, :PIECES], other], axis=1)
    for j in range(NPJ):
        both = jnp.concatenate([own[j], came[j]], axis=0)
        for k in range(ALL // LANES):
            at = slice(k * LANES, (k + 1) * LANES)
            placed[j, :, at] = shifted(both[at], index[1:2, at])


def column_hot(index, at, wide):
    where = lax.broadcasted_iota(jnp.int32, (COLS, wide), 0) == index[0:1, at : at + wide]
    return where.astype(F32).astype(BF16)


def atom_hot(index):
    codes = index[3:4, :]
    return (lax.broadcasted_iota(jnp.int32, (SLOTS, codes.shape[1]), 0) == codes).astype(F32).astype(BF16)


def shifted(block, shift):
    block = jnp.concatenate([jnp.transpose(block), jnp.zeros((NZ - PTS, LANES), F32)], axis=0)
    for bit in (64, 32, 16, 8, 4, 2, 1):
        block = jnp.where((shift & bit) != 0, pltpu.roll(block, bit, 0), block)
    return block


def gather_table(index, spread):
    codes = index[2:3, :]
    rows = jnp.concatenate([jnp.where(codes == code, spread, 0.0) for code in range(CODES)], axis=0)
    high, low = split(rows)
    atoms = atom_hot(index)
    return mul_t(high, atoms) + mul_t(low, atoms)


def first_table_kernel(index, keep, going, proj, potential, energy, table, local, note, placed, partial, near, far):
    blocks = OWN // LANES
    for j in range(NPJ):
        for k in range(blocks):
            block = proj[j, k * LANES : min((k + 1) * LANES, PIECES)]
            if k == blocks - 1:
                block = jnp.concatenate([block, jnp.zeros((OWN - PIECES, LANES), F32)], axis=0)
            placed[j, :, k * LANES : (k + 1) * LANES] = shifted(block, index[1:2, k * LANES : (k + 1) * LANES])
    hot = (lax.broadcasted_iota(jnp.int32, (LANES, OWN), 0) == index[4:5, :]).astype(F32).astype(BF16)
    hot = jnp.concatenate([hot, hot], axis=0)
    for source, out in ((keep, table), (going, note)):
        both = jnp.concatenate([jnp.concatenate(split(source[o]), axis=1) for o in range(ORB)], axis=0)
        for at in range(0, OWN, 256):
            picked = mul(both, hot[:, at : at + 256])
            for j in range(NPJ):
                values = placed[j, :, at : at + 256]
                for o in range(ORB):
                    term = picked[o * NZ : (o + 1) * NZ] * values
                    partial[o * NPJ + j : o * NPJ + j + 1, at : at + 256] = jnp.sum(term, axis=0, keepdims=True)
        out[:TABLE] = gather_table(index, partial[...])
    turned = to_columns(lambda at: potential[:, at : at + NZ], near, far)
    local[...] = turned
    note[TABLE:NOTE] = turned
    note[NOTE : NOTE + NPJ] = energy[...]
    note[NOTE + NPJ : NOTE + 8] = jnp.zeros((4, LANES), F32)
    numbers = index[:4].astype(F32)
    for k in range(OWN // LANES):
        note[NOTE + 8 + 4 * k : NOTE + 12 + 4 * k] = numbers[:, k * LANES : (k + 1) * LANES]


def table_kernel(index, field, placed, table, partial):
    parts = [split(field[o]) for o in range(ORB)]
    both = jnp.concatenate([jnp.concatenate(p, axis=1) for p in parts], axis=0)
    for at, wide in CHUNKS:
        hot = column_hot(index, at, wide)
        picked = mul(both, jnp.concatenate([hot, hot], axis=0))
        for j in range(NPJ):
            values = placed[j, :, at : at + wide]
            for o in range(ORB):
                term = picked[o * NZ : (o + 1) * NZ] * values
                partial[o * NPJ + j : o * NPJ + j + 1, at : at + wide] = jnp.sum(term, axis=0, keepdims=True)
    table[...] = gather_table(index, partial[...])


def pair_sum(second, table, came):
    gap = jnp.zeros((THIRD, LANES), F32)
    up = table[THIRD:] + jnp.concatenate([came[HALF:], gap], axis=0)
    down = table[:HALF] + jnp.concatenate([gap, came[:THIRD]], axis=0)
    return jnp.where(second, up, down)


def join_table_kernel(table, note_came, out):
    out[...] = table[...] + note_came[:TABLE]


def first_pair_kernel(params, table, came, energy, note_came, half):
    half[:HALF] = pair_sum(flag(params, 1), table[...], came[...])
    upper = flag(params, 0)
    there = note_came[NOTE : NOTE + NPJ]
    half[HALF : HALF + NPJ] = jnp.where(upper, there, energy[...])
    half[HALF + NPJ :] = jnp.where(upper, energy[...], there)


def pair_kernel(params, table, came, half):
    half[...] = pair_sum(flag(params, 1), table[...], came[...])


def sum_kernel(mine, came, acc, low, high, acc_out):
    total = mine[:HALF] + came[:HALF]
    step = 2 * ROWS
    for q in range(2):
        low[q * step : (q + 1) * step] = total[2 * q * step : (2 * q + 1) * step]
        high[q * step : (q + 1) * step] = total[(2 * q + 1) * step : (2 * q + 2) * step]


def first_sum_kernel(params, mine, came, acc, low, high, acc_out):
    sum_kernel(mine, came, acc, low, high, acc_out)
    second = flag(params, 1)
    for sub, out in ((0, low), (1, high)):
        at = HALF + sub * NPJ
        here, there = mine[at : at + NPJ], came[at : at + NPJ]
        out[THIRD : THIRD + NPJ] = jnp.where(second, here, there)
        out[THIRD + NPJ :] = jnp.where(second, there, here)


def spread_energy(low, high, below, above, energy):
    for q in range(2):
        at = slice(THIRD + q * NPJ, THIRD + (q + 1) * NPJ)
        for r, source in enumerate((below, low, high, above)):
            row = (q * 4 + r) * ROWS
            energy[row : row + ROWS] = jnp.concatenate([source[at]] * ORB, axis=0)


def scale_of(first, params):
    row = 3 if first else 4
    return params[row : row + 1, 0:1]


def total_kernel(first, params, low, high, below, above, acc, energy, out, acc_out, energy_out=None):
    if first:
        spread_energy(low, high, below, above, energy_out)
        energy = energy_out
    step = 2 * ROWS
    scale = params[3 if first else 4 : 4 if first else 5, :]
    for q in range(2):
        at = slice(q * step, (q + 1) * step)
        row = 2 * q * step
        out[row : row + step] = (low[at] + below[at]) * energy[row : row + step] * scale
        row = row + step
        out[row : row + step] = (high[at] + above[at]) * energy[row : row + step] * scale


def first_total_kernel(params, low, high, below, above, acc, out, energy, acc_out):
    total_kernel(True, params, low, high, below, above, acc, None, out, acc_out, energy)


def later_total_kernel(params, low, high, below, above, energy, acc, out, acc_out):
    total_kernel(False, params, low, high, below, above, acc, energy, out, acc_out)


def local_kernel(first, params, half, field, before, pot, own_w, ring_w, out):
    center = params[2:3, 0:1]
    scale = scale_of(first, params)
    diagonal = pot[...] + (3.0 * WEIGHTS[0] * KINETIC - center)
    for o in range(ORB):
        value = field[o]
        high, low = split(value)
        across = mul(jnp.concatenate([high, low, high], axis=1), own_w[...])
        along = mul(ring_w[...], jnp.concatenate([high, low, high], axis=0))
        total = scale * (across + along + diagonal * value)
        out[o] = total if first else total - before[o]


def halo_kernel(first, params, outer, xl, xh, inner, acc, halo_w, out):
    scale = scale_of(first, params)
    below_inner = flag(params, 1)
    for o in range(ORB):
        inside, outside = unpack_edge(inner[o]), unpack_edge(outer[o])
        bottom = jnp.where(below_inner, inside, outside)
        top = jnp.where(below_inner, outside, inside)
        line = jnp.concatenate([unpack_edge(xl[o]), unpack_edge(xh[o]), bottom, top], axis=1)
        high, low = split(line)
        out[o] = acc[o] + scale * mul(jnp.concatenate([high, low, high], axis=1), halo_w[...])


def update_kernel(last, params, index, acc, mine, came, placed, *rest):
    second = flag(params, 1)
    total = jnp.concatenate(
        [jnp.where(second, came[THIRD:], mine[...][:THIRD]), jnp.where(second, mine[...][:THIRD], mine[...][THIRD:]),
         jnp.where(second, mine[...][THIRD:], came[:THIRD])], axis=0
    )
    atoms = atom_hot(index)
    spread = mul(jnp.concatenate(split(total), axis=1), jnp.concatenate([atoms, atoms], axis=0))
    codes = index[2:3, :]
    coefs = jnp.zeros((ROWS, ALL), F32)
    for code in range(CODES):
        coefs = jnp.where(codes == code, spread[code * ROWS : (code + 1) * ROWS], coefs)
    total = jnp.zeros((ORB * NZ, COLS), F32)
    for at, wide in CHUNKS:
        hot = column_hot(index, at, wide)
        lines = []
        for o in range(ORB):
            line = coefs[o * NPJ : o * NPJ + 1, at : at + wide] * placed[0, :, at : at + wide]
            for j in range(1, NPJ):
                row = o * NPJ + j
                line = line + coefs[row : row + 1, at : at + wide] * placed[j, :, at : at + wide]
            lines.append(jnp.concatenate(split(line), axis=1))
        total = total + mul_t(jnp.concatenate(lines, axis=0), jnp.concatenate([hot, hot], axis=1))
    fields = [acc[o] + total[o * NZ : (o + 1) * NZ] for o in range(ORB)]
    if not last:
        edge, field, xl, xh, inner, outer = rest
        for o in range(ORB):
            field[o] = fields[o]
        emit_edges(fields, second, edge, xl, xh, inner, outer)
        return
    kept, sent, hold, near, far = rest
    upper = flag(params, 0)
    for o in range(ORB):
        left, right = fields[o][:, :LANES], fields[o][:, LANES:]
        hold[o] = fields[o]
        for spot, pair in from_columns(jnp.where(upper, left, right), near, far):
            sent[o, :, spot : spot + 2 * NZ] = pair
    for o in range(ORB):
        left, right = fields[o][:, :LANES], fields[o][:, LANES:]
        for spot, pair in from_columns(jnp.where(upper, right, left), near, far):
            kept[o, :, spot : spot + 2 * NZ] = pair


def join_kernel(params, mine, came, out):
    upper = params[0:1, 0:1] == 1.0
    for o in range(ORB):
        out[o] = jnp.where(upper, came[o], mine[o])
        out[ORB + o] = jnp.where(upper, mine[o], came[o])


def add_kernel(a, b, c, d, filtered, out, filtered_out):
    out[...] = a[...] + b[...] + c[...] + d[...]


def density_kernel(params, field, quarter, across_x, across_band, across_both, plane, near, far):
    dens = jnp.zeros((NZ, COLS), F32)
    for o in range(ORB):
        dens = dens + params[8 + o : 9 + o, 0:1] * field[o] * field[o]
    left, right = dens[:, :LANES], dens[:, LANES:]
    upper = flag(params, 0)
    second = params[5:6, 0:1] == 1.0
    span = CY * NZ // 2
    for value, same, opposite in (
        (jnp.where(upper, right, left), quarter, across_band),
        (jnp.where(upper, left, right), across_x, across_both),
    ):
        for spot, pair in from_columns(value, near, far):
            plane[:, spot : spot + 2 * NZ] = pair
        same[...] = jnp.where(second, plane[:, span:], plane[:, :span])
        opposite[...] = jnp.where(second, plane[:, :span], plane[:, span:])


VM = pl.BlockSpec(memory_space=pltpu.VMEM)
ANY = pl.BlockSpec(memory_space=pl.ANY)
SM = pl.BlockSpec(memory_space=pltpu.SMEM)


def call(kernel, in_specs, shapes, args, scratch=(), flops=10**8, name=None, passed=0):
    single = isinstance(shapes, tuple)
    outs = [shapes] if single else list(shapes)
    outs = [shape if isinstance(shape[0], tuple) else (shape, F32) for shape in outs]
    plain = len(outs) - passed
    result = pl.pallas_call(
        kernel,
        out_shape=[jax.ShapeDtypeStruct(*out) for out in outs],
        in_specs=in_specs,
        out_specs=[VM] * plain + [ANY] * passed,
        scratch_shapes=list(scratch),
        input_output_aliases={len(args) - passed + k: plain + k for k in range(passed)},
        compiler_params=pltpu.CompilerParams(vmem_limit_bytes=48 * 1024 * 1024),
        cost_estimate=pl.CostEstimate(flops=flops, bytes_accessed=4 * 10**6, transcendentals=0),
        name=name,
    )(*args)
    return result[0] if single else result


def send(value, pairs):
    return lax.ppermute(value, "dom", pairs)


def along_z(step):
    return [(d, (d + 16 * step) % 64) for d in range(64)]


def outward(d):
    y = d % 8
    return d // 8 * 8 + ((y - 1) % 8 if y % 2 == 0 else (y + 1) % 8)


SWAP = [(d, d ^ 8) for d in range(64)]
CORES = [(d, d ^ 1) for d in range(64)]
OUTER = [(d, outward(d)) for d in range(64)]


def body(
    orbitals,
    occupation,
    potential,
    projectors,
    energies,
    piece_column,
    piece_shift,
    piece_owner,
    piece_atom,
    lower_edge,
    upper_edge,
):
    own_m, halo_m, ring_m, edge_m = stencil_matrices()
    a, b = two_parts(own_m)
    own_w = jnp.asarray(np.concatenate([a, a, b], axis=0))
    a, b = two_parts(halo_m)
    halo_w = jnp.asarray(np.concatenate([a, a, b], axis=0))
    a, b = two_parts(ring_m)
    ring_w = jnp.asarray(np.concatenate([a, a, b], axis=1))
    edge_w = jnp.asarray(edge_m.astype(np.float32).astype(jnp.bfloat16))

    here = lax.axis_index("dom")
    side = (here // 8 % 2).astype(jnp.int32)
    core = (here % 2).astype(jnp.int32)
    place = jnp.stack([side, core, lax.axis_index("band").astype(jnp.int32)])
    packed = (ORB, PACKED, LANES)
    grid = (ORB, NZ, COLS)
    stage = [pltpu.VMEM((LANES, LANES), F32)] * 2

    raw = orbitals[:, 0]
    came = send(lax.dynamic_slice_in_dim(raw, (1 - side) * ORB, ORB, 0), SWAP)
    keep, going, params, ints = call(
        turn_kernel,
        [SM] * 4 + [VM] * 5,
        [(ORB, NZ, LANES)] * 2 + [(16, LANES), ((8, OWN), jnp.int32)],
        (place, upper_edge, lower_edge, occupation, piece_column, piece_shift, piece_owner, piece_atom, raw),
        stage,
        name="turn",
    )
    own_table, local, note = call(
        first_table_kernel,
        [VM] * 6,
        [(TABLE, LANES), (NZ, LANES), (NOTE + 24, LANES)],
        (ints, keep, going, projectors[0], potential[0], energies[0]),
        [pltpu.VMEM((NPJ, NZ, OWN), F32), pltpu.VMEM((ROWS, OWN), F32)] + stage,
        name="first_table",
    )
    note_came = send(note, SWAP)
    proj = call(gate_kernel, [ANY] * 3, [(NPJ, PIECES, LANES)], (came, note_came, projectors[0]), flops=10**6, name="gate", passed=1)
    proj_came = send(proj[0], SWAP)
    table = call(join_table_kernel, [VM] * 2, (TABLE, LANES), (own_table, note_came), flops=10**6, name="join_table")
    field, pot, xl, xh, inner, outer = call(
        start_kernel,
        [VM] * 6,
        [grid, (NZ, COLS)] + [packed] * 4,
        (params, keep, came, local, note_came, edge_w),
        stage,
        name="start",
    )
    placed, index = call(
        prepare_kernel,
        [VM] * 4,
        [(NPJ, NZ, ALL), ((4, ALL), jnp.int32)],
        (ints, note_came, projectors[0], proj_came),
        name="prepare",
    )

    before = field
    for level in range(DEG):
        first, last = level == 0, level == DEG - 1
        if not first:
            table = call(
                table_kernel,
                [VM] * 3,
                (TABLE, LANES),
                (index, field, placed),
                [pltpu.VMEM((ROWS, ALL), F32)],
                name="table",
            )
        inner_came = send(inner, CORES)
        table_came = send(table, CORES)
        if first:
            half = call(
                first_pair_kernel,
                [VM] * 5,
                (HALF + 8, LANES),
                (params, table, table_came, energies[0], note_came),
                flops=10**6,
                name="pair",
            )
        else:
            half = call(pair_kernel, [VM] * 3, (HALF, LANES), (params, table, table_came), flops=10**6, name="pair")
        half_came = send(half, OUTER)
        xl_came = send(xh, along_z(1))
        xh_came = send(xl, along_z(-1))
        outer_came = send(outer, OUTER)
        acc = call(
            functools.partial(local_kernel, first),
            [VM, ANY] + [VM] * 5,
            grid,
            (params, half, field, before, pot, own_w, ring_w),
            name="local",
        )
        size = (THIRD + 8, LANES) if first else (THIRD, LANES)
        low, high, acc = call(
            first_sum_kernel if first else sum_kernel,
            [VM] * (3 if first else 2) + [ANY],
            [size, size, grid],
            ((params,) if first else ()) + (half, half_came, acc),
            flops=10**6,
            name="sums",
            passed=1,
        )
        below = send(high, along_z(1))
        above = send(low, along_z(-1))
        acc = call(
            functools.partial(halo_kernel, first),
            [VM] * 7,
            grid,
            (params, outer_came, xl_came, xh_came, inner_came, acc, halo_w),
            name="halo",
        )
        if first:
            total, energy, acc = call(
                first_total_kernel,
                [VM] * 5 + [ANY],
                [(HALF, LANES), (HALF, LANES), grid],
                (params, low, high, below, above, acc),
                flops=10**6,
                name="totals",
                passed=1,
            )
        else:
            total, acc = call(
                later_total_kernel,
                [VM] * 6 + [ANY],
                [(HALF, LANES), grid],
                (params, low, high, below, above, energy, acc),
                flops=10**6,
                name="totals",
                passed=1,
            )
        total_came = send(total, CORES)
        args = (params, index, acc, total, total_came, placed)
        if not last:
            before, (field, xl, xh, inner, outer) = field, call(
                functools.partial(update_kernel, last),
                [VM] * 7,
                [grid] + [packed] * 4,
                args + (edge_w,),
                name="update",
            )
        else:
            flat = (ORB, CX, CY * NZ)
            mine, other, result = call(
                functools.partial(update_kernel, last),
                [VM] * 6,
                [flat, flat, grid],
                args,
                stage,
                name="finish",
            )
    part = (CX, CY * NZ // 2)
    quarter, across_x, across_band, across_both = call(
        density_kernel,
        [VM] * 2,
        [part] * 4,
        (params, result),
        [pltpu.VMEM((CX, CY * NZ), F32)] + stage,
        name="density",
    )
    swapped = send(other, SWAP)
    both = [(d, d ^ 72) for d in range(128)]
    filtered = call(join_kernel, [VM] * 3, (2 * ORB, CX, CY * NZ), (params, mine, swapped), name="join")
    sums = (
        quarter,
        send(across_x, SWAP),
        lax.ppermute(across_band, "band", [(0, 1), (1, 0)]),
        lax.ppermute(across_both, ("band", "dom"), both),
    )
    density, filtered = call(
        add_kernel, [VM] * 4 + [ANY], [part, filtered.shape], sums + (filtered,), name="add", passed=1
    )
    return filtered[:, None], density[None]


def solution(mesh):
    in_specs = (
        P("band", "dom", None, None),
        P("band"),
        P("dom", None, None),
        P("dom", None, None, None),
        P("dom", None, None),
        P("dom", None),
        P("dom", None),
        P("dom", None),
        P("dom", None),
        P(),
        P(),
    )
    out_specs = (P("band", "dom", None, None), P("dom", None, "band"))
    return jax.shard_map(body, mesh=mesh, in_specs=in_specs, out_specs=out_specs, check_vma=False)
```

```python
import functools

import jax
import jax.numpy as jnp
import numpy as np
from jax import lax
from jax.experimental import pallas as pl
from jax.experimental.pallas import tpu as pltpu
from jax.sharding import PartitionSpec as P

NZ = 192
HALO = 6
DEG = 4
CX = 8
CY = 16
WX = 2 * CX
COLS = WX * CY
ORB = 4
NPJ = 4
PIECES = 448
ALL = 2 * PIECES
PTS = 128
SLOTS = 128
ROWS = ORB * NPJ
PACKED = 144
TAIL = NZ - PACKED
LANES = 128
EDGE = HALO * 16
OWN = 512
ROOM = 58
CODES = 12
TABLE = CODES * ROWS
THIRD = TABLE // 3
HALF = 2 * THIRD
NOTE = TABLE + NZ
CHUNKS = ((0, 256), (256, 256), (512, 256), (768, 128))

WEIGHTS = (
    -5369.0 / 1800.0,
    12.0 / 7.0,
    -15.0 / 56.0,
    10.0 / 189.0,
    -1.0 / 112.0,
    2.0 / 1925.0,
    -1.0 / 16632.0,
)
KINETIC = -0.5 / 0.16
F32 = jnp.float32
BF16 = jnp.bfloat16


def coupling(steps):
    reach = np.abs(steps)
    near = (reach >= 1) & (reach <= HALO)
    table = np.array(WEIGHTS) * KINETIC
    return np.where(near, table[np.minimum(reach, HALO)], 0.0)


def stencil_matrices():
    col = np.arange(COLS)
    x, y = col // CY, col % CY
    same_x = x[:, None] == x[None, :]
    same_y = y[:, None] == y[None, :]
    own = np.where(same_y, coupling(x[None, :] - x[:, None]), 0.0)
    own = own + np.where(same_x, coupling(y[None, :] - y[:, None]), 0.0)
    lane = np.arange(LANES)
    used = (lane < EDGE)[:, None]
    parts = []
    for start in (-HALO, WX):
        hx, hy = start + lane // CY, lane % CY
        parts.append(np.where(used & (hy[:, None] == y[None, :]), coupling(x[None, :] - hx[:, None]), 0.0))
    for start in (-HALO, CY):
        hy, hx = start + lane // WX, lane % WX
        parts.append(np.where(used & (hx[:, None] == x[None, :]), coupling(y[None, :] - hy[:, None]), 0.0))
    halo = np.concatenate(parts, axis=0)
    depth = np.arange(NZ)
    apart = (depth[None, :] - depth[:, None] + NZ // 2) % NZ - NZ // 2
    ring = coupling(apart)
    picks = []
    for start in (0, CY - HALO):
        hy, hx = start + lane // WX, lane % WX
        picks.append(np.where(used.T & (col[:, None] == (hx * CY + hy)[None, :]), 1.0, 0.0))
    edge = np.concatenate(picks, axis=1)
    return own, halo, ring, edge


def two_parts(matrix):
    high = np.asarray(matrix, np.float32).astype(jnp.bfloat16)
    low = (np.asarray(matrix, np.float64) - high.astype(np.float64)).astype(np.float32).astype(jnp.bfloat16)
    return high, low


def split(value):
    high = value.astype(BF16)
    low = (value - high.astype(F32)).astype(BF16)
    return high, low


def mul(left, right):
    return jnp.dot(left, right, preferred_element_type=F32)


def mul_t(left, right):
    return lax.dot_general(left, right, (((1,), (1,)), ((), ())), preferred_element_type=F32)


def pack_edge(value):
    main = value[:PACKED]
    lane = lax.broadcasted_iota(jnp.int32, (TAIL, LANES), 1)
    rows = []
    for k in range(3):
        tail = pltpu.roll(value[PACKED:], (EDGE - 32 * k) % LANES, 1)
        rows.append(jnp.where(lane < EDGE, main[k * TAIL : (k + 1) * TAIL], tail))
    return jnp.concatenate(rows, axis=0)


def unpack_edge(value):
    lane = lax.broadcasted_iota(jnp.int32, (TAIL, LANES), 1)
    tail = jnp.zeros((TAIL, LANES), F32)
    for k in range(3):
        moved = pltpu.roll(value[k * TAIL : (k + 1) * TAIL], (32 * k - EDGE) % LANES, 1)
        tail = jnp.where((lane >= 32 * k) & (lane < 32 * k + 32), moved, tail)
    return jnp.concatenate([value, tail], axis=0)


def emit_edges(fields, below_inner, edge_ref, xl_ref, xh_ref, inner_ref, outer_ref):
    for o in range(ORB):
        value = fields[o]
        high, low = split(value)
        picked = mul(high, edge_ref[...]) + mul(low, edge_ref[...])
        xl_ref[o] = pack_edge(value[:, :LANES])
        xh_ref[o] = pack_edge(pltpu.roll(value[:, LANES:], LANES - 32, 1))
        bottom, top = pack_edge(picked[:, :LANES]), pack_edge(picked[:, LANES:])
        inner_ref[o] = jnp.where(below_inner, bottom, top)
        outer_ref[o] = jnp.where(below_inner, top, bottom)


def to_columns(source, near, far):
    for y in range(CY):
        at = y * NZ
        line = source(at)
        near[pl.ds(y, CX, stride=CY), :] = line[:, :LANES]
        tail = line[:, LANES:]
        far[pl.ds(y, CX, stride=CY), :] = jnp.concatenate([tail, jnp.zeros((CX, 2 * LANES - NZ), F32)], axis=1)
    return jnp.concatenate([jnp.transpose(near[...]), jnp.transpose(far[...])[: NZ - LANES]], axis=0)


def from_columns(value, near, far):
    near[...] = jnp.transpose(value[:LANES])
    far[...] = jnp.transpose(jnp.concatenate([value[LANES:], jnp.zeros((2 * LANES - NZ, LANES), F32)], axis=0))
    for y in range(0, CY, 2):
        lines = []
        for at in (y, y + 1):
            lines.append(near[pl.ds(at, CX, stride=CY), :])
            lines.append(far[pl.ds(at, CX, stride=CY), :][:, : NZ - LANES])
        yield y * NZ, jnp.concatenate(lines, axis=1)


def flag(params, row):
    return params[row : row + 1, :] == 1.0


def begin_kernel(
    place, upper_edge, lower_edge, weights, column_in, shift_in, owner_in, atom_in, raw_in, proj_in, pot_in, energy_in,
    keep, params, ints, table, local, note,
    column, shift, owner, atom, raw, proj, potential, energy, going, placed, partial, near, far, sems,
):
    pairs = (
        (raw_in, raw), (column_in, column), (shift_in, shift), (owner_in, owner),
        (atom_in, atom), (proj_in, proj), (pot_in, potential), (energy_in, energy),
    )
    copies = [pltpu.make_async_copy(source, target, sems.at[k]) for k, (source, target) in enumerate(pairs)]
    for copy in copies:
        copy.start()
    side, core = place[0], place[1]
    upper = jnp.full((1, LANES), side, jnp.int32) == 1
    params[0:1] = jnp.full((1, LANES), side, jnp.int32).astype(F32)
    params[1:2] = jnp.full((1, LANES), core, jnp.int32).astype(F32)
    top = jnp.full((1, LANES), upper_edge[0], F32)
    bottom = jnp.full((1, LANES), lower_edge[0], F32)
    half_width = (top - bottom) / 2.0
    params[2:3] = (top + bottom) / 2.0
    params[3:4] = 1.0 / half_width
    params[4:5] = 2.0 / half_width
    params[5:6] = jnp.full((1, LANES), place[2], jnp.int32).astype(F32)
    params[6:8] = jnp.zeros((2, LANES), F32)
    for o in range(ORB):
        params[8 + o : 9 + o] = jnp.full((1, LANES), weights[side * ORB + o], F32)
    params[8 + ORB :] = jnp.zeros((8 - ORB, LANES), F32)
    sub = jnp.full((1, PIECES), side, jnp.int32)
    for copy in copies[:5]:
        copy.wait()
    step_x = (owner[...] >= 3).astype(jnp.int32) + (owner[...] >= 6).astype(jnp.int32)
    row = owner[...] - 3 * step_x
    lines = [
        sub * LANES + column[...],
        shift[...],
        row * 4 + sub + step_x,
        atom[...],
        column[...],
    ]
    gap = jnp.full((1, OWN - PIECES), -1, jnp.int32)
    for k, line in enumerate(lines):
        ints[k : k + 1] = jnp.concatenate([line, gap], axis=1)
    ints[len(lines) :] = jnp.zeros((8 - len(lines), OWN), jnp.int32)
    for o in range(ORB):
        def kept(at, o=o):
            return jnp.where(upper[:, :1], raw[ORB + o, :, at : at + NZ], raw[o, :, at : at + NZ])

        def sent(at, o=o):
            return jnp.where(upper[:, :1], raw[o, :, at : at + NZ], raw[ORB + o, :, at : at + NZ])

        going[o] = to_columns(sent, near, far)
        keep[o] = to_columns(kept, near, far)
    for copy in copies[5:]:
        copy.wait()
    first_tables(ints, keep, going, proj, potential, energy, table, local, note, placed, partial, near, far)


def start_kernel(params, keep, came, edge, field, xl, xh, inner, outer, near, far):
    upper = flag(params, 0)
    for o in range(ORB):
        turned = to_columns(lambda at, o=o: came[o, :, at : at + NZ], near, far)
        field[o, :, :LANES] = jnp.where(upper, turned, keep[o])
        field[o, :, LANES:] = jnp.where(upper, keep[o], turned)
    emit_edges([field[o] for o in range(ORB)], flag(params, 1), edge, xl, xh, inner, outer)


def gate_kernel(came, note_came, proj, out):
    pass


def prepare_kernel(ints, note_came, own, came, placed, index):
    lines = [note_came[NOTE + 8 + 4 * k : NOTE + 12 + 4 * k] for k in range(OWN // LANES)]
    other = jnp.concatenate(lines, axis=1)[:, :PIECES].astype(jnp.int32)
    index[...] = jnp.concatenate([ints[:4, :PIECES], other], axis=1)
    for j in range(NPJ):
        both = jnp.concatenate([own[j], came[j]], axis=0)
        for k in range(ALL // LANES):
            at = slice(k * LANES, (k + 1) * LANES)
            placed[j, :, at] = shifted(both[at], index[1:2, at])


def column_hot(index, at, wide):
    where = lax.broadcasted_iota(jnp.int32, (COLS, wide), 0) == index[0:1, at : at + wide]
    return where.astype(F32).astype(BF16)


def atom_hot(index):
    codes = index[3:4, :]
    return (lax.broadcasted_iota(jnp.int32, (SLOTS, codes.shape[1]), 0) == codes).astype(F32).astype(BF16)


def shifted(block, shift):
    block = jnp.concatenate([jnp.transpose(block), jnp.zeros((NZ - PTS, LANES), F32)], axis=0)
    for bit in (64, 32, 16, 8, 4, 2, 1):
        block = jnp.where((shift & bit) != 0, pltpu.roll(block, bit, 0), block)
    return block


def gather_table(index, spread):
    codes = index[2:3, :]
    rows = jnp.concatenate([jnp.where(codes == code, spread, 0.0) for code in range(CODES)], axis=0)
    high, low = split(rows)
    atoms = atom_hot(index)
    return mul_t(high, atoms) + mul_t(low, atoms)


def first_tables(index, keep, going, proj, potential, energy, table, local, note, placed, partial, near, far):
    blocks = OWN // LANES
    for j in range(NPJ):
        for k in range(blocks):
            block = proj[j, k * LANES : min((k + 1) * LANES, PIECES)]
            if k == blocks - 1:
                block = jnp.concatenate([block, jnp.zeros((OWN - PIECES, LANES), F32)], axis=0)
            placed[j, :, k * LANES : (k + 1) * LANES] = shifted(block, index[1:2, k * LANES : (k + 1) * LANES])
    hot = (lax.broadcasted_iota(jnp.int32, (LANES, OWN), 0) == index[4:5, :]).astype(F32).astype(BF16)
    hot = jnp.concatenate([hot, hot], axis=0)
    for source, out in ((keep, table), (going, note)):
        both = jnp.concatenate([jnp.concatenate(split(source[o]), axis=1) for o in range(ORB)], axis=0)
        for at in range(0, OWN, 256):
            picked = mul(both, hot[:, at : at + 256])
            for j in range(NPJ):
                values = placed[j, :, at : at + 256]
                for o in range(ORB):
                    term = picked[o * NZ : (o + 1) * NZ] * values
                    partial[o * NPJ + j : o * NPJ + j + 1, at : at + 256] = jnp.sum(term, axis=0, keepdims=True)
        out[:TABLE] = gather_table(index, partial[...])
    turned = to_columns(lambda at: potential[:, at : at + NZ], near, far)
    local[...] = turned
    note[TABLE:NOTE] = turned
    note[NOTE : NOTE + NPJ] = energy[...]
    note[NOTE + NPJ : NOTE + 8] = jnp.zeros((4, LANES), F32)
    numbers = index[:4].astype(F32)
    for k in range(OWN // LANES):
        note[NOTE + 8 + 4 * k : NOTE + 12 + 4 * k] = numbers[:, k * LANES : (k + 1) * LANES]


def table_kernel(index, field, placed, table, partial):
    parts = [split(field[o]) for o in range(ORB)]
    both = jnp.concatenate([jnp.concatenate(p, axis=1) for p in parts], axis=0)
    for at, wide in CHUNKS:
        hot = column_hot(index, at, wide)
        picked = mul(both, jnp.concatenate([hot, hot], axis=0))
        for j in range(NPJ):
            values = placed[j, :, at : at + wide]
            for o in range(ORB):
                term = picked[o * NZ : (o + 1) * NZ] * values
                partial[o * NPJ + j : o * NPJ + j + 1, at : at + wide] = jnp.sum(term, axis=0, keepdims=True)
    table[...] = gather_table(index, partial[...])


def pair_sum(second, table, came):
    gap = jnp.zeros((THIRD, LANES), F32)
    up = table[THIRD:] + jnp.concatenate([came[HALF:], gap], axis=0)
    down = table[:HALF] + jnp.concatenate([gap, came[:THIRD]], axis=0)
    return jnp.where(second, up, down)


def join_table_kernel(params, table, local, note_came, field, out, pot):
    out[...] = table[...] + note_came[:TABLE]
    upper = flag(params, 0)
    there = note_came[TABLE:NOTE]
    pot[:, :LANES] = jnp.where(upper, there, local[...])
    pot[:, LANES:] = jnp.where(upper, local[...], there)


def first_pair_kernel(params, table, came, energy, note_came, half):
    half[:HALF] = pair_sum(flag(params, 1), table[...], came[...])
    upper = flag(params, 0)
    there = note_came[NOTE : NOTE + NPJ]
    half[HALF : HALF + NPJ] = jnp.where(upper, there, energy[...])
    half[HALF + NPJ :] = jnp.where(upper, energy[...], there)


def pair_kernel(params, table, came, half):
    half[...] = pair_sum(flag(params, 1), table[...], came[...])


def sum_kernel(mine, came, acc, low, high, acc_out):
    total = mine[:HALF] + came[:HALF]
    step = 2 * ROWS
    for q in range(2):
        low[q * step : (q + 1) * step] = total[2 * q * step : (2 * q + 1) * step]
        high[q * step : (q + 1) * step] = total[(2 * q + 1) * step : (2 * q + 2) * step]


def first_sum_kernel(params, mine, came, acc, low, high, acc_out):
    sum_kernel(mine, came, acc, low, high, acc_out)
    second = flag(params, 1)
    for sub, out in ((0, low), (1, high)):
        at = HALF + sub * NPJ
        here, there = mine[at : at + NPJ], came[at : at + NPJ]
        out[THIRD : THIRD + NPJ] = jnp.where(second, here, there)
        out[THIRD + NPJ :] = jnp.where(second, there, here)


def spread_energy(low, high, below, above, energy):
    for q in range(2):
        at = slice(THIRD + q * NPJ, THIRD + (q + 1) * NPJ)
        for r, source in enumerate((below, low, high, above)):
            row = (q * 4 + r) * ROWS
            energy[row : row + ROWS] = jnp.concatenate([source[at]] * ORB, axis=0)


def scale_of(first, params):
    row = 3 if first else 4
    return params[row : row + 1, 0:1]


def total_kernel(first, params, low, high, below, above, acc, energy, out, acc_out, energy_out=None):
    if first:
        spread_energy(low, high, below, above, energy_out)
        energy = energy_out
    step = 2 * ROWS
    scale = params[3 if first else 4 : 4 if first else 5, :]
    for q in range(2):
        at = slice(q * step, (q + 1) * step)
        row = 2 * q * step
        out[row : row + step] = (low[at] + below[at]) * energy[row : row + step] * scale
        row = row + step
        out[row : row + step] = (high[at] + above[at]) * energy[row : row + step] * scale


def first_total_kernel(params, low, high, below, above, acc, out, energy, acc_out):
    total_kernel(True, params, low, high, below, above, acc, None, out, acc_out, energy)


def later_total_kernel(params, low, high, below, above, energy, acc, out, acc_out):
    total_kernel(False, params, low, high, below, above, acc, energy, out, acc_out)


def local_kernel(first, params, half, field, before, pot, own_w, ring_w, out):
    center = params[2:3, 0:1]
    scale = scale_of(first, params)
    diagonal = pot[...] + (3.0 * WEIGHTS[0] * KINETIC - center)
    for o in range(ORB):
        value = field[o]
        high, low = split(value)
        across = mul(jnp.concatenate([high, low, high], axis=1), own_w[...])
        along = mul(ring_w[...], jnp.concatenate([high, low, high], axis=0))
        total = scale * (across + along + diagonal * value)
        out[o] = total if first else total - before[o]


def halo_kernel(first, params, inner, outer, xl, xh, acc, halo_w, out):
    scale = scale_of(first, params)
    below_inner = flag(params, 1)
    for o in range(ORB):
        inside, outside = unpack_edge(inner[o]), unpack_edge(outer[o])
        bottom = jnp.where(below_inner, inside, outside)
        top = jnp.where(below_inner, outside, inside)
        line = jnp.concatenate([unpack_edge(xl[o]), unpack_edge(xh[o]), bottom, top], axis=1)
        high, low = split(line)
        out[o] = acc[o] + scale * mul(jnp.concatenate([high, low, high], axis=1), halo_w[...])


def update_kernel(last, params, index, acc, mine, came, placed, *rest):
    second = flag(params, 1)
    total = jnp.concatenate(
        [jnp.where(second, came[THIRD:], mine[...][:THIRD]), jnp.where(second, mine[...][:THIRD], mine[...][THIRD:]),
         jnp.where(second, mine[...][THIRD:], came[:THIRD])], axis=0
    )
    atoms = atom_hot(index)
    spread = mul(jnp.concatenate(split(total), axis=1), jnp.concatenate([atoms, atoms], axis=0))
    codes = index[2:3, :]
    coefs = jnp.zeros((ROWS, ALL), F32)
    for code in range(CODES):
        coefs = jnp.where(codes == code, spread[code * ROWS : (code + 1) * ROWS], coefs)
    total = jnp.zeros((ORB * NZ, COLS), F32)
    for at, wide in CHUNKS:
        hot = column_hot(index, at, wide)
        lines = []
        for o in range(ORB):
            line = coefs[o * NPJ : o * NPJ + 1, at : at + wide] * placed[0, :, at : at + wide]
            for j in range(1, NPJ):
                row = o * NPJ + j
                line = line + coefs[row : row + 1, at : at + wide] * placed[j, :, at : at + wide]
            lines.append(jnp.concatenate(split(line), axis=1))
        total = total + mul_t(jnp.concatenate(lines, axis=0), jnp.concatenate([hot, hot], axis=1))
    fields = [acc[o] + total[o * NZ : (o + 1) * NZ] for o in range(ORB)]
    if not last:
        edge, field, xl, xh, inner, outer = rest
        for o in range(ORB):
            field[o] = fields[o]
        emit_edges(fields, second, edge, xl, xh, inner, outer)
        return
    kept, sent, hold, near, far = rest
    upper = flag(params, 0)
    for o in range(ORB):
        left, right = fields[o][:, :LANES], fields[o][:, LANES:]
        hold[o] = fields[o]
        for spot, pair in from_columns(jnp.where(upper, left, right), near, far):
            sent[o, :, spot : spot + 2 * NZ] = pair
    for o in range(ORB):
        left, right = fields[o][:, :LANES], fields[o][:, LANES:]
        for spot, pair in from_columns(jnp.where(upper, right, left), near, far):
            kept[o, :, spot : spot + 2 * NZ] = pair


def join_kernel(params, mine, came, out):
    upper = params[0:1, 0:1] == 1.0
    for o in range(ORB):
        out[o] = jnp.where(upper, came[o], mine[o])
        out[ORB + o] = jnp.where(upper, mine[o], came[o])


def add_kernel(a, b, c, d, filtered, out, filtered_out):
    out[...] = a[...] + b[...] + c[...] + d[...]


def density_kernel(params, field, quarter, across_x, across_band, across_both, plane, near, far):
    dens = jnp.zeros((NZ, COLS), F32)
    for o in range(ORB):
        dens = dens + params[8 + o : 9 + o, 0:1] * field[o] * field[o]
    left, right = dens[:, :LANES], dens[:, LANES:]
    upper = flag(params, 0)
    second = params[5:6, 0:1] == 1.0
    span = CY * NZ // 2
    for value, same, opposite in (
        (jnp.where(upper, right, left), quarter, across_band),
        (jnp.where(upper, left, right), across_x, across_both),
    ):
        for spot, pair in from_columns(value, near, far):
            plane[:, spot : spot + 2 * NZ] = pair
        same[...] = jnp.where(second, plane[:, span:], plane[:, :span])
        opposite[...] = jnp.where(second, plane[:, :span], plane[:, span:])


VM = pl.BlockSpec(memory_space=pltpu.VMEM)
ANY = pl.BlockSpec(memory_space=pl.ANY)
SM = pl.BlockSpec(memory_space=pltpu.SMEM)
HB = pl.BlockSpec(memory_space=pltpu.HBM)


def call(kernel, in_specs, shapes, args, scratch=(), flops=10**8, name=None, passed=0, room=48):
    single = isinstance(shapes, tuple)
    outs = [shapes] if single else list(shapes)
    outs = [shape if isinstance(shape[0], tuple) else (shape, F32) for shape in outs]
    plain = len(outs) - passed
    result = pl.pallas_call(
        kernel,
        out_shape=[jax.ShapeDtypeStruct(*out) for out in outs],
        in_specs=in_specs,
        out_specs=[VM] * plain + [ANY] * passed,
        scratch_shapes=list(scratch),
        input_output_aliases={len(args) - passed + k: plain + k for k in range(passed)},
        compiler_params=pltpu.CompilerParams(vmem_limit_bytes=room * 1024 * 1024),
        cost_estimate=pl.CostEstimate(flops=flops, bytes_accessed=4 * 10**6, transcendentals=0),
        name=name,
    )(*args)
    return result[0] if single else result


def send(value, pairs):
    return lax.ppermute(value, "dom", pairs)


def along_z(step):
    return [(d, (d + 16 * step) % 64) for d in range(64)]


def outward(d):
    y = d % 8
    return d // 8 * 8 + ((y - 1) % 8 if y % 2 == 0 else (y + 1) % 8)


SWAP = [(d, d ^ 8) for d in range(64)]
CORES = [(d, d ^ 1) for d in range(64)]
OUTER = [(d, outward(d)) for d in range(64)]


def body(
    orbitals,
    occupation,
    potential,
    projectors,
    energies,
    piece_column,
    piece_shift,
    piece_owner,
    piece_atom,
    lower_edge,
    upper_edge,
):
    own_m, halo_m, ring_m, edge_m = stencil_matrices()
    a, b = two_parts(own_m)
    own_w = jnp.asarray(np.concatenate([a, a, b], axis=0))
    a, b = two_parts(halo_m)
    halo_w = jnp.asarray(np.concatenate([a, a, b], axis=0))
    a, b = two_parts(ring_m)
    ring_w = jnp.asarray(np.concatenate([a, a, b], axis=1))
    edge_w = jnp.asarray(edge_m.astype(np.float32).astype(jnp.bfloat16))

    here = lax.axis_index("dom")
    side = (here // 8 % 2).astype(jnp.int32)
    core = (here % 2).astype(jnp.int32)
    place = jnp.stack([side, core, lax.axis_index("band").astype(jnp.int32)])
    packed = (ORB, PACKED, LANES)
    grid = (ORB, NZ, COLS)
    stage = [pltpu.VMEM((LANES, LANES), F32)] * 2

    raw = orbitals[:, 0]
    came = send(lax.dynamic_slice_in_dim(raw, (1 - side) * ORB, ORB, 0), SWAP)
    line = pltpu.VMEM((1, PIECES), jnp.int32)
    keep, params, ints, own_table, local, note = call(
        begin_kernel,
        [SM] * 4 + [HB] * 8,
        [
            (ORB, NZ, LANES),
            (16, LANES),
            ((8, OWN), jnp.int32),
            (TABLE, LANES),
            (NZ, LANES),
            (NOTE + 24, LANES),
        ],
        (
            place, upper_edge, lower_edge, occupation, piece_column, piece_shift, piece_owner, piece_atom,
            raw, projectors[0], potential[0], energies[0],
        ),
        [
            line, line, line, line,
            pltpu.VMEM((2 * ORB, CX, CY * NZ), F32),
            pltpu.VMEM((NPJ, PIECES, LANES), F32),
            pltpu.VMEM((CX, CY * NZ), F32),
            pltpu.VMEM((NPJ, LANES), F32),
            pltpu.VMEM((ORB, NZ, LANES), F32),
            pltpu.VMEM((NPJ, NZ, OWN), F32),
            pltpu.VMEM((ROWS, OWN), F32),
            *stage,
            pltpu.SemaphoreType.DMA((8,)),
        ],
        name="begin",
        room=ROOM,
    )
    note_came = send(note, SWAP)
    proj = call(gate_kernel, [ANY] * 3, [(NPJ, PIECES, LANES)], (came, note_came, projectors[0]), flops=10**6, name="gate", passed=1)
    proj_came = send(proj[0], SWAP)
    field, xl, xh, inner, outer = call(
        start_kernel,
        [VM] * 4,
        [grid] + [packed] * 4,
        (params, keep, came, edge_w),
        stage,
        name="start",
    )
    table, pot = call(
        join_table_kernel,
        [VM] * 4 + [ANY],
        [(TABLE, LANES), (NZ, COLS)],
        (params, own_table, local, note_came, field),
        flops=10**6,
        name="join_table",
    )
    placed, index = call(
        prepare_kernel,
        [VM] * 4,
        [(NPJ, NZ, ALL), ((4, ALL), jnp.int32)],
        (ints, note_came, projectors[0], proj_came),
        name="prepare",
    )

    before = field
    for level in range(DEG):
        first, last = level == 0, level == DEG - 1
        if not first:
            table = call(
                table_kernel,
                [VM] * 3,
                (TABLE, LANES),
                (index, field, placed),
                [pltpu.VMEM((ROWS, ALL), F32)],
                name="table",
            )
        inner_came = send(inner, CORES)
        table_came = send(table, CORES)
        if first:
            half = call(
                first_pair_kernel,
                [VM] * 5,
                (HALF + 8, LANES),
                (params, table, table_came, energies[0], note_came),
                flops=10**6,
                name="pair",
            )
        else:
            half = call(pair_kernel, [VM] * 3, (HALF, LANES), (params, table, table_came), flops=10**6, name="pair")
        half_came = send(half, OUTER)
        xl_came = send(xh, along_z(1))
        xh_came = send(xl, along_z(-1))
        outer_came = send(outer, OUTER)
        acc = call(
            functools.partial(local_kernel, first),
            [VM, ANY] + [VM] * 5,
            grid,
            (params, half, field, before, pot, own_w, ring_w),
            name="local",
        )
        size = (THIRD + 8, LANES) if first else (THIRD, LANES)
        low, high, acc = call(
            first_sum_kernel if first else sum_kernel,
            [VM] * (3 if first else 2) + [ANY],
            [size, size, grid],
            ((params,) if first else ()) + (half, half_came, acc),
            flops=10**6,
            name="sums",
            passed=1,
        )
        below = send(high, along_z(1))
        above = send(low, along_z(-1))
        acc = call(
            functools.partial(halo_kernel, first),
            [VM] * 7,
            grid,
            (params, inner_came, outer_came, xl_came, xh_came, acc, halo_w),
            name="halo",
        )
        if first:
            total, energy, acc = call(
                first_total_kernel,
                [VM] * 5 + [ANY],
                [(HALF, LANES), (HALF, LANES), grid],
                (params, low, high, below, above, acc),
                flops=10**6,
                name="totals",
                passed=1,
            )
        else:
            total, acc = call(
                later_total_kernel,
                [VM] * 6 + [ANY],
                [(HALF, LANES), grid],
                (params, low, high, below, above, energy, acc),
                flops=10**6,
                name="totals",
                passed=1,
            )
        total_came = send(total, CORES)
        args = (params, index, acc, total, total_came, placed)
        if not last:
            before, (field, xl, xh, inner, outer) = field, call(
                functools.partial(update_kernel, last),
                [VM] * 7,
                [grid] + [packed] * 4,
                args + (edge_w,),
                name="update",
            )
        else:
            flat = (ORB, CX, CY * NZ)
            mine, other, result = call(
                functools.partial(update_kernel, last),
                [VM] * 6,
                [flat, flat, grid],
                args,
                stage,
                name="finish",
            )
    part = (CX, CY * NZ // 2)
    quarter, across_x, across_band, across_both = call(
        density_kernel,
        [VM] * 2,
        [part] * 4,
        (params, result),
        [pltpu.VMEM((CX, CY * NZ), F32)] + stage,
        name="density",
    )
    swapped = send(other, SWAP)
    both = [(d, d ^ 72) for d in range(128)]
    filtered = call(join_kernel, [VM] * 3, (2 * ORB, CX, CY * NZ), (params, mine, swapped), name="join")
    sums = (
        quarter,
        send(across_x, SWAP),
        lax.ppermute(across_band, "band", [(0, 1), (1, 0)]),
        lax.ppermute(across_both, ("band", "dom"), both),
    )
    density, filtered = call(
        add_kernel, [VM] * 4 + [ANY], [part, filtered.shape], sums + (filtered,), name="add", passed=1
    )
    return filtered[:, None], density[None]


def solution(mesh):
    in_specs = (
        P("band", "dom", None, None),
        P("band"),
        P("dom", None, None),
        P("dom", None, None, None),
        P("dom", None, None),
        P("dom", None),
        P("dom", None),
        P("dom", None),
        P("dom", None),
        P(),
        P(),
    )
    out_specs = (P("band", "dom", None, None), P("dom", None, "band"))
    return jax.shard_map(body, mesh=mesh, in_specs=in_specs, out_specs=out_specs, check_vma=False)
```

```python
import functools

import jax
import jax.numpy as jnp
import numpy as np
from jax import lax
from jax.experimental import pallas as pl
from jax.experimental.pallas import tpu as pltpu
from jax.sharding import PartitionSpec as P

NZ = 192
HALO = 6
DEG = 4
CX = 8
CY = 16
WX = 2 * CX
COLS = WX * CY
ORB = 4
NPJ = 4
PIECES = 448
ALL = 2 * PIECES
PTS = 128
SLOTS = 128
ROWS = ORB * NPJ
PACKED = 144
TAIL = NZ - PACKED
LANES = 128
EDGE = HALO * 16
OWN = 512
ROOM = 58
CODES = 12
TABLE = CODES * ROWS
THIRD = TABLE // 3
HALF = 2 * THIRD
NOTE = TABLE + NZ

WEIGHTS = (
    -5369.0 / 1800.0,
    12.0 / 7.0,
    -15.0 / 56.0,
    10.0 / 189.0,
    -1.0 / 112.0,
    2.0 / 1925.0,
    -1.0 / 16632.0,
)
KINETIC = -0.5 / 0.16
F32 = jnp.float32
BF16 = jnp.bfloat16


def coupling(steps):
    reach = np.abs(steps)
    near = (reach >= 1) & (reach <= HALO)
    table = np.array(WEIGHTS) * KINETIC
    return np.where(near, table[np.minimum(reach, HALO)], 0.0)


def stencil_matrices():
    col = np.arange(COLS)
    x, y = col // CY, col % CY
    same_x = x[:, None] == x[None, :]
    same_y = y[:, None] == y[None, :]
    own = np.where(same_y, coupling(x[None, :] - x[:, None]), 0.0)
    own = own + np.where(same_x, coupling(y[None, :] - y[:, None]), 0.0)
    lane = np.arange(LANES)
    used = (lane < EDGE)[:, None]
    parts = []
    for start in (-HALO, WX):
        hx, hy = start + lane // CY, lane % CY
        parts.append(np.where(used & (hy[:, None] == y[None, :]), coupling(x[None, :] - hx[:, None]), 0.0))
    for start in (-HALO, CY):
        hy, hx = start + lane // WX, lane % WX
        parts.append(np.where(used & (hx[:, None] == x[None, :]), coupling(y[None, :] - hy[:, None]), 0.0))
    halo = np.concatenate(parts, axis=0)
    depth = np.arange(NZ)
    apart = (depth[None, :] - depth[:, None] + NZ // 2) % NZ - NZ // 2
    ring = coupling(apart)
    picks = []
    for start in (0, CY - HALO):
        hy, hx = start + lane // WX, lane % WX
        picks.append(np.where(used.T & (col[:, None] == (hx * CY + hy)[None, :]), 1.0, 0.0))
    edge = np.concatenate(picks, axis=1)
    return own, halo, ring, edge


def two_parts(matrix):
    high = np.asarray(matrix, np.float32).astype(jnp.bfloat16)
    low = (np.asarray(matrix, np.float64) - high.astype(np.float64)).astype(np.float32).astype(jnp.bfloat16)
    return high, low


def split(value):
    high = value.astype(BF16)
    low = (value - high.astype(F32)).astype(BF16)
    return high, low


def mul(left, right):
    return jnp.dot(left, right, preferred_element_type=F32)


def mul_t(left, right):
    return lax.dot_general(left, right, (((1,), (1,)), ((), ())), preferred_element_type=F32)


def pack_edge(value):
    main = value[:PACKED]
    lane = lax.broadcasted_iota(jnp.int32, (TAIL, LANES), 1)
    rows = []
    for k in range(3):
        tail = pltpu.roll(value[PACKED:], (EDGE - 32 * k) % LANES, 1)
        rows.append(jnp.where(lane < EDGE, main[k * TAIL : (k + 1) * TAIL], tail))
    return jnp.concatenate(rows, axis=0)


def unpack_edge(value):
    lane = lax.broadcasted_iota(jnp.int32, (TAIL, LANES), 1)
    tail = jnp.zeros((TAIL, LANES), F32)
    for k in range(3):
        moved = pltpu.roll(value[k * TAIL : (k + 1) * TAIL], (32 * k - EDGE) % LANES, 1)
        tail = jnp.where((lane >= 32 * k) & (lane < 32 * k + 32), moved, tail)
    return jnp.concatenate([value, tail], axis=0)


def each(count, step):
    def run(k, carry):
        step(k)
        return carry

    lax.fori_loop(0, count, run, 0)


def emit_edges(field, below_inner, edge_ref, xl_ref, xh_ref, inner_ref, outer_ref):
    def step(o):
        value = field[o]
        high, low = split(value)
        picked = mul(high, edge_ref[...]) + mul(low, edge_ref[...])
        xl_ref[o] = pack_edge(value[:, :LANES])
        xh_ref[o] = pack_edge(pltpu.roll(value[:, LANES:], LANES - 32, 1))
        bottom, top = pack_edge(picked[:, :LANES]), pack_edge(picked[:, LANES:])
        inner_ref[o] = jnp.where(below_inner, bottom, top)
        outer_ref[o] = jnp.where(below_inner, top, bottom)

    each(ORB, step)


def to_columns(source, near, far):
    for y in range(CY):
        at = y * NZ
        line = source(at)
        near[pl.ds(y, CX, stride=CY), :] = line[:, :LANES]
        tail = line[:, LANES:]
        far[pl.ds(y, CX, stride=CY), :] = jnp.concatenate([tail, jnp.zeros((CX, 2 * LANES - NZ), F32)], axis=1)
    return jnp.concatenate([jnp.transpose(near[...]), jnp.transpose(far[...])[: NZ - LANES]], axis=0)


def from_columns(value, near, far):
    near[...] = jnp.transpose(value[:LANES])
    far[...] = jnp.transpose(jnp.concatenate([value[LANES:], jnp.zeros((2 * LANES - NZ, LANES), F32)], axis=0))
    for y in range(0, CY, 2):
        lines = []
        for at in (y, y + 1):
            lines.append(near[pl.ds(at, CX, stride=CY), :])
            lines.append(far[pl.ds(at, CX, stride=CY), :][:, : NZ - LANES])
        yield y * NZ, jnp.concatenate(lines, axis=1)


def flag(params, row):
    return params[row : row + 1, :] == 1.0


def begin_kernel(
    place, upper_edge, lower_edge, weights, column_in, shift_in, owner_in, atom_in, raw_in, proj_in, pot_in, energy_in,
    keep, params, ints, table, local, note,
    column, shift, owner, atom, raw, proj, potential, energy, turned, tables, both, placed, partial, near, far, sems,
):
    pairs = (
        (raw_in, raw), (column_in, column), (shift_in, shift), (owner_in, owner),
        (atom_in, atom), (proj_in, proj), (pot_in, potential), (energy_in, energy),
    )
    copies = [pltpu.make_async_copy(source, target, sems.at[k]) for k, (source, target) in enumerate(pairs)]
    for copy in copies:
        copy.start()
    side, core = place[0], place[1]
    upper = jnp.full((1, LANES), side, jnp.int32) == 1
    params[0:1] = jnp.full((1, LANES), side, jnp.int32).astype(F32)
    params[1:2] = jnp.full((1, LANES), core, jnp.int32).astype(F32)
    top = jnp.full((1, LANES), upper_edge[0], F32)
    bottom = jnp.full((1, LANES), lower_edge[0], F32)
    half_width = (top - bottom) / 2.0
    params[2:3] = (top + bottom) / 2.0
    params[3:4] = 1.0 / half_width
    params[4:5] = 2.0 / half_width
    params[5:6] = jnp.full((1, LANES), place[2], jnp.int32).astype(F32)
    params[6:8] = jnp.zeros((2, LANES), F32)
    for o in range(ORB):
        params[8 + o : 9 + o] = jnp.full((1, LANES), weights[side * ORB + o], F32)
    params[8 + ORB :] = jnp.zeros((8 - ORB, LANES), F32)
    sub = jnp.full((1, PIECES), side, jnp.int32)
    for copy in copies[:5]:
        copy.wait()
    step_x = (owner[...] >= 3).astype(jnp.int32) + (owner[...] >= 6).astype(jnp.int32)
    row = owner[...] - 3 * step_x
    lines = [
        sub * LANES + column[...],
        shift[...],
        row * 4 + sub + step_x,
        atom[...],
        column[...],
    ]
    gap = jnp.full((1, OWN - PIECES), -1, jnp.int32)
    for k, line in enumerate(lines):
        ints[k : k + 1] = jnp.concatenate([line, gap], axis=1)
    ints[len(lines) :] = jnp.zeros((8 - len(lines), OWN), jnp.int32)
    def turn(o):
        def kept(at):
            return jnp.where(upper[:, :1], raw[ORB + o, :, at : at + NZ], raw[o, :, at : at + NZ])

        def sent(at):
            return jnp.where(upper[:, :1], raw[o, :, at : at + NZ], raw[ORB + o, :, at : at + NZ])

        turned[o] = to_columns(kept, near, far)
        turned[ORB + o] = to_columns(sent, near, far)
        keep[o] = turned[o]

    each(ORB, turn)
    for copy in copies[5:]:
        copy.wait()
    first_tables(ints, turned, tables, both, proj, placed, partial)
    table[...] = tables[0]
    note[:TABLE] = tables[1]
    lines = to_columns(lambda at: potential[:, at : at + NZ], near, far)
    local[...] = lines
    note[TABLE:NOTE] = lines
    note[NOTE : NOTE + NPJ] = energy[...]
    note[NOTE + NPJ : NOTE + 8] = jnp.zeros((4, LANES), F32)
    numbers = ints[:4].astype(F32)
    for k in range(OWN // LANES):
        note[NOTE + 8 + 4 * k : NOTE + 12 + 4 * k] = numbers[:, k * LANES : (k + 1) * LANES]


def start_kernel(params, keep, came, edge, field, xl, xh, inner, outer, near, far):
    upper = flag(params, 0)

    def step(o):
        turned = to_columns(lambda at: came[o, :, at : at + NZ], near, far)
        kept = keep[o]
        field[o, :, :LANES] = jnp.where(upper, turned, kept)
        field[o, :, LANES:] = jnp.where(upper, kept, turned)

    each(ORB, step)
    emit_edges(field, flag(params, 1), edge, xl, xh, inner, outer)


def gate_kernel(came, note_came, proj, out):
    pass


def prepare_kernel(ints, note_came, own, came, placed, index):
    lines = [note_came[NOTE + 8 + 4 * k : NOTE + 12 + 4 * k] for k in range(OWN // LANES)]
    other = jnp.concatenate(lines, axis=1)[:, :PIECES].astype(jnp.int32)
    index[...] = jnp.concatenate([ints[:4, :PIECES], other], axis=1)

    def step(j):
        both = jnp.concatenate([own[j], came[j]], axis=0)
        for k in range(ALL // LANES):
            at = slice(k * LANES, (k + 1) * LANES)
            placed[j, :, at] = shifted(both[at], ints_row(index, at))

    each(NPJ, step)


def ints_row(index, at):
    return index[1:2, at]


def column_hot(index, at, wide):
    where = lax.broadcasted_iota(jnp.int32, (COLS, wide), 0) == index[0:1, pl.ds(at, wide)]
    return where.astype(F32).astype(BF16)


def chunks(step):
    each(ALL // 256, lambda k: step(pl.multiple_of(k * 256, 256), 256))
    step(ALL - LANES, LANES)


def atom_hot(index):
    codes = index[3:4, :]
    return (lax.broadcasted_iota(jnp.int32, (SLOTS, codes.shape[1]), 0) == codes).astype(F32).astype(BF16)


def shifted(block, shift):
    block = jnp.concatenate([jnp.transpose(block), jnp.zeros((NZ - PTS, LANES), F32)], axis=0)
    for bit in (64, 32, 16, 8, 4, 2, 1):
        block = jnp.where((shift & bit) != 0, pltpu.roll(block, bit, 0), block)
    return block


def gather_table(index, spread):
    codes = index[2:3, :]
    rows = jnp.concatenate([jnp.where(codes == code, spread, 0.0) for code in range(CODES)], axis=0)
    high, low = split(rows)
    atoms = atom_hot(index)
    return mul_t(high, atoms) + mul_t(low, atoms)


def project(both, hot, placed, partial, at, wide):
    picked = mul(both, jnp.concatenate([hot, hot], axis=0))
    for j in range(NPJ):
        values = placed[j, :, pl.ds(at, wide)]
        for o in range(ORB):
            term = picked[o * NZ : (o + 1) * NZ] * values
            row = o * NPJ + j
            partial[row : row + 1, pl.ds(at, wide)] = jnp.sum(term, axis=0, keepdims=True)


def first_tables(index, turned, tables, both, proj, placed, partial):
    blocks = OWN // LANES

    def place(j):
        for k in range(blocks):
            block = proj[j, k * LANES : min((k + 1) * LANES, PIECES)]
            if k == blocks - 1:
                block = jnp.concatenate([block, jnp.zeros((OWN - PIECES, LANES), F32)], axis=0)
            placed[j, :, k * LANES : (k + 1) * LANES] = shifted(block, index[1:2, k * LANES : (k + 1) * LANES])

    each(NPJ, place)

    def table(s):
        for o in range(ORB):
            both[o * NZ : (o + 1) * NZ, :] = jnp.concatenate(split(turned[s * ORB + o]), axis=1)

        def chunk(k):
            at = pl.multiple_of(k * 256, 256)
            where = lax.broadcasted_iota(jnp.int32, (LANES, 256), 0) == index[4:5, pl.ds(at, 256)]
            project(both[...], where.astype(F32).astype(BF16), placed, partial, at, 256)

        each(OWN // 256, chunk)
        tables[s] = gather_table(index, partial[...])

    each(2, table)


def table_kernel(index, field, placed, table, partial, both):
    def gather(o):
        rows = pl.ds(pl.multiple_of(o * NZ, NZ), NZ)
        both[rows, :] = jnp.concatenate(split(field[o]), axis=1)

    each(ORB, gather)
    chunks(lambda at, wide: project(both[...], column_hot(index, at, wide), placed, partial, at, wide))
    table[...] = gather_table(index, partial[...])


def pair_sum(second, table, came):
    gap = jnp.zeros((THIRD, LANES), F32)
    up = table[THIRD:] + jnp.concatenate([came[HALF:], gap], axis=0)
    down = table[:HALF] + jnp.concatenate([gap, came[:THIRD]], axis=0)
    return jnp.where(second, up, down)


def join_table_kernel(params, table, local, note_came, field, out, pot):
    out[...] = table[...] + note_came[:TABLE]
    upper = flag(params, 0)
    there = note_came[TABLE:NOTE]
    pot[:, :LANES] = jnp.where(upper, there, local[...])
    pot[:, LANES:] = jnp.where(upper, local[...], there)


def first_pair_kernel(params, table, came, energy, note_came, half):
    half[:HALF] = pair_sum(flag(params, 1), table[...], came[...])
    upper = flag(params, 0)
    there = note_came[NOTE : NOTE + NPJ]
    half[HALF : HALF + NPJ] = jnp.where(upper, there, energy[...])
    half[HALF + NPJ :] = jnp.where(upper, energy[...], there)


def pair_kernel(params, table, came, half):
    half[...] = pair_sum(flag(params, 1), table[...], came[...])


def sum_kernel(mine, came, acc, low, high, acc_out):
    total = mine[:HALF] + came[:HALF]
    step = 2 * ROWS
    for q in range(2):
        low[q * step : (q + 1) * step] = total[2 * q * step : (2 * q + 1) * step]
        high[q * step : (q + 1) * step] = total[(2 * q + 1) * step : (2 * q + 2) * step]


def first_sum_kernel(params, mine, came, acc, low, high, acc_out):
    sum_kernel(mine, came, acc, low, high, acc_out)
    second = flag(params, 1)
    for sub, out in ((0, low), (1, high)):
        at = HALF + sub * NPJ
        here, there = mine[at : at + NPJ], came[at : at + NPJ]
        out[THIRD : THIRD + NPJ] = jnp.where(second, here, there)
        out[THIRD + NPJ :] = jnp.where(second, there, here)


def spread_energy(low, high, below, above, energy):
    for q in range(2):
        at = slice(THIRD + q * NPJ, THIRD + (q + 1) * NPJ)
        for r, source in enumerate((below, low, high, above)):
            row = (q * 4 + r) * ROWS
            energy[row : row + ROWS] = jnp.concatenate([source[at]] * ORB, axis=0)


def scale_of(first, params):
    row = 3 if first else 4
    return params[row : row + 1, 0:1]


def total_kernel(first, params, low, high, below, above, acc, energy, out, acc_out, energy_out=None):
    if first:
        spread_energy(low, high, below, above, energy_out)
        energy = energy_out
    step = 2 * ROWS
    scale = params[3 if first else 4 : 4 if first else 5, :]
    for q in range(2):
        at = slice(q * step, (q + 1) * step)
        row = 2 * q * step
        out[row : row + step] = (low[at] + below[at]) * energy[row : row + step] * scale
        row = row + step
        out[row : row + step] = (high[at] + above[at]) * energy[row : row + step] * scale


def first_total_kernel(params, low, high, below, above, acc, out, energy, acc_out):
    total_kernel(True, params, low, high, below, above, acc, None, out, acc_out, energy)


def later_total_kernel(params, low, high, below, above, energy, acc, out, acc_out):
    total_kernel(False, params, low, high, below, above, acc, energy, out, acc_out)


def local_kernel(first, params, half, field, before, pot, own_w, ring_w, out):
    center = params[2:3, 0:1]
    scale = scale_of(first, params)
    diagonal = pot[...] + (3.0 * WEIGHTS[0] * KINETIC - center)

    def step(o):
        value = field[o]
        high, low = split(value)
        across = mul(jnp.concatenate([high, low, high], axis=1), own_w[...])
        along = mul(ring_w[...], jnp.concatenate([high, low, high], axis=0))
        total = scale * (across + along + diagonal * value)
        out[o] = total if first else total - before[o]

    each(ORB, step)


def halo_kernel(first, params, inner, outer, xl, xh, acc, halo_w, out):
    scale = scale_of(first, params)
    below_inner = flag(params, 1)

    def step(o):
        inside, outside = unpack_edge(inner[o]), unpack_edge(outer[o])
        bottom = jnp.where(below_inner, inside, outside)
        top = jnp.where(below_inner, outside, inside)
        line = jnp.concatenate([unpack_edge(xl[o]), unpack_edge(xh[o]), bottom, top], axis=1)
        high, low = split(line)
        out[o] = acc[o] + scale * mul(jnp.concatenate([high, low, high], axis=1), halo_w[...])

    each(ORB, step)


def update_kernel(last, params, index, acc, mine, came, placed, *rest):
    if last:
        kept, sent, field, coef_rows, near_sums, near, far = rest
    else:
        edge, field, xl, xh, inner, outer, coef_rows, near_sums = rest
    second = flag(params, 1)
    total = jnp.concatenate(
        [jnp.where(second, came[THIRD:], mine[...][:THIRD]), jnp.where(second, mine[...][:THIRD], mine[...][THIRD:]),
         jnp.where(second, mine[...][THIRD:], came[:THIRD])], axis=0
    )
    atoms = atom_hot(index)
    spread = mul(jnp.concatenate(split(total), axis=1), jnp.concatenate([atoms, atoms], axis=0))
    codes = index[2:3, :]
    coefs = jnp.zeros((ROWS, ALL), F32)
    for code in range(CODES):
        coefs = jnp.where(codes == code, spread[code * ROWS : (code + 1) * ROWS], coefs)
    near_sums[...] = jnp.zeros((ORB * NZ, COLS), F32)
    coef_rows[...] = coefs

    def chunk(at, wide):
        hot = column_hot(index, at, wide)
        lines = []
        for o in range(ORB):
            rows = coef_rows[o * NPJ : (o + 1) * NPJ, pl.ds(at, wide)]
            line = rows[0:1] * placed[0, :, pl.ds(at, wide)]
            for j in range(1, NPJ):
                line = line + rows[j : j + 1] * placed[j, :, pl.ds(at, wide)]
            lines.append(jnp.concatenate(split(line), axis=1))
        near_sums[...] += mul_t(jnp.concatenate(lines, axis=0), jnp.concatenate([hot, hot], axis=1))

    chunks(chunk)

    def finish(o):
        rows = pl.ds(pl.multiple_of(o * NZ, NZ), NZ)
        field[o] = acc[o] + near_sums[rows, :]

    each(ORB, finish)
    if not last:
        emit_edges(field, second, edge, xl, xh, inner, outer)
        return
    upper = flag(params, 0)

    def emit(o):
        left, right = field[o, :, :LANES], field[o, :, LANES:]
        for spot, pair in from_columns(jnp.where(upper, left, right), near, far):
            sent[o, :, spot : spot + 2 * NZ] = pair
        for spot, pair in from_columns(jnp.where(upper, right, left), near, far):
            kept[o, :, spot : spot + 2 * NZ] = pair

    each(ORB, emit)


def join_kernel(params, came, b, c, d, mine, a, out, density):
    upper = params[0:1, 0:1] == 1.0
    density[...] = a[...] + b[...] + c[...] + d[...]

    def step(o):
        out[o] = jnp.where(upper, came[o], mine[o])
        out[ORB + o] = jnp.where(upper, mine[o], came[o])

    each(ORB, step)


def density_kernel(params, field, quarter, across_x, across_band, across_both, plane, near, far):
    dens = jnp.zeros((NZ, COLS), F32)
    for o in range(ORB):
        dens = dens + params[8 + o : 9 + o, 0:1] * field[o] * field[o]
    left, right = dens[:, :LANES], dens[:, LANES:]
    upper = flag(params, 0)
    second = params[5:6, 0:1] == 1.0
    span = CY * NZ // 2
    for value, same, opposite in (
        (jnp.where(upper, right, left), quarter, across_band),
        (jnp.where(upper, left, right), across_x, across_both),
    ):
        for spot, pair in from_columns(value, near, far):
            plane[:, spot : spot + 2 * NZ] = pair
        same[...] = jnp.where(second, plane[:, span:], plane[:, :span])
        opposite[...] = jnp.where(second, plane[:, :span], plane[:, span:])


VM = pl.BlockSpec(memory_space=pltpu.VMEM)
ANY = pl.BlockSpec(memory_space=pl.ANY)
SM = pl.BlockSpec(memory_space=pltpu.SMEM)
HB = pl.BlockSpec(memory_space=pltpu.HBM)


def call(kernel, in_specs, shapes, args, scratch=(), flops=10**8, name=None, passed=0, room=48):
    single = isinstance(shapes, tuple)
    outs = [shapes] if single else list(shapes)
    outs = [shape if isinstance(shape[0], tuple) else (shape, F32) for shape in outs]
    plain = len(outs) - passed
    result = pl.pallas_call(
        kernel,
        out_shape=[jax.ShapeDtypeStruct(*out) for out in outs],
        in_specs=in_specs,
        out_specs=[VM] * plain + [ANY] * passed,
        scratch_shapes=list(scratch),
        input_output_aliases={len(args) - passed + k: plain + k for k in range(passed)},
        compiler_params=pltpu.CompilerParams(vmem_limit_bytes=room * 1024 * 1024),
        cost_estimate=pl.CostEstimate(flops=flops, bytes_accessed=4 * 10**6, transcendentals=0),
        name=name,
    )(*args)
    return result[0] if single else result


def send(value, pairs):
    return lax.ppermute(value, "dom", pairs)


def along_z(step):
    return [(d, (d + 16 * step) % 64) for d in range(64)]


def outward(d):
    y = d % 8
    return d // 8 * 8 + ((y - 1) % 8 if y % 2 == 0 else (y + 1) % 8)


SWAP = [(d, d ^ 8) for d in range(64)]
CORES = [(d, d ^ 1) for d in range(64)]
OUTER = [(d, outward(d)) for d in range(64)]


def body(
    orbitals,
    occupation,
    potential,
    projectors,
    energies,
    piece_column,
    piece_shift,
    piece_owner,
    piece_atom,
    lower_edge,
    upper_edge,
):
    own_m, halo_m, ring_m, edge_m = stencil_matrices()
    a, b = two_parts(own_m)
    own_w = jnp.asarray(np.concatenate([a, a, b], axis=0))
    a, b = two_parts(halo_m)
    halo_w = jnp.asarray(np.concatenate([a, a, b], axis=0))
    a, b = two_parts(ring_m)
    ring_w = jnp.asarray(np.concatenate([a, a, b], axis=1))
    edge_w = jnp.asarray(edge_m.astype(np.float32).astype(jnp.bfloat16))

    here = lax.axis_index("dom")
    side = (here // 8 % 2).astype(jnp.int32)
    core = (here % 2).astype(jnp.int32)
    place = jnp.stack([side, core, lax.axis_index("band").astype(jnp.int32)])
    packed = (ORB, PACKED, LANES)
    grid = (ORB, NZ, COLS)
    stage = [pltpu.VMEM((LANES, LANES), F32)] * 2

    raw = orbitals[:, 0]
    came = send(lax.dynamic_slice_in_dim(raw, (1 - side) * ORB, ORB, 0), SWAP)
    line = pltpu.VMEM((1, PIECES), jnp.int32)
    keep, params, ints, own_table, local, note = call(
        begin_kernel,
        [SM] * 4 + [HB] * 8,
        [
            (ORB, NZ, LANES),
            (16, LANES),
            ((8, OWN), jnp.int32),
            (TABLE, LANES),
            (NZ, LANES),
            (NOTE + 24, LANES),
        ],
        (
            place, upper_edge, lower_edge, occupation, piece_column, piece_shift, piece_owner, piece_atom,
            raw, projectors[0], potential[0], energies[0],
        ),
        [
            line, line, line, line,
            pltpu.VMEM((2 * ORB, CX, CY * NZ), F32),
            pltpu.VMEM((NPJ, PIECES, LANES), F32),
            pltpu.VMEM((CX, CY * NZ), F32),
            pltpu.VMEM((NPJ, LANES), F32),
            pltpu.VMEM((2 * ORB, NZ, LANES), F32),
            pltpu.VMEM((2, TABLE, LANES), F32),
            pltpu.VMEM((ORB * NZ, 2 * LANES), BF16),
            pltpu.VMEM((NPJ, NZ, OWN), F32),
            pltpu.VMEM((ROWS, OWN), F32),
            *stage,
            pltpu.SemaphoreType.DMA((8,)),
        ],
        name="begin",
        room=ROOM,
    )
    note_came = send(note, SWAP)
    proj = call(gate_kernel, [ANY] * 3, [(NPJ, PIECES, LANES)], (came, note_came, projectors[0]), flops=10**6, name="gate", passed=1)
    proj_came = send(proj[0], SWAP)
    field, xl, xh, inner, outer = call(
        start_kernel,
        [VM] * 4,
        [grid] + [packed] * 4,
        (params, keep, came, edge_w),
        stage,
        name="start",
    )
    table, pot = call(
        join_table_kernel,
        [VM] * 4 + [ANY],
        [(TABLE, LANES), (NZ, COLS)],
        (params, own_table, local, note_came, field),
        flops=10**6,
        name="join_table",
    )
    placed, index = call(
        prepare_kernel,
        [VM] * 4,
        [(NPJ, NZ, ALL), ((4, ALL), jnp.int32)],
        (ints, note_came, projectors[0], proj_came),
        name="prepare",
    )

    sums_room = [pltpu.VMEM((ROWS, ALL), F32), pltpu.VMEM((ORB * NZ, COLS), F32)]
    before = field
    for level in range(DEG):
        first, last = level == 0, level == DEG - 1
        if not first:
            table = call(
                table_kernel,
                [VM] * 3,
                (TABLE, LANES),
                (index, field, placed),
                [pltpu.VMEM((ROWS, ALL), F32), pltpu.VMEM((ORB * NZ, 2 * COLS), BF16)],
                name="table",
            )
        inner_came = send(inner, CORES)
        table_came = send(table, CORES)
        if first:
            half = call(
                first_pair_kernel,
                [VM] * 5,
                (HALF + 8, LANES),
                (params, table, table_came, energies[0], note_came),
                flops=10**6,
                name="pair",
            )
        else:
            half = call(pair_kernel, [VM] * 3, (HALF, LANES), (params, table, table_came), flops=10**6, name="pair")
        half_came = send(half, OUTER)
        xl_came = send(xh, along_z(1))
        xh_came = send(xl, along_z(-1))
        outer_came = send(outer, OUTER)
        acc = call(
            functools.partial(local_kernel, first),
            [VM, ANY] + [VM] * 5,
            grid,
            (params, half, field, before, pot, own_w, ring_w),
            name="local",
        )
        size = (THIRD + 8, LANES) if first else (THIRD, LANES)
        low, high, acc = call(
            first_sum_kernel if first else sum_kernel,
            [VM] * (3 if first else 2) + [ANY],
            [size, size, grid],
            ((params,) if first else ()) + (half, half_came, acc),
            flops=10**6,
            name="sums",
            passed=1,
        )
        below = send(high, along_z(1))
        above = send(low, along_z(-1))
        acc = call(
            functools.partial(halo_kernel, first),
            [VM] * 7,
            grid,
            (params, inner_came, outer_came, xl_came, xh_came, acc, halo_w),
            name="halo",
        )
        if first:
            total, energy, acc = call(
                first_total_kernel,
                [VM] * 5 + [ANY],
                [(HALF, LANES), (HALF, LANES), grid],
                (params, low, high, below, above, acc),
                flops=10**6,
                name="totals",
                passed=1,
            )
        else:
            total, acc = call(
                later_total_kernel,
                [VM] * 6 + [ANY],
                [(HALF, LANES), grid],
                (params, low, high, below, above, energy, acc),
                flops=10**6,
                name="totals",
                passed=1,
            )
        total_came = send(total, CORES)
        args = (params, index, acc, total, total_came, placed)
        if not last:
            before, (field, xl, xh, inner, outer) = field, call(
                functools.partial(update_kernel, last),
                [VM] * 7,
                [grid] + [packed] * 4,
                args + (edge_w,),
                sums_room,
                name="update",
            )
        else:
            flat = (ORB, CX, CY * NZ)
            mine, other, result = call(
                functools.partial(update_kernel, last),
                [VM] * 6,
                [flat, flat, grid],
                args,
                sums_room + stage,
                name="finish",
            )
    part = (CX, CY * NZ // 2)
    quarter, across_x, across_band, across_both = call(
        density_kernel,
        [VM] * 2,
        [part] * 4,
        (params, result),
        [pltpu.VMEM((CX, CY * NZ), F32)] + stage,
        name="density",
    )
    swapped = send(other, SWAP)
    both = [(d, d ^ 72) for d in range(128)]
    filtered, density = call(
        join_kernel,
        [VM] * 7,
        [(2 * ORB, CX, CY * NZ), part],
        (
            params,
            swapped,
            send(across_x, SWAP),
            lax.ppermute(across_band, "band", [(0, 1), (1, 0)]),
            lax.ppermute(across_both, ("band", "dom"), both),
            mine,
            quarter,
        ),
        name="join",
    )
    return filtered[:, None], density[None]


def solution(mesh):
    in_specs = (
        P("band", "dom", None, None),
        P("band"),
        P("dom", None, None),
        P("dom", None, None, None),
        P("dom", None, None),
        P("dom", None),
        P("dom", None),
        P("dom", None),
        P("dom", None),
        P(),
        P(),
    )
    out_specs = (P("band", "dom", None, None), P("dom", None, "band"))
    return jax.shard_map(body, mesh=mesh, in_specs=in_specs, out_specs=out_specs, check_vma=False)
```

```python
import functools

import jax
import jax.numpy as jnp
import numpy as np
from jax import lax
from jax.experimental import pallas as pl
from jax.experimental.pallas import tpu as pltpu
from jax.sharding import PartitionSpec as P

NZ = 192
HALO = 6
DEG = 4
CX = 8
CY = 16
WX = 2 * CX
COLS = WX * CY
ORB = 4
NPJ = 4
PIECES = 448
ALL = 2 * PIECES
PTS = 128
SLOTS = 128
ROWS = ORB * NPJ
PACKED = 144
TAIL = NZ - PACKED
LANES = 128
EDGE = HALO * 16
OWN = 512
ROOM = 58
LOOP_A = False
LOOP_B = False
CODES = 12
TABLE = CODES * ROWS
THIRD = TABLE // 3
HALF = 2 * THIRD
NOTE = TABLE + NZ

WEIGHTS = (
    -5369.0 / 1800.0,
    12.0 / 7.0,
    -15.0 / 56.0,
    10.0 / 189.0,
    -1.0 / 112.0,
    2.0 / 1925.0,
    -1.0 / 16632.0,
)
KINETIC = -0.5 / 0.16
F32 = jnp.float32
BF16 = jnp.bfloat16


def coupling(steps):
    reach = np.abs(steps)
    near = (reach >= 1) & (reach <= HALO)
    table = np.array(WEIGHTS) * KINETIC
    return np.where(near, table[np.minimum(reach, HALO)], 0.0)


def stencil_matrices():
    col = np.arange(COLS)
    x, y = col // CY, col % CY
    same_x = x[:, None] == x[None, :]
    same_y = y[:, None] == y[None, :]
    own = np.where(same_y, coupling(x[None, :] - x[:, None]), 0.0)
    own = own + np.where(same_x, coupling(y[None, :] - y[:, None]), 0.0)
    lane = np.arange(LANES)
    used = (lane < EDGE)[:, None]
    parts = []
    for start in (-HALO, WX):
        hx, hy = start + lane // CY, lane % CY
        parts.append(np.where(used & (hy[:, None] == y[None, :]), coupling(x[None, :] - hx[:, None]), 0.0))
    for start in (-HALO, CY):
        hy, hx = start + lane // WX, lane % WX
        parts.append(np.where(used & (hx[:, None] == x[None, :]), coupling(y[None, :] - hy[:, None]), 0.0))
    halo = np.concatenate(parts, axis=0)
    depth = np.arange(NZ)
    apart = (depth[None, :] - depth[:, None] + NZ // 2) % NZ - NZ // 2
    ring = coupling(apart)
    picks = []
    for start in (0, CY - HALO):
        hy, hx = start + lane // WX, lane % WX
        picks.append(np.where(used.T & (col[:, None] == (hx * CY + hy)[None, :]), 1.0, 0.0))
    edge = np.concatenate(picks, axis=1)
    return own, halo, ring, edge


def two_parts(matrix):
    high = np.asarray(matrix, np.float32).astype(jnp.bfloat16)
    low = (np.asarray(matrix, np.float64) - high.astype(np.float64)).astype(np.float32).astype(jnp.bfloat16)
    return high, low


def split(value):
    high = value.astype(BF16)
    low = (value - high.astype(F32)).astype(BF16)
    return high, low


def mul(left, right):
    return jnp.dot(left, right, preferred_element_type=F32)


def mul_t(left, right):
    return lax.dot_general(left, right, (((1,), (1,)), ((), ())), preferred_element_type=F32)


def three(high, low, parts):
    return mul(high, parts[0]) + mul(low, parts[0]) + mul(high, parts[1])


def pack_edge(value):
    main = value[:PACKED]
    lane = lax.broadcasted_iota(jnp.int32, (TAIL, LANES), 1)
    rows = []
    for k in range(3):
        tail = pltpu.roll(value[PACKED:], (EDGE - 32 * k) % LANES, 1)
        rows.append(jnp.where(lane < EDGE, main[k * TAIL : (k + 1) * TAIL], tail))
    return jnp.concatenate(rows, axis=0)


def unpack_edge(value):
    lane = lax.broadcasted_iota(jnp.int32, (TAIL, LANES), 1)
    tail = jnp.zeros((TAIL, LANES), F32)
    for k in range(3):
        moved = pltpu.roll(value[k * TAIL : (k + 1) * TAIL], (32 * k - EDGE) % LANES, 1)
        tail = jnp.where((lane >= 32 * k) & (lane < 32 * k + 32), moved, tail)
    return jnp.concatenate([value, tail], axis=0)


def each(count, step, loop=True):
    if not loop:
        for k in range(count):
            step(k)
        return

    def run(k, carry):
        step(k)
        return carry

    lax.fori_loop(0, count, run, 0)


def emit_edges(field, below_inner, edge_ref, xl_ref, xh_ref, inner_ref, outer_ref):
    def step(o):
        value = field[o]
        high, low = split(value)
        picked = mul(high, edge_ref[...]) + mul(low, edge_ref[...])
        xl_ref[o] = pack_edge(value[:, :LANES])
        xh_ref[o] = pack_edge(pltpu.roll(value[:, LANES:], LANES - 32, 1))
        bottom, top = pack_edge(picked[:, :LANES]), pack_edge(picked[:, LANES:])
        inner_ref[o] = jnp.where(below_inner, bottom, top)
        outer_ref[o] = jnp.where(below_inner, top, bottom)

    each(ORB, step, LOOP_B)


def to_columns(source, near, far):
    for y in range(CY):
        at = y * NZ
        line = source(at)
        near[pl.ds(y, CX, stride=CY), :] = line[:, :LANES]
        tail = line[:, LANES:]
        far[pl.ds(y, CX, stride=CY), :] = jnp.concatenate([tail, jnp.zeros((CX, 2 * LANES - NZ), F32)], axis=1)
    return jnp.concatenate([jnp.transpose(near[...]), jnp.transpose(far[...])[: NZ - LANES]], axis=0)


def from_columns(value, near, far):
    near[...] = jnp.transpose(value[:LANES])
    far[...] = jnp.transpose(jnp.concatenate([value[LANES:], jnp.zeros((2 * LANES - NZ, LANES), F32)], axis=0))
    for y in range(0, CY, 2):
        lines = []
        for at in (y, y + 1):
            lines.append(near[pl.ds(at, CX, stride=CY), :])
            lines.append(far[pl.ds(at, CX, stride=CY), :][:, : NZ - LANES])
        yield y * NZ, jnp.concatenate(lines, axis=1)


def flag(params, row):
    return params[row : row + 1, :] == 1.0


def begin_kernel(
    place, upper_edge, lower_edge, weights, column_in, shift_in, owner_in, atom_in, raw_in, proj_in, pot_in, energy_in,
    keep, params, ints, table, local, note,
    column, shift, owner, atom, raw, proj, potential, energy, turned, tables, both, placed, partial, near, far, sems,
):
    pairs = (
        (raw_in, raw), (column_in, column), (shift_in, shift), (owner_in, owner),
        (atom_in, atom), (proj_in, proj), (pot_in, potential), (energy_in, energy),
    )
    copies = [pltpu.make_async_copy(source, target, sems.at[k]) for k, (source, target) in enumerate(pairs)]
    for copy in copies:
        copy.start()
    side, core = place[0], place[1]
    upper = jnp.full((1, LANES), side, jnp.int32) == 1
    params[0:1] = jnp.full((1, LANES), side, jnp.int32).astype(F32)
    params[1:2] = jnp.full((1, LANES), core, jnp.int32).astype(F32)
    top = jnp.full((1, LANES), upper_edge[0], F32)
    bottom = jnp.full((1, LANES), lower_edge[0], F32)
    half_width = (top - bottom) / 2.0
    params[2:3] = (top + bottom) / 2.0
    params[3:4] = 1.0 / half_width
    params[4:5] = 2.0 / half_width
    params[5:6] = jnp.full((1, LANES), place[2], jnp.int32).astype(F32)
    params[6:8] = jnp.zeros((2, LANES), F32)
    for o in range(ORB):
        params[8 + o : 9 + o] = jnp.full((1, LANES), weights[side * ORB + o], F32)
    params[8 + ORB :] = jnp.zeros((8 - ORB, LANES), F32)
    sub = jnp.full((1, PIECES), side, jnp.int32)
    for copy in copies[:5]:
        copy.wait()
    step_x = (owner[...] >= 3).astype(jnp.int32) + (owner[...] >= 6).astype(jnp.int32)
    row = owner[...] - 3 * step_x
    lines = [
        sub * LANES + column[...],
        shift[...],
        row * 4 + sub + step_x,
        atom[...],
        column[...],
    ]
    gap = jnp.full((1, OWN - PIECES), -1, jnp.int32)
    for k, line in enumerate(lines):
        ints[k : k + 1] = jnp.concatenate([line, gap], axis=1)
    ints[len(lines) :] = jnp.zeros((8 - len(lines), OWN), jnp.int32)
    def turn(o):
        def kept(at):
            return jnp.where(upper[:, :1], raw[ORB + o, :, at : at + NZ], raw[o, :, at : at + NZ])

        def sent(at):
            return jnp.where(upper[:, :1], raw[o, :, at : at + NZ], raw[ORB + o, :, at : at + NZ])

        turned[o] = to_columns(kept, near, far)
        turned[ORB + o] = to_columns(sent, near, far)
        keep[o] = turned[o]

    each(ORB, turn)
    for copy in copies[5:]:
        copy.wait()
    first_tables(ints, turned, tables, both, proj, placed, partial)
    table[...] = tables[0]
    note[:TABLE] = tables[1]
    lines = to_columns(lambda at: potential[:, at : at + NZ], near, far)
    local[...] = lines
    note[TABLE:NOTE] = lines
    note[NOTE : NOTE + NPJ] = energy[...]
    note[NOTE + NPJ : NOTE + 8] = jnp.zeros((4, LANES), F32)
    numbers = ints[:4].astype(F32)
    for k in range(OWN // LANES):
        note[NOTE + 8 + 4 * k : NOTE + 12 + 4 * k] = numbers[:, k * LANES : (k + 1) * LANES]


def start_kernel(params, keep, came, edge, field, xl, xh, inner, outer, near, far):
    upper = flag(params, 0)

    def step(o):
        turned = to_columns(lambda at: came[o, :, at : at + NZ], near, far)
        kept = keep[o]
        field[o, :, :LANES] = jnp.where(upper, turned, kept)
        field[o, :, LANES:] = jnp.where(upper, kept, turned)

    each(ORB, step)
    emit_edges(field, flag(params, 1), edge, xl, xh, inner, outer)


def gate_kernel(came, note_came, proj, out):
    pass


def prepare_kernel(ints, note_came, own, came, placed, index):
    lines = [note_came[NOTE + 8 + 4 * k : NOTE + 12 + 4 * k] for k in range(OWN // LANES)]
    other = jnp.concatenate(lines, axis=1)[:, :PIECES].astype(jnp.int32)
    index[...] = jnp.concatenate([ints[:4, :PIECES], other], axis=1)

    def step(j):
        both = jnp.concatenate([own[j], came[j]], axis=0)
        for k in range(ALL // LANES):
            at = slice(k * LANES, (k + 1) * LANES)
            placed[j, :, at] = shifted(both[at], ints_row(index, at))

    each(NPJ, step)


def ints_row(index, at):
    return index[1:2, at]


def column_hot(index, at, wide):
    where = lax.broadcasted_iota(jnp.int32, (COLS, wide), 0) == index[0:1, pl.ds(at, wide)]
    return where.astype(F32).astype(BF16)


def chunks(step):
    each(ALL // 256, lambda k: step(k * 256, 256), LOOP_A)
    step(ALL - LANES, LANES)


def atom_hot(index):
    codes = index[3:4, :]
    return (lax.broadcasted_iota(jnp.int32, (SLOTS, codes.shape[1]), 0) == codes).astype(F32).astype(BF16)


def shifted(block, shift):
    block = jnp.concatenate([jnp.transpose(block), jnp.zeros((NZ - PTS, LANES), F32)], axis=0)
    for bit in (64, 32, 16, 8, 4, 2, 1):
        block = jnp.where((shift & bit) != 0, pltpu.roll(block, bit, 0), block)
    return block


def gather_table(index, spread):
    codes = index[2:3, :]
    rows = jnp.concatenate([jnp.where(codes == code, spread, 0.0) for code in range(CODES)], axis=0)
    high, low = split(rows)
    atoms = atom_hot(index)
    return mul_t(high, atoms) + mul_t(low, atoms)


def project(both, hot, placed, partial, at, wide):
    picked = mul(both, jnp.concatenate([hot, hot], axis=0))
    for j in range(NPJ):
        values = placed[j, :, pl.ds(at, wide)]
        for o in range(ORB):
            term = picked[o * NZ : (o + 1) * NZ] * values
            row = o * NPJ + j
            partial[row : row + 1, pl.ds(at, wide)] = jnp.sum(term, axis=0, keepdims=True)


def first_tables(index, turned, tables, both, proj, placed, partial):
    blocks = OWN // LANES

    def place(j):
        for k in range(blocks):
            block = proj[j, k * LANES : min((k + 1) * LANES, PIECES)]
            if k == blocks - 1:
                block = jnp.concatenate([block, jnp.zeros((OWN - PIECES, LANES), F32)], axis=0)
            placed[j, :, k * LANES : (k + 1) * LANES] = shifted(block, index[1:2, k * LANES : (k + 1) * LANES])

    each(NPJ, place)

    def table(s):
        for o in range(ORB):
            both[o * NZ : (o + 1) * NZ, :] = jnp.concatenate(split(turned[s * ORB + o]), axis=1)

        def chunk(k):
            at = pl.multiple_of(k * 256, 256)
            where = lax.broadcasted_iota(jnp.int32, (LANES, 256), 0) == index[4:5, pl.ds(at, 256)]
            project(both[...], where.astype(F32).astype(BF16), placed, partial, at, 256)

        each(OWN // 256, chunk)
        tables[s] = gather_table(index, partial[...])

    each(2, table)


def table_kernel(index, field, placed, table, partial, both):
    def gather(o):
        rows = pl.ds(o * NZ, NZ)
        both[rows, :] = jnp.concatenate(split(field[o]), axis=1)

    each(ORB, gather, LOOP_B)
    chunks(lambda at, wide: project(both[...], column_hot(index, at, wide), placed, partial, at, wide))
    table[...] = gather_table(index, partial[...])


def pair_sum(second, table, came):
    gap = jnp.zeros((THIRD, LANES), F32)
    up = table[THIRD:] + jnp.concatenate([came[HALF:], gap], axis=0)
    down = table[:HALF] + jnp.concatenate([gap, came[:THIRD]], axis=0)
    return jnp.where(second, up, down)


def join_table_kernel(params, table, local, note_came, field, out, pot):
    out[...] = table[...] + note_came[:TABLE]
    upper = flag(params, 0)
    there = note_came[TABLE:NOTE]
    pot[:, :LANES] = jnp.where(upper, there, local[...])
    pot[:, LANES:] = jnp.where(upper, local[...], there)


def first_pair_kernel(params, table, came, energy, note_came, half):
    half[:HALF] = pair_sum(flag(params, 1), table[...], came[...])
    upper = flag(params, 0)
    there = note_came[NOTE : NOTE + NPJ]
    half[HALF : HALF + NPJ] = jnp.where(upper, there, energy[...])
    half[HALF + NPJ :] = jnp.where(upper, energy[...], there)


def pair_kernel(params, table, came, half):
    half[...] = pair_sum(flag(params, 1), table[...], came[...])


def sum_kernel(mine, came, acc, low, high, acc_out):
    total = mine[:HALF] + came[:HALF]
    step = 2 * ROWS
    for q in range(2):
        low[q * step : (q + 1) * step] = total[2 * q * step : (2 * q + 1) * step]
        high[q * step : (q + 1) * step] = total[(2 * q + 1) * step : (2 * q + 2) * step]


def first_sum_kernel(params, mine, came, acc, low, high, acc_out):
    sum_kernel(mine, came, acc, low, high, acc_out)
    second = flag(params, 1)
    for sub, out in ((0, low), (1, high)):
        at = HALF + sub * NPJ
        here, there = mine[at : at + NPJ], came[at : at + NPJ]
        out[THIRD : THIRD + NPJ] = jnp.where(second, here, there)
        out[THIRD + NPJ :] = jnp.where(second, there, here)


def spread_energy(low, high, below, above, energy):
    for q in range(2):
        at = slice(THIRD + q * NPJ, THIRD + (q + 1) * NPJ)
        for r, source in enumerate((below, low, high, above)):
            row = (q * 4 + r) * ROWS
            energy[row : row + ROWS] = jnp.concatenate([source[at]] * ORB, axis=0)


def scale_of(first, params):
    row = 3 if first else 4
    return params[row : row + 1, 0:1]


def total_kernel(first, params, low, high, below, above, acc, energy, out, acc_out, energy_out=None):
    if first:
        spread_energy(low, high, below, above, energy_out)
        energy = energy_out
    step = 2 * ROWS
    scale = params[3 if first else 4 : 4 if first else 5, :]
    for q in range(2):
        at = slice(q * step, (q + 1) * step)
        row = 2 * q * step
        out[row : row + step] = (low[at] + below[at]) * energy[row : row + step] * scale
        row = row + step
        out[row : row + step] = (high[at] + above[at]) * energy[row : row + step] * scale


def first_total_kernel(params, low, high, below, above, acc, out, energy, acc_out):
    total_kernel(True, params, low, high, below, above, acc, None, out, acc_out, energy)


def later_total_kernel(params, low, high, below, above, energy, acc, out, acc_out):
    total_kernel(False, params, low, high, below, above, acc, energy, out, acc_out)


def local_kernel(first, params, half, field, before, pot, own_w, ring_w, out):
    center = params[2:3, 0:1]
    scale = scale_of(first, params)
    diagonal = pot[...] + (3.0 * WEIGHTS[0] * KINETIC - center)

    def step(o):
        value = field[o]
        high, low = split(value)
        across = three(high, low, own_w)
        along = mul(ring_w[0], high) + mul(ring_w[0], low) + mul(ring_w[1], high)
        total = scale * (across + along + diagonal * value)
        out[o] = total if first else total - before[o]

    each(ORB, step)


def halo_kernel(first, params, inner, outer, xl, xh, acc, halo_w, out):
    scale = scale_of(first, params)
    below_inner = flag(params, 1)

    def step(o):
        inside, outside = unpack_edge(inner[o]), unpack_edge(outer[o])
        bottom = jnp.where(below_inner, inside, outside)
        top = jnp.where(below_inner, outside, inside)
        line = jnp.concatenate([unpack_edge(xl[o]), unpack_edge(xh[o]), bottom, top], axis=1)
        high, low = split(line)
        out[o] = acc[o] + scale * three(high, low, halo_w)

    each(ORB, step)


def update_kernel(last, params, index, acc, mine, came, placed, *rest):
    if last:
        kept, sent, field, coef_rows, near_sums, near, far = rest
    else:
        edge, field, xl, xh, inner, outer, coef_rows, near_sums = rest
    second = flag(params, 1)
    total = jnp.concatenate(
        [jnp.where(second, came[THIRD:], mine[...][:THIRD]), jnp.where(second, mine[...][:THIRD], mine[...][THIRD:]),
         jnp.where(second, mine[...][THIRD:], came[:THIRD])], axis=0
    )
    atoms = atom_hot(index)
    spread = mul(jnp.concatenate(split(total), axis=1), jnp.concatenate([atoms, atoms], axis=0))
    codes = index[2:3, :]
    coefs = jnp.zeros((ROWS, ALL), F32)
    for code in range(CODES):
        coefs = jnp.where(codes == code, spread[code * ROWS : (code + 1) * ROWS], coefs)
    near_sums[...] = jnp.zeros((ORB * NZ, COLS), F32)
    coef_rows[...] = coefs

    def chunk(at, wide):
        hot = column_hot(index, at, wide)
        lines = []
        for o in range(ORB):
            rows = coef_rows[o * NPJ : (o + 1) * NPJ, pl.ds(at, wide)]
            line = rows[0:1] * placed[0, :, pl.ds(at, wide)]
            for j in range(1, NPJ):
                line = line + rows[j : j + 1] * placed[j, :, pl.ds(at, wide)]
            lines.append(jnp.concatenate(split(line), axis=1))
        near_sums[...] += mul_t(jnp.concatenate(lines, axis=0), jnp.concatenate([hot, hot], axis=1))

    chunks(chunk)

    def finish(o):
        rows = pl.ds(o * NZ, NZ)
        field[o] = acc[o] + near_sums[rows, :]

    each(ORB, finish, LOOP_B)
    if not last:
        emit_edges(field, second, edge, xl, xh, inner, outer)
        return
    upper = flag(params, 0)

    def emit(o):
        left, right = field[o, :, :LANES], field[o, :, LANES:]
        for spot, pair in from_columns(jnp.where(upper, left, right), near, far):
            sent[o, :, spot : spot + 2 * NZ] = pair
        for spot, pair in from_columns(jnp.where(upper, right, left), near, far):
            kept[o, :, spot : spot + 2 * NZ] = pair

    each(ORB, emit)


def join_kernel(params, came, b, c, d, mine, a, out, density):
    upper = params[0:1, 0:1] == 1.0
    density[...] = a[...] + b[...] + c[...] + d[...]

    def step(o):
        out[o] = jnp.where(upper, came[o], mine[o])
        out[ORB + o] = jnp.where(upper, mine[o], came[o])

    each(ORB, step)


def density_kernel(params, field, quarter, across_x, across_band, across_both, plane, near, far):
    dens = jnp.zeros((NZ, COLS), F32)
    for o in range(ORB):
        dens = dens + params[8 + o : 9 + o, 0:1] * field[o] * field[o]
    left, right = dens[:, :LANES], dens[:, LANES:]
    upper = flag(params, 0)
    second = params[5:6, 0:1] == 1.0
    span = CY * NZ // 2
    for value, same, opposite in (
        (jnp.where(upper, right, left), quarter, across_band),
        (jnp.where(upper, left, right), across_x, across_both),
    ):
        for spot, pair in from_columns(value, near, far):
            plane[:, spot : spot + 2 * NZ] = pair
        same[...] = jnp.where(second, plane[:, span:], plane[:, :span])
        opposite[...] = jnp.where(second, plane[:, :span], plane[:, span:])


VM = pl.BlockSpec(memory_space=pltpu.VMEM)
ANY = pl.BlockSpec(memory_space=pl.ANY)
SM = pl.BlockSpec(memory_space=pltpu.SMEM)
HB = pl.BlockSpec(memory_space=pltpu.HBM)


def call(kernel, in_specs, shapes, args, scratch=(), flops=10**8, name=None, passed=0, room=48):
    single = isinstance(shapes, tuple)
    outs = [shapes] if single else list(shapes)
    outs = [shape if isinstance(shape[0], tuple) else (shape, F32) for shape in outs]
    plain = len(outs) - passed
    result = pl.pallas_call(
        kernel,
        out_shape=[jax.ShapeDtypeStruct(*out) for out in outs],
        in_specs=in_specs,
        out_specs=[VM] * plain + [ANY] * passed,
        scratch_shapes=list(scratch),
        input_output_aliases={len(args) - passed + k: plain + k for k in range(passed)},
        compiler_params=pltpu.CompilerParams(vmem_limit_bytes=room * 1024 * 1024),
        cost_estimate=pl.CostEstimate(flops=flops, bytes_accessed=4 * 10**6, transcendentals=0),
        name=name,
    )(*args)
    return result[0] if single else result


def send(value, pairs):
    return lax.ppermute(value, "dom", pairs)


def along_z(step):
    return [(d, (d + 16 * step) % 64) for d in range(64)]


def outward(d):
    y = d % 8
    return d // 8 * 8 + ((y - 1) % 8 if y % 2 == 0 else (y + 1) % 8)


SWAP = [(d, d ^ 8) for d in range(64)]
CORES = [(d, d ^ 1) for d in range(64)]
OUTER = [(d, outward(d)) for d in range(64)]


def body(
    orbitals,
    occupation,
    potential,
    projectors,
    energies,
    piece_column,
    piece_shift,
    piece_owner,
    piece_atom,
    lower_edge,
    upper_edge,
):
    own_m, halo_m, ring_m, edge_m = stencil_matrices()
    own_w = jnp.asarray(np.stack(two_parts(own_m)))
    halo_w = jnp.asarray(np.stack(two_parts(halo_m)))
    ring_w = jnp.asarray(np.stack(two_parts(ring_m)))
    edge_w = jnp.asarray(edge_m.astype(np.float32).astype(jnp.bfloat16))

    here = lax.axis_index("dom")
    side = (here // 8 % 2).astype(jnp.int32)
    core = (here % 2).astype(jnp.int32)
    place = jnp.stack([side, core, lax.axis_index("band").astype(jnp.int32)])
    packed = (ORB, PACKED, LANES)
    grid = (ORB, NZ, COLS)
    stage = [pltpu.VMEM((LANES, LANES), F32)] * 2

    raw = orbitals[:, 0]
    came = send(lax.dynamic_slice_in_dim(raw, (1 - side) * ORB, ORB, 0), SWAP)
    line = pltpu.VMEM((1, PIECES), jnp.int32)
    keep, params, ints, own_table, local, note = call(
        begin_kernel,
        [SM] * 4 + [HB] * 8,
        [
            (ORB, NZ, LANES),
            (16, LANES),
            ((8, OWN), jnp.int32),
            (TABLE, LANES),
            (NZ, LANES),
            (NOTE + 24, LANES),
        ],
        (
            place, upper_edge, lower_edge, occupation, piece_column, piece_shift, piece_owner, piece_atom,
            raw, projectors[0], potential[0], energies[0],
        ),
        [
            line, line, line, line,
            pltpu.VMEM((2 * ORB, CX, CY * NZ), F32),
            pltpu.VMEM((NPJ, PIECES, LANES), F32),
            pltpu.VMEM((CX, CY * NZ), F32),
            pltpu.VMEM((NPJ, LANES), F32),
            pltpu.VMEM((2 * ORB, NZ, LANES), F32),
            pltpu.VMEM((2, TABLE, LANES), F32),
            pltpu.VMEM((ORB * NZ, 2 * LANES), BF16),
            pltpu.VMEM((NPJ, NZ, OWN), F32),
            pltpu.VMEM((ROWS, OWN), F32),
            *stage,
            pltpu.SemaphoreType.DMA((8,)),
        ],
        name="begin",
        room=ROOM,
    )
    note_came = send(note, SWAP)
    proj = call(gate_kernel, [ANY] * 3, [(NPJ, PIECES, LANES)], (came, note_came, projectors[0]), flops=10**6, name="gate", passed=1)
    proj_came = send(proj[0], SWAP)
    field, xl, xh, inner, outer = call(
        start_kernel,
        [VM] * 4,
        [grid] + [packed] * 4,
        (params, keep, came, edge_w),
        stage,
        name="start",
    )
    table, pot = call(
        join_table_kernel,
        [VM] * 4 + [ANY],
        [(TABLE, LANES), (NZ, COLS)],
        (params, own_table, local, note_came, field),
        flops=10**6,
        name="join_table",
    )
    placed, index = call(
        prepare_kernel,
        [VM] * 4,
        [(NPJ, NZ, ALL), ((4, ALL), jnp.int32)],
        (ints, note_came, projectors[0], proj_came),
        name="prepare",
    )

    sums_room = [pltpu.VMEM((ROWS, ALL), F32), pltpu.VMEM((ORB * NZ, COLS), F32)]
    before = field
    for level in range(DEG):
        first, last = level == 0, level == DEG - 1
        if not first:
            table = call(
                table_kernel,
                [VM] * 3,
                (TABLE, LANES),
                (index, field, placed),
                [pltpu.VMEM((ROWS, ALL), F32), pltpu.VMEM((ORB * NZ, 2 * COLS), BF16)],
                name="table",
            )
        inner_came = send(inner, CORES)
        table_came = send(table, CORES)
        if first:
            half = call(
                first_pair_kernel,
                [VM] * 5,
                (HALF + 8, LANES),
                (params, table, table_came, energies[0], note_came),
                flops=10**6,
                name="pair",
            )
        else:
            half = call(pair_kernel, [VM] * 3, (HALF, LANES), (params, table, table_came), flops=10**6, name="pair")
        half_came = send(half, OUTER)
        xl_came = send(xh, along_z(1))
        xh_came = send(xl, along_z(-1))
        outer_came = send(outer, OUTER)
        acc = call(
            functools.partial(local_kernel, first),
            [VM, ANY] + [VM] * 5,
            grid,
            (params, half, field, before, pot, own_w, ring_w),
            name="local",
        )
        size = (THIRD + 8, LANES) if first else (THIRD, LANES)
        low, high, acc = call(
            first_sum_kernel if first else sum_kernel,
            [VM] * (3 if first else 2) + [ANY],
            [size, size, grid],
            ((params,) if first else ()) + (half, half_came, acc),
            flops=10**6,
            name="sums",
            passed=1,
        )
        below = send(high, along_z(1))
        above = send(low, along_z(-1))
        acc = call(
            functools.partial(halo_kernel, first),
            [VM] * 7,
            grid,
            (params, inner_came, outer_came, xl_came, xh_came, acc, halo_w),
            name="halo",
        )
        if first:
            total, energy, acc = call(
                first_total_kernel,
                [VM] * 5 + [ANY],
                [(HALF, LANES), (HALF, LANES), grid],
                (params, low, high, below, above, acc),
                flops=10**6,
                name="totals",
                passed=1,
            )
        else:
            total, acc = call(
                later_total_kernel,
                [VM] * 6 + [ANY],
                [(HALF, LANES), grid],
                (params, low, high, below, above, energy, acc),
                flops=10**6,
                name="totals",
                passed=1,
            )
        total_came = send(total, CORES)
        args = (params, index, acc, total, total_came, placed)
        if not last:
            before, (field, xl, xh, inner, outer) = field, call(
                functools.partial(update_kernel, last),
                [VM] * 7,
                [grid] + [packed] * 4,
                args + (edge_w,),
                sums_room,
                name="update",
            )
        else:
            flat = (ORB, CX, CY * NZ)
            mine, other, result = call(
                functools.partial(update_kernel, last),
                [VM] * 6,
                [flat, flat, grid],
                args,
                sums_room + stage,
                name="finish",
            )
    part = (CX, CY * NZ // 2)
    quarter, across_x, across_band, across_both = call(
        density_kernel,
        [VM] * 2,
        [part] * 4,
        (params, result),
        [pltpu.VMEM((CX, CY * NZ), F32)] + stage,
        name="density",
    )
    swapped = send(other, SWAP)
    both = [(d, d ^ 72) for d in range(128)]
    filtered, density = call(
        join_kernel,
        [VM] * 7,
        [(2 * ORB, CX, CY * NZ), part],
        (
            params,
            swapped,
            send(across_x, SWAP),
            lax.ppermute(across_band, "band", [(0, 1), (1, 0)]),
            lax.ppermute(across_both, ("band", "dom"), both),
            mine,
            quarter,
        ),
        name="join",
    )
    return filtered[:, None], density[None]


def solution(mesh):
    in_specs = (
        P("band", "dom", None, None),
        P("band"),
        P("dom", None, None),
        P("dom", None, None, None),
        P("dom", None, None),
        P("dom", None),
        P("dom", None),
        P("dom", None),
        P("dom", None),
        P(),
        P(),
    )
    out_specs = (P("band", "dom", None, None), P("dom", None, "band"))
    return jax.shard_map(body, mesh=mesh, in_specs=in_specs, out_specs=out_specs, check_vma=False)
```

```python
import functools

import jax
import jax.numpy as jnp
import numpy as np
from jax import lax
from jax.experimental import pallas as pl
from jax.experimental.pallas import tpu as pltpu
from jax.sharding import PartitionSpec as P

NZ = 192
HALO = 6
DEG = 4
CX = 8
CY = 16
WX = 2 * CX
COLS = WX * CY
ORB = 4
NPJ = 4
PIECES = 448
ALL = 2 * PIECES
PTS = 128
SLOTS = 128
ROWS = ORB * NPJ
PACKED = 144
TAIL = NZ - PACKED
LANES = 128
EDGE = HALO * 16
OWN = 512
ROOM = 58
LOOP_A = False
LOOP_B = False
CODES = 12
TABLE = CODES * ROWS
THIRD = TABLE // 3
HALF = 2 * THIRD
NOTE = TABLE

WEIGHTS = (
    -5369.0 / 1800.0,
    12.0 / 7.0,
    -15.0 / 56.0,
    10.0 / 189.0,
    -1.0 / 112.0,
    2.0 / 1925.0,
    -1.0 / 16632.0,
)
KINETIC = -0.5 / 0.16
F32 = jnp.float32
BF16 = jnp.bfloat16


def coupling(steps):
    reach = np.abs(steps)
    near = (reach >= 1) & (reach <= HALO)
    table = np.array(WEIGHTS) * KINETIC
    return np.where(near, table[np.minimum(reach, HALO)], 0.0)


def stencil_matrices():
    col = np.arange(COLS)
    x, y = col // CY, col % CY
    same_x = x[:, None] == x[None, :]
    same_y = y[:, None] == y[None, :]
    own = np.where(same_y, coupling(x[None, :] - x[:, None]), 0.0)
    own = own + np.where(same_x, coupling(y[None, :] - y[:, None]), 0.0)
    lane = np.arange(LANES)
    used = (lane < EDGE)[:, None]
    parts = []
    for start in (-HALO, WX):
        hx, hy = start + lane // CY, lane % CY
        parts.append(np.where(used & (hy[:, None] == y[None, :]), coupling(x[None, :] - hx[:, None]), 0.0))
    for start in (-HALO, CY):
        hy, hx = start + lane // WX, lane % WX
        parts.append(np.where(used & (hx[:, None] == x[None, :]), coupling(y[None, :] - hy[:, None]), 0.0))
    halo = np.concatenate(parts, axis=0)
    depth = np.arange(NZ)
    apart = (depth[None, :] - depth[:, None] + NZ // 2) % NZ - NZ // 2
    ring = coupling(apart)
    picks = []
    for start in (0, CY - HALO):
        hy, hx = start + lane // WX, lane % WX
        picks.append(np.where(used.T & (col[:, None] == (hx * CY + hy)[None, :]), 1.0, 0.0))
    edge = np.concatenate(picks, axis=1)
    return own, halo, ring, edge


def two_parts(matrix):
    high = np.asarray(matrix, np.float32).astype(jnp.bfloat16)
    low = (np.asarray(matrix, np.float64) - high.astype(np.float64)).astype(np.float32).astype(jnp.bfloat16)
    return high, low


def split(value):
    high = value.astype(BF16)
    low = (value - high.astype(F32)).astype(BF16)
    return high, low


def mul(left, right):
    return jnp.dot(left, right, preferred_element_type=F32)


def mul_t(left, right):
    return lax.dot_general(left, right, (((1,), (1,)), ((), ())), preferred_element_type=F32)


def three(high, low, parts):
    return mul(high, parts[0]) + mul(low, parts[0]) + mul(high, parts[1])


def pack_edge(value):
    main = value[:PACKED]
    lane = lax.broadcasted_iota(jnp.int32, (TAIL, LANES), 1)
    rows = []
    for k in range(3):
        tail = pltpu.roll(value[PACKED:], (EDGE - 32 * k) % LANES, 1)
        rows.append(jnp.where(lane < EDGE, main[k * TAIL : (k + 1) * TAIL], tail))
    return jnp.concatenate(rows, axis=0)


def unpack_edge(value):
    lane = lax.broadcasted_iota(jnp.int32, (TAIL, LANES), 1)
    tail = jnp.zeros((TAIL, LANES), F32)
    for k in range(3):
        moved = pltpu.roll(value[k * TAIL : (k + 1) * TAIL], (32 * k - EDGE) % LANES, 1)
        tail = jnp.where((lane >= 32 * k) & (lane < 32 * k + 32), moved, tail)
    return jnp.concatenate([value, tail], axis=0)


def each(count, step, loop=True):
    if not loop:
        for k in range(count):
            step(k)
        return

    def run(k, carry):
        step(k)
        return carry

    lax.fori_loop(0, count, run, 0)


def emit_edges(field, below_inner, edge_ref, xl_ref, xh_ref, inner_ref, outer_ref):
    def step(o):
        value = field[o]
        high, low = split(value)
        picked = mul(high, edge_ref[...]) + mul(low, edge_ref[...])
        xl_ref[o] = pack_edge(value[:, :LANES])
        xh_ref[o] = pack_edge(pltpu.roll(value[:, LANES:], LANES - 32, 1))
        bottom, top = pack_edge(picked[:, :LANES]), pack_edge(picked[:, LANES:])
        inner_ref[o] = jnp.where(below_inner, bottom, top)
        outer_ref[o] = jnp.where(below_inner, top, bottom)

    each(ORB, step, LOOP_B)


def to_columns(source, near, far):
    for y in range(CY):
        at = y * NZ
        line = source(at)
        near[pl.ds(y, CX, stride=CY), :] = line[:, :LANES]
        tail = line[:, LANES:]
        far[pl.ds(y, CX, stride=CY), :] = jnp.concatenate([tail, jnp.zeros((CX, 2 * LANES - NZ), F32)], axis=1)
    return jnp.concatenate([jnp.transpose(near[...]), jnp.transpose(far[...])[: NZ - LANES]], axis=0)


def from_columns(value, near, far):
    near[...] = jnp.transpose(value[:LANES])
    far[...] = jnp.transpose(jnp.concatenate([value[LANES:], jnp.zeros((2 * LANES - NZ, LANES), F32)], axis=0))
    for y in range(0, CY, 2):
        lines = []
        for at in (y, y + 1):
            lines.append(near[pl.ds(at, CX, stride=CY), :])
            lines.append(far[pl.ds(at, CX, stride=CY), :][:, : NZ - LANES])
        yield y * NZ, jnp.concatenate(lines, axis=1)


def flag(params, row):
    return params[row : row + 1, :] == 1.0


def begin_kernel(
    place, upper_edge, lower_edge, weights, column_in, shift_in, owner_in, atom_in, raw_in, proj_in, energy_in,
    keep, params, ints, table, note,
    column, shift, owner, atom, raw, proj, energy, turned, tables, both, placed, partial, near, far, sems,
):
    pairs = (
        (raw_in, raw), (column_in, column), (shift_in, shift), (owner_in, owner),
        (atom_in, atom), (proj_in, proj), (energy_in, energy),
    )
    copies = [pltpu.make_async_copy(source, target, sems.at[k]) for k, (source, target) in enumerate(pairs)]
    for copy in copies:
        copy.start()
    side, core = place[0], place[1]
    upper = jnp.full((1, LANES), side, jnp.int32) == 1
    params[0:1] = jnp.full((1, LANES), side, jnp.int32).astype(F32)
    params[1:2] = jnp.full((1, LANES), core, jnp.int32).astype(F32)
    top = jnp.full((1, LANES), upper_edge[0], F32)
    bottom = jnp.full((1, LANES), lower_edge[0], F32)
    half_width = (top - bottom) / 2.0
    params[2:3] = (top + bottom) / 2.0
    params[3:4] = 1.0 / half_width
    params[4:5] = 2.0 / half_width
    params[5:6] = jnp.full((1, LANES), place[2], jnp.int32).astype(F32)
    params[6:8] = jnp.zeros((2, LANES), F32)
    for o in range(ORB):
        params[8 + o : 9 + o] = jnp.full((1, LANES), weights[side * ORB + o], F32)
    params[8 + ORB :] = jnp.zeros((8 - ORB, LANES), F32)
    sub = jnp.full((1, PIECES), side, jnp.int32)
    for copy in copies[:5]:
        copy.wait()
    step_x = (owner[...] >= 3).astype(jnp.int32) + (owner[...] >= 6).astype(jnp.int32)
    row = owner[...] - 3 * step_x
    lines = [
        sub * LANES + column[...],
        shift[...],
        row * 4 + sub + step_x,
        atom[...],
        column[...],
    ]
    gap = jnp.full((1, OWN - PIECES), -1, jnp.int32)
    for k, line in enumerate(lines):
        ints[k : k + 1] = jnp.concatenate([line, gap], axis=1)
    ints[len(lines) :] = jnp.zeros((8 - len(lines), OWN), jnp.int32)
    def turn(o):
        def kept(at):
            return jnp.where(upper[:, :1], raw[ORB + o, :, at : at + NZ], raw[o, :, at : at + NZ])

        def sent(at):
            return jnp.where(upper[:, :1], raw[o, :, at : at + NZ], raw[ORB + o, :, at : at + NZ])

        turned[o] = to_columns(kept, near, far)
        turned[ORB + o] = to_columns(sent, near, far)
        keep[o] = turned[o]

    each(ORB, turn)
    for copy in copies[5:]:
        copy.wait()
    first_tables(ints, turned, tables, both, proj, placed, partial)
    table[...] = tables[0]
    note[:TABLE] = tables[1]
    note[NOTE : NOTE + NPJ] = energy[...]
    note[NOTE + NPJ : NOTE + 8] = jnp.zeros((4, LANES), F32)
    numbers = ints[:4].astype(F32)
    for k in range(OWN // LANES):
        note[NOTE + 8 + 4 * k : NOTE + 12 + 4 * k] = numbers[:, k * LANES : (k + 1) * LANES]


def start_kernel(params, keep, came, potential, edge, field, pot, xl, xh, inner, outer, near, far):
    upper = flag(params, 0)
    here = to_columns(lambda at: potential[0, :, at : at + NZ], near, far)
    there = to_columns(lambda at: came[ORB, :, at : at + NZ], near, far)
    pot[:, :LANES] = jnp.where(upper, there, here)
    pot[:, LANES:] = jnp.where(upper, here, there)

    def step(o):
        turned = to_columns(lambda at: came[o, :, at : at + NZ], near, far)
        kept = keep[o]
        field[o, :, :LANES] = jnp.where(upper, turned, kept)
        field[o, :, LANES:] = jnp.where(upper, kept, turned)

    each(ORB, step)
    emit_edges(field, flag(params, 1), edge, xl, xh, inner, outer)


def gate_kernel(came, note_came, proj, out):
    pass


def prepare_kernel(ints, note_came, own, came, placed, index):
    lines = [note_came[NOTE + 8 + 4 * k : NOTE + 12 + 4 * k] for k in range(OWN // LANES)]
    other = jnp.concatenate(lines, axis=1)[:, :PIECES].astype(jnp.int32)
    index[...] = jnp.concatenate([ints[:4, :PIECES], other], axis=1)

    def step(j):
        both = jnp.concatenate([own[j], came[j]], axis=0)
        for k in range(ALL // LANES):
            at = slice(k * LANES, (k + 1) * LANES)
            placed[j, :, at] = shifted(both[at], ints_row(index, at))

    each(NPJ, step)


def ints_row(index, at):
    return index[1:2, at]


def column_hot(index, at, wide):
    where = lax.broadcasted_iota(jnp.int32, (COLS, wide), 0) == index[0:1, pl.ds(at, wide)]
    return where.astype(F32).astype(BF16)


def chunks(step):
    each(ALL // 256, lambda k: step(k * 256, 256), LOOP_A)
    step(ALL - LANES, LANES)


def atom_hot(index):
    codes = index[3:4, :]
    return (lax.broadcasted_iota(jnp.int32, (SLOTS, codes.shape[1]), 0) == codes).astype(F32).astype(BF16)


def shifted(block, shift):
    block = jnp.concatenate([jnp.transpose(block), jnp.zeros((NZ - PTS, LANES), F32)], axis=0)
    for bit in (64, 32, 16, 8, 4, 2, 1):
        block = jnp.where((shift & bit) != 0, pltpu.roll(block, bit, 0), block)
    return block


def gather_table(index, spread):
    codes = index[2:3, :]
    rows = jnp.concatenate([jnp.where(codes == code, spread, 0.0) for code in range(CODES)], axis=0)
    high, low = split(rows)
    atoms = atom_hot(index)
    return mul_t(high, atoms) + mul_t(low, atoms)


def project(both, hot, placed, partial, at, wide):
    picked = mul(both, jnp.concatenate([hot, hot], axis=0))
    sums = [None] * ROWS
    for z in range(0, NZ, 8):
        lines = [picked[o * NZ + z : o * NZ + z + 8] for o in range(ORB)]
        for j in range(NPJ):
            values = placed[j, z : z + 8, pl.ds(at, wide)]
            for o in range(ORB):
                term = lines[o] * values
                row = o * NPJ + j
                sums[row] = term if z == 0 else sums[row] + term
    for row in range(ROWS):
        partial[row : row + 1, pl.ds(at, wide)] = jnp.sum(sums[row], axis=0, keepdims=True)


def first_tables(index, turned, tables, both, proj, placed, partial):
    blocks = OWN // LANES

    def place(j):
        for k in range(blocks):
            block = proj[j, k * LANES : min((k + 1) * LANES, PIECES)]
            if k == blocks - 1:
                block = jnp.concatenate([block, jnp.zeros((OWN - PIECES, LANES), F32)], axis=0)
            placed[j, :, k * LANES : (k + 1) * LANES] = shifted(block, index[1:2, k * LANES : (k + 1) * LANES])

    each(NPJ, place)

    def table(s):
        for o in range(ORB):
            both[o * NZ : (o + 1) * NZ, :] = jnp.concatenate(split(turned[s * ORB + o]), axis=1)

        def chunk(k):
            at = k * 256
            where = lax.broadcasted_iota(jnp.int32, (LANES, 256), 0) == index[4:5, pl.ds(at, 256)]
            project(both[...], where.astype(F32).astype(BF16), placed, partial, at, 256)

        each(OWN // 256, chunk, False)
        tables[s] = gather_table(index, partial[...])

    each(2, table)


def table_kernel(index, field, placed, table, partial, both):
    def gather(o):
        rows = pl.ds(o * NZ, NZ)
        both[rows, :] = jnp.concatenate(split(field[o]), axis=1)

    each(ORB, gather, LOOP_B)
    chunks(lambda at, wide: project(both[...], column_hot(index, at, wide), placed, partial, at, wide))
    table[...] = gather_table(index, partial[...])


def pair_sum(second, table, came):
    gap = jnp.zeros((THIRD, LANES), F32)
    up = table[THIRD:] + jnp.concatenate([came[HALF:], gap], axis=0)
    down = table[:HALF] + jnp.concatenate([gap, came[:THIRD]], axis=0)
    return jnp.where(second, up, down)


def join_table_kernel(table, note_came, field, out):
    out[...] = table[...] + note_came[:TABLE]


def first_pair_kernel(params, table, came, energy, note_came, half):
    half[:HALF] = pair_sum(flag(params, 1), table[...], came[...])
    upper = flag(params, 0)
    there = note_came[NOTE : NOTE + NPJ]
    half[HALF : HALF + NPJ] = jnp.where(upper, there, energy[...])
    half[HALF + NPJ :] = jnp.where(upper, energy[...], there)


def pair_kernel(params, table, came, half):
    half[...] = pair_sum(flag(params, 1), table[...], came[...])


def sum_kernel(mine, came, acc, low, high, acc_out):
    total = mine[:HALF] + came[:HALF]
    step = 2 * ROWS
    for q in range(2):
        low[q * step : (q + 1) * step] = total[2 * q * step : (2 * q + 1) * step]
        high[q * step : (q + 1) * step] = total[(2 * q + 1) * step : (2 * q + 2) * step]


def first_sum_kernel(params, mine, came, acc, low, high, acc_out):
    sum_kernel(mine, came, acc, low, high, acc_out)
    second = flag(params, 1)
    for sub, out in ((0, low), (1, high)):
        at = HALF + sub * NPJ
        here, there = mine[at : at + NPJ], came[at : at + NPJ]
        out[THIRD : THIRD + NPJ] = jnp.where(second, here, there)
        out[THIRD + NPJ :] = jnp.where(second, there, here)


def spread_energy(low, high, below, above, energy):
    for q in range(2):
        at = slice(THIRD + q * NPJ, THIRD + (q + 1) * NPJ)
        for r, source in enumerate((below, low, high, above)):
            row = (q * 4 + r) * ROWS
            energy[row : row + ROWS] = jnp.concatenate([source[at]] * ORB, axis=0)


def scale_of(first, params):
    row = 3 if first else 4
    return params[row : row + 1, 0:1]


def total_kernel(first, params, low, high, below, above, acc, energy, out, acc_out, energy_out=None):
    if first:
        spread_energy(low, high, below, above, energy_out)
        energy = energy_out
    step = 2 * ROWS
    scale = params[3 if first else 4 : 4 if first else 5, :]
    for q in range(2):
        at = slice(q * step, (q + 1) * step)
        row = 2 * q * step
        out[row : row + step] = (low[at] + below[at]) * energy[row : row + step] * scale
        row = row + step
        out[row : row + step] = (high[at] + above[at]) * energy[row : row + step] * scale


def first_total_kernel(params, low, high, below, above, acc, out, energy, acc_out):
    total_kernel(True, params, low, high, below, above, acc, None, out, acc_out, energy)


def later_total_kernel(params, low, high, below, above, energy, acc, out, acc_out):
    total_kernel(False, params, low, high, below, above, acc, energy, out, acc_out)


def local_kernel(first, params, half, field, before, pot, own_w, ring_w, out):
    center = params[2:3, 0:1]
    scale = scale_of(first, params)
    diagonal = pot[...] + (3.0 * WEIGHTS[0] * KINETIC - center)

    def step(o):
        value = field[o]
        high, low = split(value)
        across = three(high, low, own_w)
        along = mul(ring_w[0], high) + mul(ring_w[0], low) + mul(ring_w[1], high)
        total = scale * (across + along + diagonal * value)
        out[o] = total if first else total - before[o]

    each(ORB, step)


def halo_kernel(first, params, inner, outer, xl, xh, acc, halo_w, out):
    scale = scale_of(first, params)
    below_inner = flag(params, 1)

    def step(o):
        inside, outside = unpack_edge(inner[o]), unpack_edge(outer[o])
        bottom = jnp.where(below_inner, inside, outside)
        top = jnp.where(below_inner, outside, inside)
        line = jnp.concatenate([unpack_edge(xl[o]), unpack_edge(xh[o]), bottom, top], axis=1)
        high, low = split(line)
        out[o] = acc[o] + scale * three(high, low, halo_w)

    each(ORB, step)


def update_kernel(last, params, index, acc, mine, came, placed, *rest):
    if last:
        kept, sent, field, coef_rows, near_sums, near, far = rest
    else:
        edge, field, xl, xh, inner, outer, coef_rows, near_sums = rest
    second = flag(params, 1)
    total = jnp.concatenate(
        [jnp.where(second, came[THIRD:], mine[...][:THIRD]), jnp.where(second, mine[...][:THIRD], mine[...][THIRD:]),
         jnp.where(second, mine[...][THIRD:], came[:THIRD])], axis=0
    )
    atoms = atom_hot(index)
    spread = mul(jnp.concatenate(split(total), axis=1), jnp.concatenate([atoms, atoms], axis=0))
    codes = index[2:3, :]
    coefs = jnp.zeros((ROWS, ALL), F32)
    for code in range(CODES):
        coefs = jnp.where(codes == code, spread[code * ROWS : (code + 1) * ROWS], coefs)
    near_sums[...] = jnp.zeros((ORB * NZ, COLS), F32)
    coef_rows[...] = coefs

    def chunk(at, wide):
        hot = column_hot(index, at, wide)
        lines = []
        for o in range(ORB):
            rows = coef_rows[o * NPJ : (o + 1) * NPJ, pl.ds(at, wide)]
            line = rows[0:1] * placed[0, :, pl.ds(at, wide)]
            for j in range(1, NPJ):
                line = line + rows[j : j + 1] * placed[j, :, pl.ds(at, wide)]
            lines.append(jnp.concatenate(split(line), axis=1))
        near_sums[...] += mul_t(jnp.concatenate(lines, axis=0), jnp.concatenate([hot, hot], axis=1))

    chunks(chunk)

    def finish(o):
        rows = pl.ds(o * NZ, NZ)
        field[o] = acc[o] + near_sums[rows, :]

    each(ORB, finish, LOOP_B)
    if not last:
        emit_edges(field, second, edge, xl, xh, inner, outer)
        return
    upper = flag(params, 0)

    def emit(o):
        left, right = field[o, :, :LANES], field[o, :, LANES:]
        for spot, pair in from_columns(jnp.where(upper, left, right), near, far):
            sent[o, :, spot : spot + 2 * NZ] = pair
        for spot, pair in from_columns(jnp.where(upper, right, left), near, far):
            kept[o, :, spot : spot + 2 * NZ] = pair

    each(ORB, emit)


def join_kernel(params, came, b, c, d, mine, a, out, density):
    upper = params[0:1, 0:1] == 1.0
    density[...] = a[...] + b[...] + c[...] + d[...]

    def step(o):
        out[o] = jnp.where(upper, came[o], mine[o])
        out[ORB + o] = jnp.where(upper, mine[o], came[o])

    each(ORB, step)


def density_kernel(params, field, quarter, across_x, across_band, across_both, plane, near, far):
    dens = jnp.zeros((NZ, COLS), F32)
    for o in range(ORB):
        dens = dens + params[8 + o : 9 + o, 0:1] * field[o] * field[o]
    left, right = dens[:, :LANES], dens[:, LANES:]
    upper = flag(params, 0)
    second = params[5:6, 0:1] == 1.0
    span = CY * NZ // 2
    for value, same, opposite in (
        (jnp.where(upper, right, left), quarter, across_band),
        (jnp.where(upper, left, right), across_x, across_both),
    ):
        for spot, pair in from_columns(value, near, far):
            plane[:, spot : spot + 2 * NZ] = pair
        same[...] = jnp.where(second, plane[:, span:], plane[:, :span])
        opposite[...] = jnp.where(second, plane[:, :span], plane[:, span:])


VM = pl.BlockSpec(memory_space=pltpu.VMEM)
ANY = pl.BlockSpec(memory_space=pl.ANY)
SM = pl.BlockSpec(memory_space=pltpu.SMEM)
HB = pl.BlockSpec(memory_space=pltpu.HBM)


def call(kernel, in_specs, shapes, args, scratch=(), flops=10**8, name=None, passed=0, room=48):
    single = isinstance(shapes, tuple)
    outs = [shapes] if single else list(shapes)
    outs = [shape if isinstance(shape[0], tuple) else (shape, F32) for shape in outs]
    plain = len(outs) - passed
    result = pl.pallas_call(
        kernel,
        out_shape=[jax.ShapeDtypeStruct(*out) for out in outs],
        in_specs=in_specs,
        out_specs=[VM] * plain + [ANY] * passed,
        scratch_shapes=list(scratch),
        input_output_aliases={len(args) - passed + k: plain + k for k in range(passed)},
        compiler_params=pltpu.CompilerParams(vmem_limit_bytes=room * 1024 * 1024),
        cost_estimate=pl.CostEstimate(flops=flops, bytes_accessed=4 * 10**6, transcendentals=0),
        name=name,
    )(*args)
    return result[0] if single else result


def send(value, pairs):
    return lax.ppermute(value, "dom", pairs)


def along_z(step):
    return [(d, (d + 16 * step) % 64) for d in range(64)]


def outward(d):
    y = d % 8
    return d // 8 * 8 + ((y - 1) % 8 if y % 2 == 0 else (y + 1) % 8)


SWAP = [(d, d ^ 8) for d in range(64)]
CORES = [(d, d ^ 1) for d in range(64)]
OUTER = [(d, outward(d)) for d in range(64)]


def body(
    orbitals,
    occupation,
    potential,
    projectors,
    energies,
    piece_column,
    piece_shift,
    piece_owner,
    piece_atom,
    lower_edge,
    upper_edge,
):
    own_m, halo_m, ring_m, edge_m = stencil_matrices()
    own_w = jnp.asarray(np.stack(two_parts(own_m)))
    halo_w = jnp.asarray(np.stack(two_parts(halo_m)))
    ring_w = jnp.asarray(np.stack(two_parts(ring_m)))
    edge_w = jnp.asarray(edge_m.astype(np.float32).astype(jnp.bfloat16))

    here = lax.axis_index("dom")
    side = (here // 8 % 2).astype(jnp.int32)
    core = (here % 2).astype(jnp.int32)
    place = jnp.stack([side, core, lax.axis_index("band").astype(jnp.int32)])
    packed = (ORB, PACKED, LANES)
    grid = (ORB, NZ, COLS)
    stage = [pltpu.VMEM((LANES, LANES), F32)] * 2

    raw = orbitals[:, 0]
    going = lax.dynamic_slice_in_dim(raw, (1 - side) * ORB, ORB, 0)
    came = send(jnp.concatenate([going, potential], axis=0), SWAP)
    line = pltpu.VMEM((1, PIECES), jnp.int32)
    keep, params, ints, own_table, note = call(
        begin_kernel,
        [SM] * 4 + [HB] * 7,
        [
            (ORB, NZ, LANES),
            (16, LANES),
            ((8, OWN), jnp.int32),
            (TABLE, LANES),
            (NOTE + 24, LANES),
        ],
        (
            place, upper_edge, lower_edge, occupation, piece_column, piece_shift, piece_owner, piece_atom,
            raw, projectors[0], energies[0],
        ),
        [
            line, line, line, line,
            pltpu.VMEM((2 * ORB, CX, CY * NZ), F32),
            pltpu.VMEM((NPJ, PIECES, LANES), F32),
            pltpu.VMEM((NPJ, LANES), F32),
            pltpu.VMEM((2 * ORB, NZ, LANES), F32),
            pltpu.VMEM((2, TABLE, LANES), F32),
            pltpu.VMEM((ORB * NZ, 2 * LANES), BF16),
            pltpu.VMEM((NPJ, NZ, OWN), F32),
            pltpu.VMEM((ROWS, OWN), F32),
            *stage,
            pltpu.SemaphoreType.DMA((7,)),
        ],
        name="begin",
        room=ROOM,
    )
    note_came = send(note, SWAP)
    proj = call(gate_kernel, [ANY] * 3, [(NPJ, PIECES, LANES)], (came, note_came, projectors[0]), flops=10**6, name="gate", passed=1)
    proj_came = send(proj[0], SWAP)
    field, pot, xl, xh, inner, outer = call(
        start_kernel,
        [VM] * 5,
        [grid, (NZ, COLS)] + [packed] * 4,
        (params, keep, came, potential, edge_w),
        stage,
        name="start",
    )
    table = call(
        join_table_kernel, [VM] * 2 + [ANY], (TABLE, LANES), (own_table, note_came, field), flops=10**6, name="join_table"
    )
    placed, index = call(
        prepare_kernel,
        [VM] * 4,
        [(NPJ, NZ, ALL), ((4, ALL), jnp.int32)],
        (ints, note_came, projectors[0], proj_came),
        name="prepare",
    )

    sums_room = [pltpu.VMEM((ROWS, ALL), F32), pltpu.VMEM((ORB * NZ, COLS), F32)]
    before = field
    for level in range(DEG):
        first, last = level == 0, level == DEG - 1
        if not first:
            table = call(
                table_kernel,
                [VM] * 3,
                (TABLE, LANES),
                (index, field, placed),
                [pltpu.VMEM((ROWS, ALL), F32), pltpu.VMEM((ORB * NZ, 2 * COLS), BF16)],
                name="table",
            )
        inner_came = send(inner, CORES)
        table_came = send(table, CORES)
        if first:
            half = call(
                first_pair_kernel,
                [VM] * 5,
                (HALF + 8, LANES),
                (params, table, table_came, energies[0], note_came),
                flops=10**6,
                name="pair",
            )
        else:
            half = call(pair_kernel, [VM] * 3, (HALF, LANES), (params, table, table_came), flops=10**6, name="pair")
        half_came = send(half, OUTER)
        xl_came = send(xh, along_z(1))
        xh_came = send(xl, along_z(-1))
        outer_came = send(outer, OUTER)
        acc = call(
            functools.partial(local_kernel, first),
            [VM, ANY] + [VM] * 5,
            grid,
            (params, half, field, before, pot, own_w, ring_w),
            name="local",
        )
        size = (THIRD + 8, LANES) if first else (THIRD, LANES)
        low, high, acc = call(
            first_sum_kernel if first else sum_kernel,
            [VM] * (3 if first else 2) + [ANY],
            [size, size, grid],
            ((params,) if first else ()) + (half, half_came, acc),
            flops=10**6,
            name="sums",
            passed=1,
        )
        below = send(high, along_z(1))
        above = send(low, along_z(-1))
        acc = call(
            functools.partial(halo_kernel, first),
            [VM] * 7,
            grid,
            (params, inner_came, outer_came, xl_came, xh_came, acc, halo_w),
            name="halo",
        )
        if first:
            total, energy, acc = call(
                first_total_kernel,
                [VM] * 5 + [ANY],
                [(HALF, LANES), (HALF, LANES), grid],
                (params, low, high, below, above, acc),
                flops=10**6,
                name="totals",
                passed=1,
            )
        else:
            total, acc = call(
                later_total_kernel,
                [VM] * 6 + [ANY],
                [(HALF, LANES), grid],
                (params, low, high, below, above, energy, acc),
                flops=10**6,
                name="totals",
                passed=1,
            )
        total_came = send(total, CORES)
        args = (params, index, acc, total, total_came, placed)
        if not last:
            before, (field, xl, xh, inner, outer) = field, call(
                functools.partial(update_kernel, last),
                [VM] * 7,
                [grid] + [packed] * 4,
                args + (edge_w,),
                sums_room,
                name="update",
            )
        else:
            flat = (ORB, CX, CY * NZ)
            mine, other, result = call(
                functools.partial(update_kernel, last),
                [VM] * 6,
                [flat, flat, grid],
                args,
                sums_room + stage,
                name="finish",
            )
    part = (CX, CY * NZ // 2)
    quarter, across_x, across_band, across_both = call(
        density_kernel,
        [VM] * 2,
        [part] * 4,
        (params, result),
        [pltpu.VMEM((CX, CY * NZ), F32)] + stage,
        name="density",
    )
    swapped = send(other, SWAP)
    both = [(d, d ^ 72) for d in range(128)]
    filtered, density = call(
        join_kernel,
        [VM] * 7,
        [(2 * ORB, CX, CY * NZ), part],
        (
            params,
            swapped,
            send(across_x, SWAP),
            lax.ppermute(across_band, "band", [(0, 1), (1, 0)]),
            lax.ppermute(across_both, ("band", "dom"), both),
            mine,
            quarter,
        ),
        name="join",
    )
    return filtered[:, None], density[None]


def solution(mesh):
    in_specs = (
        P("band", "dom", None, None),
        P("band"),
        P("dom", None, None),
        P("dom", None, None, None),
        P("dom", None, None),
        P("dom", None),
        P("dom", None),
        P("dom", None),
        P("dom", None),
        P(),
        P(),
    )
    out_specs = (P("band", "dom", None, None), P("dom", None, "band"))
    return jax.shard_map(body, mesh=mesh, in_specs=in_specs, out_specs=out_specs, check_vma=False)
```

```python
import functools

import jax
import jax.numpy as jnp
import numpy as np
from jax import lax
from jax.experimental import pallas as pl
from jax.experimental.pallas import tpu as pltpu
from jax.sharding import PartitionSpec as P

NZ = 192
HALO = 6
DEG = 4
CX = 8
CY = 16
WX = 2 * CX
COLS = WX * CY
ORB = 4
NPJ = 4
PIECES = 448
ALL = 2 * PIECES
PTS = 128
SLOTS = 128
ROWS = ORB * NPJ
PACKED = 144
TAIL = NZ - PACKED
LANES = 128
EDGE = HALO * 16
OWN = 512
ROOM = 58
CODES = 12
TABLE = CODES * ROWS
THIRD = TABLE // 3
HALF = 2 * THIRD
NOTE = TABLE

WEIGHTS = (
    -5369.0 / 1800.0,
    12.0 / 7.0,
    -15.0 / 56.0,
    10.0 / 189.0,
    -1.0 / 112.0,
    2.0 / 1925.0,
    -1.0 / 16632.0,
)
KINETIC = -0.5 / 0.16
F32 = jnp.float32
BF16 = jnp.bfloat16


def coupling(steps):
    reach = np.abs(steps)
    near = (reach >= 1) & (reach <= HALO)
    table = np.array(WEIGHTS) * KINETIC
    return np.where(near, table[np.minimum(reach, HALO)], 0.0)


def stencil_matrices():
    col = np.arange(COLS)
    x, y = col // CY, col % CY
    same_x = x[:, None] == x[None, :]
    same_y = y[:, None] == y[None, :]
    own = np.where(same_y, coupling(x[None, :] - x[:, None]), 0.0)
    own = own + np.where(same_x, coupling(y[None, :] - y[:, None]), 0.0)
    lane = np.arange(LANES)
    used = (lane < EDGE)[:, None]
    parts = []
    for start in (-HALO, WX):
        hx, hy = start + lane // CY, lane % CY
        parts.append(np.where(used & (hy[:, None] == y[None, :]), coupling(x[None, :] - hx[:, None]), 0.0))
    for start in (-HALO, CY):
        hy, hx = start + lane // WX, lane % WX
        parts.append(np.where(used & (hx[:, None] == x[None, :]), coupling(y[None, :] - hy[:, None]), 0.0))
    halo = np.concatenate(parts, axis=0)
    depth = np.arange(NZ)
    apart = (depth[None, :] - depth[:, None] + NZ // 2) % NZ - NZ // 2
    ring = coupling(apart)
    picks = []
    for start in (0, CY - HALO):
        hy, hx = start + lane // WX, lane % WX
        picks.append(np.where(used.T & (col[:, None] == (hx * CY + hy)[None, :]), 1.0, 0.0))
    edge = np.concatenate(picks, axis=1)
    return own, halo, ring, edge


def two_parts(matrix):
    high = np.asarray(matrix, np.float32).astype(jnp.bfloat16)
    low = (np.asarray(matrix, np.float64) - high.astype(np.float64)).astype(np.float32).astype(jnp.bfloat16)
    return high, low


def split(value):
    high = value.astype(BF16)
    low = (value - high.astype(F32)).astype(BF16)
    return high, low


def mul(left, right):
    return jnp.dot(left, right, preferred_element_type=F32)


def mul_t(left, right):
    return lax.dot_general(left, right, (((1,), (1,)), ((), ())), preferred_element_type=F32)


def three(high, low, parts):
    return mul(high, parts[0]) + mul(low, parts[0]) + mul(high, parts[1])


def pack_edge(value):
    main = value[:PACKED]
    lane = lax.broadcasted_iota(jnp.int32, (TAIL, LANES), 1)
    rows = []
    for k in range(3):
        tail = pltpu.roll(value[PACKED:], (EDGE - 32 * k) % LANES, 1)
        rows.append(jnp.where(lane < EDGE, main[k * TAIL : (k + 1) * TAIL], tail))
    return jnp.concatenate(rows, axis=0)


def unpack_edge(value):
    lane = lax.broadcasted_iota(jnp.int32, (TAIL, LANES), 1)
    tail = jnp.zeros((TAIL, LANES), F32)
    for k in range(3):
        moved = pltpu.roll(value[k * TAIL : (k + 1) * TAIL], (32 * k - EDGE) % LANES, 1)
        tail = jnp.where((lane >= 32 * k) & (lane < 32 * k + 32), moved, tail)
    return jnp.concatenate([value, tail], axis=0)


def each(count, step, loop=True):
    if not loop:
        for k in range(count):
            step(k)
        return

    def run(k, carry):
        step(k)
        return carry

    lax.fori_loop(0, count, run, 0)


def emit_edges(field, below_inner, edge_ref, xl_ref, xh_ref, inner_ref, outer_ref):
    def step(o):
        value = field[o]
        high, low = split(value)
        picked = mul(high, edge_ref[...]) + mul(low, edge_ref[...])
        xl_ref[o] = pack_edge(value[:, :LANES])
        xh_ref[o] = pack_edge(pltpu.roll(value[:, LANES:], LANES - 32, 1))
        bottom, top = pack_edge(picked[:, :LANES]), pack_edge(picked[:, LANES:])
        inner_ref[o] = jnp.where(below_inner, bottom, top)
        outer_ref[o] = jnp.where(below_inner, top, bottom)

    each(ORB, step, False)


def to_columns(source, near, far):
    for y in range(CY):
        at = y * NZ
        line = source(at)
        near[pl.ds(y, CX, stride=CY), :] = line[:, :LANES]
        tail = line[:, LANES:]
        far[pl.ds(y, CX, stride=CY), :] = jnp.concatenate([tail, jnp.zeros((CX, 2 * LANES - NZ), F32)], axis=1)
    return jnp.concatenate([jnp.transpose(near[...]), jnp.transpose(far[...])[: NZ - LANES]], axis=0)


def from_columns(value, near, far):
    near[...] = jnp.transpose(value[:LANES])
    far[...] = jnp.transpose(jnp.concatenate([value[LANES:], jnp.zeros((2 * LANES - NZ, LANES), F32)], axis=0))
    for y in range(0, CY, 2):
        lines = []
        for at in (y, y + 1):
            lines.append(near[pl.ds(at, CX, stride=CY), :])
            lines.append(far[pl.ds(at, CX, stride=CY), :][:, : NZ - LANES])
        yield y * NZ, jnp.concatenate(lines, axis=1)


def flag(params, row):
    return params[row : row + 1, :] == 1.0


def begin_kernel(
    place, upper_in, lower_in, weights_in, column_in, shift_in, owner_in, atom_in, raw_in, proj_in, energy_in,
    keep, params, ints, table, note,
    column, shift, owner, atom, raw, proj, energy, turned, tables, both, placed, partial, near, far, upper_edge, lower_edge, weights, sems,
):
    pairs = (
        (raw_in, raw), (column_in, column), (shift_in, shift), (owner_in, owner),
        (atom_in, atom), (upper_in, upper_edge), (lower_in, lower_edge), (weights_in, weights),
        (proj_in, proj), (energy_in, energy),
    )
    copies = [pltpu.make_async_copy(source, target, sems.at[k]) for k, (source, target) in enumerate(pairs)]
    for copy in copies:
        copy.start()
    for copy in copies[:8]:
        copy.wait()
    side, core = place[0], place[1]
    upper = jnp.full((1, LANES), side, jnp.int32) == 1
    params[0:1] = jnp.full((1, LANES), side, jnp.int32).astype(F32)
    params[1:2] = jnp.full((1, LANES), core, jnp.int32).astype(F32)
    top = jnp.full((1, LANES), upper_edge[0], F32)
    bottom = jnp.full((1, LANES), lower_edge[0], F32)
    half_width = (top - bottom) / 2.0
    params[2:3] = (top + bottom) / 2.0
    params[3:4] = 1.0 / half_width
    params[4:5] = 2.0 / half_width
    params[5:6] = jnp.full((1, LANES), place[2], jnp.int32).astype(F32)
    params[6:8] = jnp.zeros((2, LANES), F32)
    for o in range(ORB):
        params[8 + o : 9 + o] = jnp.full((1, LANES), weights[side * ORB + o], F32)
    params[8 + ORB :] = jnp.zeros((8 - ORB, LANES), F32)
    sub = jnp.full((1, PIECES), side, jnp.int32)
    step_x = (owner[...] >= 3).astype(jnp.int32) + (owner[...] >= 6).astype(jnp.int32)
    row = owner[...] - 3 * step_x
    lines = [
        sub * LANES + column[...],
        shift[...],
        row * 4 + sub + step_x,
        atom[...],
        column[...],
    ]
    gap = jnp.full((1, OWN - PIECES), -1, jnp.int32)
    for k, line in enumerate(lines):
        ints[k : k + 1] = jnp.concatenate([line, gap], axis=1)
    ints[len(lines) :] = jnp.zeros((8 - len(lines), OWN), jnp.int32)
    def turn(o):
        def kept(at):
            return jnp.where(upper[:, :1], raw[ORB + o, :, at : at + NZ], raw[o, :, at : at + NZ])

        def sent(at):
            return jnp.where(upper[:, :1], raw[o, :, at : at + NZ], raw[ORB + o, :, at : at + NZ])

        turned[o] = to_columns(kept, near, far)
        turned[ORB + o] = to_columns(sent, near, far)
        keep[o] = turned[o]

    each(ORB, turn)
    for copy in copies[8:]:
        copy.wait()
    first_tables(ints, turned, tables, both, proj, placed, partial)
    table[...] = tables[0]
    note[:TABLE] = tables[1]
    note[NOTE : NOTE + NPJ] = energy[...]
    note[NOTE + NPJ : NOTE + 8] = jnp.zeros((4, LANES), F32)
    numbers = ints[:4].astype(F32)
    for k in range(OWN // LANES):
        note[NOTE + 8 + 4 * k : NOTE + 12 + 4 * k] = numbers[:, k * LANES : (k + 1) * LANES]


def start_kernel(params, keep, came, potential, edge, field, pot, xl, xh, inner, outer, near, far):
    upper = flag(params, 0)
    here = to_columns(lambda at: potential[0, :, at : at + NZ], near, far)
    there = to_columns(lambda at: came[ORB, :, at : at + NZ], near, far)
    pot[:, :LANES] = jnp.where(upper, there, here)
    pot[:, LANES:] = jnp.where(upper, here, there)

    def step(o):
        turned = to_columns(lambda at: came[o, :, at : at + NZ], near, far)
        kept = keep[o]
        field[o, :, :LANES] = jnp.where(upper, turned, kept)
        field[o, :, LANES:] = jnp.where(upper, kept, turned)

    each(ORB, step, False)
    emit_edges(field, flag(params, 1), edge, xl, xh, inner, outer)


def gate_kernel(came, note_came, proj, out):
    pass


def prepare_kernel(ints, note_came, own, came, placed, index):
    lines = [note_came[NOTE + 8 + 4 * k : NOTE + 12 + 4 * k] for k in range(OWN // LANES)]
    other = jnp.concatenate(lines, axis=1)[:, :PIECES].astype(jnp.int32)
    index[...] = jnp.concatenate([ints[:4, :PIECES], other], axis=1)

    def step(j):
        both = jnp.concatenate([own[j], came[j]], axis=0)
        for k in range(ALL // LANES):
            at = slice(k * LANES, (k + 1) * LANES)
            placed[j, :, at] = shifted(both[at], index[1:2, at])

    each(NPJ, step, False)


def column_hot(index, at, wide):
    where = lax.broadcasted_iota(jnp.int32, (COLS, wide), 0) == index[0:1, pl.ds(at, wide)]
    return where.astype(F32).astype(BF16)


def chunks(step):
    each(ALL // 256, lambda k: step(k * 256, 256), False)
    step(ALL - LANES, LANES)


def atom_hot(index):
    codes = index[3:4, :]
    return (lax.broadcasted_iota(jnp.int32, (SLOTS, codes.shape[1]), 0) == codes).astype(F32).astype(BF16)


def shifted(block, shift):
    block = jnp.concatenate([jnp.transpose(block), jnp.zeros((NZ - PTS, LANES), F32)], axis=0)
    for bit in (64, 32, 16, 8, 4, 2, 1):
        block = jnp.where((shift & bit) != 0, pltpu.roll(block, bit, 0), block)
    return block


def gather_table(index, spread):
    codes = index[2:3, :]
    rows = jnp.concatenate([jnp.where(codes == code, spread, 0.0) for code in range(CODES)], axis=0)
    high, low = split(rows)
    atoms = atom_hot(index)
    return mul_t(high, atoms) + mul_t(low, atoms)


def project(both, hot, placed, partial, at, wide):
    picked = mul(both, jnp.concatenate([hot, hot], axis=0))
    sums = [None] * ROWS
    for z in range(0, NZ, 8):
        lines = [picked[o * NZ + z : o * NZ + z + 8] for o in range(ORB)]
        for j in range(NPJ):
            values = placed[j, z : z + 8, pl.ds(at, wide)]
            for o in range(ORB):
                term = lines[o] * values
                row = o * NPJ + j
                sums[row] = term if z == 0 else sums[row] + term
    for row in range(ROWS):
        partial[row : row + 1, pl.ds(at, wide)] = jnp.sum(sums[row], axis=0, keepdims=True)


def first_tables(index, turned, tables, both, proj, placed, partial):
    blocks = OWN // LANES

    def place(j):
        for k in range(blocks):
            block = proj[j, k * LANES : min((k + 1) * LANES, PIECES)]
            if k == blocks - 1:
                block = jnp.concatenate([block, jnp.zeros((OWN - PIECES, LANES), F32)], axis=0)
            placed[j, :, k * LANES : (k + 1) * LANES] = shifted(block, index[1:2, k * LANES : (k + 1) * LANES])

    each(NPJ, place)

    def table(s):
        for o in range(ORB):
            both[o * NZ : (o + 1) * NZ, :] = jnp.concatenate(split(turned[s * ORB + o]), axis=1)

        def chunk(k):
            at = k * 256
            where = lax.broadcasted_iota(jnp.int32, (LANES, 256), 0) == index[4:5, pl.ds(at, 256)]
            project(both[...], where.astype(F32).astype(BF16), placed, partial, at, 256)

        each(OWN // 256, chunk, False)
        tables[s] = gather_table(index, partial[...])

    each(2, table)


def table_kernel(index, field, placed, table, partial, both):
    def gather(o):
        rows = pl.ds(o * NZ, NZ)
        both[rows, :] = jnp.concatenate(split(field[o]), axis=1)

    each(ORB, gather, False)
    chunks(lambda at, wide: project(both[...], column_hot(index, at, wide), placed, partial, at, wide))
    table[...] = gather_table(index, partial[...])


def pair_sum(second, table, came):
    gap = jnp.zeros((THIRD, LANES), F32)
    up = table[THIRD:] + jnp.concatenate([came[HALF:], gap], axis=0)
    down = table[:HALF] + jnp.concatenate([gap, came[:THIRD]], axis=0)
    return jnp.where(second, up, down)


def join_table_kernel(table, note_came, field, out):
    out[...] = table[...] + note_came[:TABLE]


def first_pair_kernel(params, table, came, energy, note_came, half):
    half[:HALF] = pair_sum(flag(params, 1), table[...], came[...])
    upper = flag(params, 0)
    there = note_came[NOTE : NOTE + NPJ]
    half[HALF : HALF + NPJ] = jnp.where(upper, there, energy[...])
    half[HALF + NPJ :] = jnp.where(upper, energy[...], there)


def pair_kernel(params, table, came, half):
    half[...] = pair_sum(flag(params, 1), table[...], came[...])


def sum_kernel(mine, came, acc, low, high, acc_out):
    total = mine[:HALF] + came[:HALF]
    step = 2 * ROWS
    for q in range(2):
        low[q * step : (q + 1) * step] = total[2 * q * step : (2 * q + 1) * step]
        high[q * step : (q + 1) * step] = total[(2 * q + 1) * step : (2 * q + 2) * step]


def first_sum_kernel(params, mine, came, acc, low, high, acc_out):
    sum_kernel(mine, came, acc, low, high, acc_out)
    second = flag(params, 1)
    for sub, out in ((0, low), (1, high)):
        at = HALF + sub * NPJ
        here, there = mine[at : at + NPJ], came[at : at + NPJ]
        out[THIRD : THIRD + NPJ] = jnp.where(second, here, there)
        out[THIRD + NPJ :] = jnp.where(second, there, here)


def spread_energy(low, high, below, above, energy):
    for q in range(2):
        at = slice(THIRD + q * NPJ, THIRD + (q + 1) * NPJ)
        for r, source in enumerate((below, low, high, above)):
            row = (q * 4 + r) * ROWS
            energy[row : row + ROWS] = jnp.concatenate([source[at]] * ORB, axis=0)


def scale_of(first, params):
    row = 3 if first else 4
    return params[row : row + 1, 0:1]


def total_kernel(first, params, low, high, below, above, acc, energy, out, acc_out, energy_out=None):
    if first:
        spread_energy(low, high, below, above, energy_out)
        energy = energy_out
    step = 2 * ROWS
    scale = params[3 if first else 4 : 4 if first else 5, :]
    for q in range(2):
        at = slice(q * step, (q + 1) * step)
        row = 2 * q * step
        out[row : row + step] = (low[at] + below[at]) * energy[row : row + step] * scale
        row = row + step
        out[row : row + step] = (high[at] + above[at]) * energy[row : row + step] * scale


def first_total_kernel(params, low, high, below, above, acc, out, energy, acc_out):
    total_kernel(True, params, low, high, below, above, acc, None, out, acc_out, energy)


def later_total_kernel(params, low, high, below, above, energy, acc, out, acc_out):
    total_kernel(False, params, low, high, below, above, acc, energy, out, acc_out)


def local_kernel(first, params, half, field, before, pot, own_w, ring_w, out):
    center = params[2:3, 0:1]
    scale = scale_of(first, params)
    diagonal = pot[...] + (3.0 * WEIGHTS[0] * KINETIC - center)

    def step(o):
        value = field[o]
        high, low = split(value)
        across = three(high, low, own_w)
        along = mul(ring_w[0], high) + mul(ring_w[0], low) + mul(ring_w[1], high)
        total = scale * (across + along + diagonal * value)
        out[o] = total if first else total - before[o]

    each(ORB, step)


def halo_kernel(first, params, inner, outer, xl, xh, acc, halo_w, out):
    scale = scale_of(first, params)
    below_inner = flag(params, 1)

    def step(o):
        inside, outside = unpack_edge(inner[o]), unpack_edge(outer[o])
        bottom = jnp.where(below_inner, inside, outside)
        top = jnp.where(below_inner, outside, inside)
        line = jnp.concatenate([unpack_edge(xl[o]), unpack_edge(xh[o]), bottom, top], axis=1)
        high, low = split(line)
        out[o] = acc[o] + scale * three(high, low, halo_w)

    each(ORB, step)


def update_kernel(last, params, index, acc, mine, came, placed, *rest):
    if last:
        sent, field, coef_rows, near, far = rest
    else:
        edge, field, xl, xh, inner, outer, coef_rows = rest
    second = flag(params, 1)
    total = jnp.concatenate(
        [jnp.where(second, came[THIRD:], mine[...][:THIRD]), jnp.where(second, mine[...][:THIRD], mine[...][THIRD:]),
         jnp.where(second, mine[...][THIRD:], came[:THIRD])], axis=0
    )
    atoms = atom_hot(index)
    spread = mul(jnp.concatenate(split(total), axis=1), jnp.concatenate([atoms, atoms], axis=0))
    codes = index[2:3, :]
    coefs = jnp.zeros((ROWS, ALL), F32)
    for code in range(CODES):
        coefs = jnp.where(codes == code, spread[code * ROWS : (code + 1) * ROWS], coefs)
    coef_rows[...] = coefs
    sums = []

    def chunk(at, wide):
        hot = column_hot(index, at, wide)
        lines = []
        for o in range(ORB):
            rows = coef_rows[o * NPJ : (o + 1) * NPJ, pl.ds(at, wide)]
            line = rows[0:1] * placed[0, :, pl.ds(at, wide)]
            for j in range(1, NPJ):
                line = line + rows[j : j + 1] * placed[j, :, pl.ds(at, wide)]
            lines.append(jnp.concatenate(split(line), axis=1))
        term = mul_t(jnp.concatenate(lines, axis=0), jnp.concatenate([hot, hot], axis=1))
        sums[:] = [sums[0] + term if sums else term]

    chunks(chunk)

    def finish(o):
        field[o] = acc[o] + sums[0][o * NZ : (o + 1) * NZ]

    each(ORB, finish, False)
    if not last:
        emit_edges(field, second, edge, xl, xh, inner, outer)
        return
    upper = flag(params, 0)

    def emit(o):
        left, right = field[o, :, :LANES], field[o, :, LANES:]
        for spot, pair in from_columns(jnp.where(upper, left, right), near, far):
            sent[o, :, spot : spot + 2 * NZ] = pair

    each(ORB, emit)


def join_kernel(params, came, b, c, d, mine, a, out, density):
    upper = params[0:1, 0:1] == 1.0
    density[...] = a[...] + b[...] + c[...] + d[...]

    def step(o):
        out[o] = jnp.where(upper, came[o], mine[o])
        out[ORB + o] = jnp.where(upper, mine[o], came[o])

    each(ORB, step)


def density_kernel(params, field, kept, quarter, across_x, across_band, across_both, plane, near, far):
    dens = jnp.zeros((NZ, COLS), F32)
    for o in range(ORB):
        dens = dens + params[8 + o : 9 + o, 0:1] * field[o] * field[o]
    left, right = dens[:, :LANES], dens[:, LANES:]
    upper = flag(params, 0)
    second = params[5:6, 0:1] == 1.0
    span = CY * NZ // 2
    for value, same, opposite in (
        (jnp.where(upper, right, left), quarter, across_band),
        (jnp.where(upper, left, right), across_x, across_both),
    ):
        for spot, pair in from_columns(value, near, far):
            plane[:, spot : spot + 2 * NZ] = pair
        same[...] = jnp.where(second, plane[:, span:], plane[:, :span])
        opposite[...] = jnp.where(second, plane[:, :span], plane[:, span:])

    def emit(o):
        mine = jnp.where(upper, field[o, :, LANES:], field[o, :, :LANES])
        for spot, pair in from_columns(mine, near, far):
            kept[o, :, spot : spot + 2 * NZ] = pair

    each(ORB, emit)


VM = pl.BlockSpec(memory_space=pltpu.VMEM)
ANY = pl.BlockSpec(memory_space=pl.ANY)
SM = pl.BlockSpec(memory_space=pltpu.SMEM)
HB = pl.BlockSpec(memory_space=pltpu.HBM)


def call(kernel, in_specs, shapes, args, scratch=(), flops=10**8, name=None, passed=0, room=48):
    single = isinstance(shapes, tuple)
    outs = [shapes] if single else list(shapes)
    outs = [shape if isinstance(shape[0], tuple) else (shape, F32) for shape in outs]
    plain = len(outs) - passed
    result = pl.pallas_call(
        kernel,
        out_shape=[jax.ShapeDtypeStruct(*out) for out in outs],
        in_specs=in_specs,
        out_specs=[VM] * plain + [ANY] * passed,
        scratch_shapes=list(scratch),
        input_output_aliases={len(args) - passed + k: plain + k for k in range(passed)},
        compiler_params=pltpu.CompilerParams(vmem_limit_bytes=room * 1024 * 1024),
        cost_estimate=pl.CostEstimate(flops=flops, bytes_accessed=4 * 10**6, transcendentals=0),
        name=name,
    )(*args)
    return result[0] if single else result


def send(value, pairs):
    return lax.ppermute(value, "dom", pairs)


def along_z(step):
    return [(d, (d + 16 * step) % 64) for d in range(64)]


def outward(d):
    y = d % 8
    return d // 8 * 8 + ((y - 1) % 8 if y % 2 == 0 else (y + 1) % 8)


SWAP = [(d, d ^ 8) for d in range(64)]
CORES = [(d, d ^ 1) for d in range(64)]
OUTER = [(d, outward(d)) for d in range(64)]


def body(
    orbitals,
    occupation,
    potential,
    projectors,
    energies,
    piece_column,
    piece_shift,
    piece_owner,
    piece_atom,
    lower_edge,
    upper_edge,
):
    own_m, halo_m, ring_m, edge_m = stencil_matrices()
    own_w = jnp.asarray(np.stack(two_parts(own_m)))
    halo_w = jnp.asarray(np.stack(two_parts(halo_m)))
    ring_w = jnp.asarray(np.stack(two_parts(ring_m)))
    edge_w = jnp.asarray(edge_m.astype(np.float32).astype(jnp.bfloat16))

    here = lax.axis_index("dom")
    side = (here // 8 % 2).astype(jnp.int32)
    core = (here % 2).astype(jnp.int32)
    place = jnp.stack([side, core, lax.axis_index("band").astype(jnp.int32)])
    packed = (ORB, PACKED, LANES)
    grid = (ORB, NZ, COLS)
    stage = [pltpu.VMEM((LANES, LANES), F32)] * 2

    raw = orbitals[:, 0]
    going = jnp.where(side == 0, raw[ORB:], raw[:ORB])
    came = send(jnp.concatenate([going, potential], axis=0), SWAP)
    line = pltpu.VMEM((1, PIECES), jnp.int32)
    keep, params, ints, own_table, note = call(
        begin_kernel,
        [SM] + [HB] * 10,
        [
            (ORB, NZ, LANES),
            (16, LANES),
            ((8, OWN), jnp.int32),
            (TABLE, LANES),
            (NOTE + 24, LANES),
        ],
        (
            place, upper_edge, lower_edge, occupation, piece_column, piece_shift, piece_owner, piece_atom,
            raw, projectors[0], energies[0],
        ),
        [
            line, line, line, line,
            pltpu.VMEM((2 * ORB, CX, CY * NZ), F32),
            pltpu.VMEM((NPJ, PIECES, LANES), F32),
            pltpu.VMEM((NPJ, LANES), F32),
            pltpu.VMEM((2 * ORB, NZ, LANES), F32),
            pltpu.VMEM((2, TABLE, LANES), F32),
            pltpu.VMEM((ORB * NZ, 2 * LANES), BF16),
            pltpu.VMEM((NPJ, NZ, OWN), F32),
            pltpu.VMEM((ROWS, OWN), F32),
            *stage,
            pltpu.SMEM((1,), F32),
            pltpu.SMEM((1,), F32),
            pltpu.SMEM((2 * ORB,), F32),
            pltpu.SemaphoreType.DMA((10,)),
        ],
        name="begin",
        room=ROOM,
    )
    note_came = send(note, SWAP)
    proj = call(gate_kernel, [ANY] * 3, [(NPJ, PIECES, LANES)], (came, note_came, projectors[0]), flops=10**6, name="gate", passed=1)
    proj_came = send(proj[0], SWAP)
    field, pot, xl, xh, inner, outer = call(
        start_kernel,
        [VM] * 5,
        [grid, (NZ, COLS)] + [packed] * 4,
        (params, keep, came, potential, edge_w),
        stage,
        name="start",
    )
    table = call(
        join_table_kernel, [VM] * 2 + [ANY], (TABLE, LANES), (own_table, note_came, field), flops=10**6, name="join_table"
    )
    placed, index = call(
        prepare_kernel,
        [VM] * 4,
        [(NPJ, NZ, ALL), ((4, ALL), jnp.int32)],
        (ints, note_came, projectors[0], proj_came),
        name="prepare",
    )

    sums_room = [pltpu.VMEM((ROWS, ALL), F32)]
    before = field
    for level in range(DEG):
        first, last = level == 0, level == DEG - 1
        if not first:
            table = call(
                table_kernel,
                [VM] * 3,
                (TABLE, LANES),
                (index, field, placed),
                [pltpu.VMEM((ROWS, ALL), F32), pltpu.VMEM((ORB * NZ, 2 * COLS), BF16)],
                name="table",
            )
        inner_came = send(inner, CORES)
        table_came = send(table, CORES)
        if first:
            half = call(
                first_pair_kernel,
                [VM] * 5,
                (HALF + 8, LANES),
                (params, table, table_came, energies[0], note_came),
                flops=10**6,
                name="pair",
            )
        else:
            half = call(pair_kernel, [VM] * 3, (HALF, LANES), (params, table, table_came), flops=10**6, name="pair")
        half_came = send(half, OUTER)
        xl_came = send(xh, along_z(1))
        xh_came = send(xl, along_z(-1))
        outer_came = send(outer, OUTER)
        acc = call(
            functools.partial(local_kernel, first),
            [VM, ANY] + [VM] * 5,
            grid,
            (params, half, field, before, pot, own_w, ring_w),
            name="local",
        )
        size = (THIRD + 8, LANES) if first else (THIRD, LANES)
        low, high, acc = call(
            first_sum_kernel if first else sum_kernel,
            [VM] * (3 if first else 2) + [ANY],
            [size, size, grid],
            ((params,) if first else ()) + (half, half_came, acc),
            flops=10**6,
            name="sums",
            passed=1,
        )
        below = send(high, along_z(1))
        above = send(low, along_z(-1))
        acc = call(
            functools.partial(halo_kernel, first),
            [VM] * 7,
            grid,
            (params, inner_came, outer_came, xl_came, xh_came, acc, halo_w),
            name="halo",
        )
        if first:
            total, energy, acc = call(
                first_total_kernel,
                [VM] * 5 + [ANY],
                [(HALF, LANES), (HALF, LANES), grid],
                (params, low, high, below, above, acc),
                flops=10**6,
                name="totals",
                passed=1,
            )
        else:
            total, acc = call(
                later_total_kernel,
                [VM] * 6 + [ANY],
                [(HALF, LANES), grid],
                (params, low, high, below, above, energy, acc),
                flops=10**6,
                name="totals",
                passed=1,
            )
        total_came = send(total, CORES)
        args = (params, index, acc, total, total_came, placed)
        if not last:
            before, (field, xl, xh, inner, outer) = field, call(
                functools.partial(update_kernel, last),
                [VM] * 7,
                [grid] + [packed] * 4,
                args + (edge_w,),
                sums_room,
                name="update",
            )
        else:
            flat = (ORB, CX, CY * NZ)
            other, result = call(
                functools.partial(update_kernel, last),
                [VM] * 6,
                [flat, grid],
                args,
                sums_room + stage,
                name="finish",
            )
    part = (CX, CY * NZ // 2)
    mine, quarter, across_x, across_band, across_both = call(
        density_kernel,
        [VM] * 2,
        [flat] + [part] * 4,
        (params, result),
        [pltpu.VMEM((CX, CY * NZ), F32)] + stage,
        name="density",
    )
    swapped = send(other, SWAP)
    both = [(d, d ^ 72) for d in range(128)]
    filtered, density = call(
        join_kernel,
        [VM] * 7,
        [(2 * ORB, CX, CY * NZ), part],
        (
            params,
            swapped,
            send(across_x, SWAP),
            lax.ppermute(across_band, "band", [(0, 1), (1, 0)]),
            lax.ppermute(across_both, ("band", "dom"), both),
            mine,
            quarter,
        ),
        name="join",
    )
    return filtered[:, None], density[None]


def solution(mesh):
    in_specs = (
        P("band", "dom", None, None),
        P("band"),
        P("dom", None, None),
        P("dom", None, None, None),
        P("dom", None, None),
        P("dom", None),
        P("dom", None),
        P("dom", None),
        P("dom", None),
        P(),
        P(),
    )
    out_specs = (P("band", "dom", None, None), P("dom", None, "band"))
    return jax.shard_map(body, mesh=mesh, in_specs=in_specs, out_specs=out_specs, check_vma=False)
```

```python
import functools

import jax
import jax.numpy as jnp
import numpy as np
from jax import lax
from jax.experimental import pallas as pl
from jax.experimental.pallas import tpu as pltpu
from jax.sharding import PartitionSpec as P

NZ = 192
HALO = 6
DEG = 4
CX = 8
CY = 16
WX = 2 * CX
COLS = WX * CY
ORB = 4
NPJ = 4
PIECES = 448
ALL = 2 * PIECES
PTS = 128
SLOTS = 128
ROWS = ORB * NPJ
PACKED = 144
TAIL = NZ - PACKED
LANES = 128
EDGE = HALO * 16
OWN = 512
HEAD = 384
ROOM = 58
CODES = 12
TABLE = CODES * ROWS
THIRD = TABLE // 3
HALF = 2 * THIRD
NOTE = TABLE

WEIGHTS = (
    -5369.0 / 1800.0,
    12.0 / 7.0,
    -15.0 / 56.0,
    10.0 / 189.0,
    -1.0 / 112.0,
    2.0 / 1925.0,
    -1.0 / 16632.0,
)
KINETIC = -0.5 / 0.16
F32 = jnp.float32
BF16 = jnp.bfloat16


def coupling(steps):
    reach = np.abs(steps)
    near = (reach >= 1) & (reach <= HALO)
    table = np.array(WEIGHTS) * KINETIC
    return np.where(near, table[np.minimum(reach, HALO)], 0.0)


def stencil_matrices():
    col = np.arange(COLS)
    x, y = col // CY, col % CY
    same_x = x[:, None] == x[None, :]
    same_y = y[:, None] == y[None, :]
    own = np.where(same_y, coupling(x[None, :] - x[:, None]), 0.0)
    own = own + np.where(same_x, coupling(y[None, :] - y[:, None]), 0.0)
    lane = np.arange(LANES)
    used = (lane < EDGE)[:, None]
    parts = []
    for start in (-HALO, WX):
        hx, hy = start + lane // CY, lane % CY
        parts.append(np.where(used & (hy[:, None] == y[None, :]), coupling(x[None, :] - hx[:, None]), 0.0))
    for start in (-HALO, CY):
        hy, hx = start + lane // WX, lane % WX
        parts.append(np.where(used & (hx[:, None] == x[None, :]), coupling(y[None, :] - hy[:, None]), 0.0))
    halo = np.concatenate(parts, axis=0)
    depth = np.arange(NZ)
    apart = (depth[None, :] - depth[:, None] + NZ // 2) % NZ - NZ // 2
    ring = coupling(apart)
    picks = []
    for start in (0, CY - HALO):
        hy, hx = start + lane // WX, lane % WX
        picks.append(np.where(used.T & (col[:, None] == (hx * CY + hy)[None, :]), 1.0, 0.0))
    edge = np.concatenate(picks, axis=1)
    return own, halo, ring, edge


def two_parts(matrix):
    high = np.asarray(matrix, np.float32).astype(jnp.bfloat16)
    low = (np.asarray(matrix, np.float64) - high.astype(np.float64)).astype(np.float32).astype(jnp.bfloat16)
    return high, low


def split(value):
    high = value.astype(BF16)
    low = (value - high.astype(F32)).astype(BF16)
    return high, low


def mul(left, right):
    return jnp.dot(left, right, preferred_element_type=F32)


def mul_t(left, right):
    return lax.dot_general(left, right, (((1,), (1,)), ((), ())), preferred_element_type=F32)


def three(high, low, parts):
    return mul(high, parts[0]) + mul(low, parts[0]) + mul(high, parts[1])


def pack_edge(value):
    main = value[:PACKED]
    lane = lax.broadcasted_iota(jnp.int32, (TAIL, LANES), 1)
    rows = []
    for k in range(3):
        tail = pltpu.roll(value[PACKED:], (EDGE - 32 * k) % LANES, 1)
        rows.append(jnp.where(lane < EDGE, main[k * TAIL : (k + 1) * TAIL], tail))
    return jnp.concatenate(rows, axis=0)


def unpack_edge(value):
    lane = lax.broadcasted_iota(jnp.int32, (TAIL, LANES), 1)
    tail = jnp.zeros((TAIL, LANES), F32)
    for k in range(3):
        moved = pltpu.roll(value[k * TAIL : (k + 1) * TAIL], (32 * k - EDGE) % LANES, 1)
        tail = jnp.where((lane >= 32 * k) & (lane < 32 * k + 32), moved, tail)
    return jnp.concatenate([value, tail], axis=0)


def each(count, step, loop=True):
    if not loop:
        for k in range(count):
            step(k)
        return

    def run(k, carry):
        step(k)
        return carry

    lax.fori_loop(0, count, run, 0)


def emit_edges(field, below_inner, edge_ref, xl_ref, xh_ref, inner_ref, outer_ref):
    def step(o):
        value = field[o]
        high, low = split(value)
        picked = mul(high, edge_ref[...]) + mul(low, edge_ref[...])
        xl_ref[o] = pack_edge(value[:, :LANES])
        xh_ref[o] = pack_edge(pltpu.roll(value[:, LANES:], LANES - 32, 1))
        bottom, top = pack_edge(picked[:, :LANES]), pack_edge(picked[:, LANES:])
        inner_ref[o] = jnp.where(below_inner, bottom, top)
        outer_ref[o] = jnp.where(below_inner, top, bottom)

    each(ORB, step, False)


def to_columns(source, near, far):
    for y in range(CY):
        at = y * NZ
        line = source(at)
        near[pl.ds(y, CX, stride=CY), :] = line[:, :LANES]
        tail = line[:, LANES:]
        far[pl.ds(y, CX, stride=CY), :] = jnp.concatenate([tail, jnp.zeros((CX, 2 * LANES - NZ), F32)], axis=1)
    return jnp.concatenate([jnp.transpose(near[...]), jnp.transpose(far[...])[: NZ - LANES]], axis=0)


def from_columns(value, near, far):
    near[...] = jnp.transpose(value[:LANES])
    far[...] = jnp.transpose(jnp.concatenate([value[LANES:], jnp.zeros((2 * LANES - NZ, LANES), F32)], axis=0))
    for y in range(0, CY, 2):
        lines = []
        for at in (y, y + 1):
            lines.append(near[pl.ds(at, CX, stride=CY), :])
            lines.append(far[pl.ds(at, CX, stride=CY), :][:, : NZ - LANES])
        yield y * NZ, jnp.concatenate(lines, axis=1)


def flag(params, row):
    return params[row : row + 1, :] == 1.0


def pick_kernel(raw, potential, out, sems):
    start = (1 - lax.axis_index("dom") // 8 % 2) * ORB
    first = pltpu.make_async_copy(raw.at[pl.ds(start, ORB)], out.at[pl.ds(0, ORB)], sems.at[0])
    second = pltpu.make_async_copy(potential, out.at[pl.ds(ORB, 1)], sems.at[1])
    first.start()
    second.start()
    first.wait()
    second.wait()


def begin_kernel(
    place, upper_in, lower_in, weights_in, column_in, shift_in, owner_in, atom_in, raw_in, proj_in, energy_in,
    keep, params, ints, table, note,
    column, shift, owner, atom, raw, proj, energy, turned, tables, both, placed, partial, near, far, upper_edge, lower_edge, weights, sems,
):
    pairs = (
        (raw_in, raw), (column_in, column), (shift_in, shift), (owner_in, owner),
        (atom_in, atom), (upper_in, upper_edge), (lower_in, lower_edge), (weights_in, weights),
        (proj_in, proj), (energy_in, energy),
    )
    copies = [pltpu.make_async_copy(source, target, sems.at[k]) for k, (source, target) in enumerate(pairs)]
    for copy in copies:
        copy.start()
    for copy in copies[:8]:
        copy.wait()
    side, core = place[0], place[1]
    upper = jnp.full((1, LANES), side, jnp.int32) == 1
    params[0:1] = jnp.full((1, LANES), side, jnp.int32).astype(F32)
    params[1:2] = jnp.full((1, LANES), core, jnp.int32).astype(F32)
    top = jnp.full((1, LANES), upper_edge[0], F32)
    bottom = jnp.full((1, LANES), lower_edge[0], F32)
    half_width = (top - bottom) / 2.0
    params[2:3] = (top + bottom) / 2.0
    params[3:4] = 1.0 / half_width
    params[4:5] = 2.0 / half_width
    params[5:6] = jnp.full((1, LANES), place[2], jnp.int32).astype(F32)
    params[6:8] = jnp.zeros((2, LANES), F32)
    for o in range(ORB):
        params[8 + o : 9 + o] = jnp.full((1, LANES), weights[side * ORB + o], F32)
    params[8 + ORB :] = jnp.zeros((8 - ORB, LANES), F32)
    sub = jnp.full((1, PIECES), side, jnp.int32)
    step_x = (owner[...] >= 3).astype(jnp.int32) + (owner[...] >= 6).astype(jnp.int32)
    row = owner[...] - 3 * step_x
    lines = [
        sub * LANES + column[...],
        shift[...],
        row * 4 + sub + step_x,
        atom[...],
        column[...],
    ]
    gap = jnp.full((1, OWN - PIECES), -1, jnp.int32)
    for k, line in enumerate(lines):
        ints[k : k + 1] = jnp.concatenate([line, gap], axis=1)
    ints[len(lines) :] = jnp.zeros((8 - len(lines), OWN), jnp.int32)
    def turn(o):
        def kept(at):
            return jnp.where(upper[:, :1], raw[ORB + o, :, at : at + NZ], raw[o, :, at : at + NZ])

        def sent(at):
            return jnp.where(upper[:, :1], raw[o, :, at : at + NZ], raw[ORB + o, :, at : at + NZ])

        turned[o] = to_columns(kept, near, far)
        turned[ORB + o] = to_columns(sent, near, far)
        keep[o] = turned[o]

    each(ORB, turn)
    for copy in copies[8:]:
        copy.wait()
    first_tables(ints, turned, tables, both, proj, placed, partial)
    table[...] = tables[0]
    note[:TABLE] = tables[1]
    note[NOTE : NOTE + NPJ] = energy[...]
    note[NOTE + NPJ : NOTE + 8] = jnp.zeros((4, LANES), F32)
    numbers = ints[:4].astype(F32)
    for k in range(OWN // LANES):
        note[NOTE + 8 + 4 * k : NOTE + 12 + 4 * k] = numbers[:, k * LANES : (k + 1) * LANES]


def start_kernel(params, keep, came, potential, edge, field, pot, xl, xh, inner, outer, near, far):
    upper = flag(params, 0)
    here = to_columns(lambda at: potential[0, :, at : at + NZ], near, far)
    there = to_columns(lambda at: came[ORB, :, at : at + NZ], near, far)
    pot[:, :LANES] = jnp.where(upper, there, here)
    pot[:, LANES:] = jnp.where(upper, here, there)

    def step(o):
        turned = to_columns(lambda at: came[o, :, at : at + NZ], near, far)
        kept = keep[o]
        field[o, :, :LANES] = jnp.where(upper, turned, kept)
        field[o, :, LANES:] = jnp.where(upper, kept, turned)

    each(ORB, step, False)
    emit_edges(field, flag(params, 1), edge, xl, xh, inner, outer)


def gate_kernel(came, note_came, proj, out):
    pass


def own_kernel(ints, own, note, placed):
    for j in range(NPJ):
        for k in range(HEAD // LANES):
            at = slice(k * LANES, (k + 1) * LANES)
            placed[j, :, at] = shifted(own[j, at], ints[1:2, at])


def prepare_kernel(ints, note_came, own, came, placed, index):
    lines = [note_came[NOTE + 8 + 4 * k : NOTE + 12 + 4 * k] for k in range(OWN // LANES)]
    other = jnp.concatenate(lines, axis=1)[:, :PIECES].astype(jnp.int32)
    index[...] = jnp.concatenate([ints[:4, :PIECES], other], axis=1)
    for j in range(NPJ):
        both = jnp.concatenate([own[j, HEAD:], came[j]], axis=0)
        for k in range((ALL - HEAD) // LANES):
            at = slice(k * LANES, (k + 1) * LANES)
            spot = slice(HEAD + k * LANES, HEAD + (k + 1) * LANES)
            placed[j, :, at] = shifted(both[at], index[1:2, spot])


def column_hot(index, at, wide):
    where = lax.broadcasted_iota(jnp.int32, (COLS, wide), 0) == index[0:1, pl.ds(at, wide)]
    return where.astype(F32).astype(BF16)


def chunks(head, tail, step):
    for source, at, base, wide in ((head, 0, 0, 256), (head, 256, 0, 128), (tail, 0, HEAD, 256), (tail, 256, HEAD, 256)):
        step(source, at, base + at, wide)


def atom_hot(index):
    codes = index[3:4, :]
    return (lax.broadcasted_iota(jnp.int32, (SLOTS, codes.shape[1]), 0) == codes).astype(F32).astype(BF16)


def shifted(block, shift):
    block = jnp.concatenate([jnp.transpose(block), jnp.zeros((NZ - PTS, LANES), F32)], axis=0)
    for bit in (64, 32, 16, 8, 4, 2, 1):
        block = jnp.where((shift & bit) != 0, pltpu.roll(block, bit, 0), block)
    return block


def gather_table(index, spread):
    codes = index[2:3, :]
    rows = jnp.concatenate([jnp.where(codes == code, spread, 0.0) for code in range(CODES)], axis=0)
    high, low = split(rows)
    atoms = atom_hot(index)
    return mul_t(high, atoms) + mul_t(low, atoms)


def project(both, hot, placed, partial, spot, at, wide):
    picked = mul(both, jnp.concatenate([hot, hot], axis=0))
    sums = [None] * ROWS
    for z in range(0, NZ, 8):
        lines = [picked[o * NZ + z : o * NZ + z + 8] for o in range(ORB)]
        for j in range(NPJ):
            values = placed[j, z : z + 8, pl.ds(spot, wide)]
            for o in range(ORB):
                term = lines[o] * values
                row = o * NPJ + j
                sums[row] = term if z == 0 else sums[row] + term
    for row in range(ROWS):
        partial[row : row + 1, pl.ds(at, wide)] = jnp.sum(sums[row], axis=0, keepdims=True)


def first_tables(index, turned, tables, both, proj, placed, partial):
    blocks = OWN // LANES

    def place(j):
        for k in range(blocks):
            block = proj[j, k * LANES : min((k + 1) * LANES, PIECES)]
            if k == blocks - 1:
                block = jnp.concatenate([block, jnp.zeros((OWN - PIECES, LANES), F32)], axis=0)
            placed[j, :, k * LANES : (k + 1) * LANES] = shifted(block, index[1:2, k * LANES : (k + 1) * LANES])

    each(NPJ, place)

    def table(s):
        for o in range(ORB):
            both[o * NZ : (o + 1) * NZ, :] = jnp.concatenate(split(turned[s * ORB + o]), axis=1)

        def chunk(k):
            at = k * 256
            where = lax.broadcasted_iota(jnp.int32, (LANES, 256), 0) == index[4:5, pl.ds(at, 256)]
            project(both[...], where.astype(F32).astype(BF16), placed, partial, at, at, 256)

        each(OWN // 256, chunk, False)
        tables[s] = gather_table(index, partial[...])

    each(2, table)


def table_kernel(index, field, head, tail, table, partial, both):
    def gather(o):
        rows = pl.ds(o * NZ, NZ)
        both[rows, :] = jnp.concatenate(split(field[o]), axis=1)

    each(ORB, gather, False)
    def chunk(placed, spot, at, wide):
        project(both[...], column_hot(index, at, wide), placed, partial, spot, at, wide)

    chunks(head, tail, chunk)
    table[...] = gather_table(index, partial[...])


def pair_sum(second, table, came):
    gap = jnp.zeros((THIRD, LANES), F32)
    up = table[THIRD:] + jnp.concatenate([came[HALF:], gap], axis=0)
    down = table[:HALF] + jnp.concatenate([gap, came[:THIRD]], axis=0)
    return jnp.where(second, up, down)


def join_table_kernel(table, note_came, field, out):
    out[...] = table[...] + note_came[:TABLE]


def first_pair_kernel(params, table, came, energy, note_came, half):
    half[:HALF] = pair_sum(flag(params, 1), table[...], came[...])
    upper = flag(params, 0)
    there = note_came[NOTE : NOTE + NPJ]
    half[HALF : HALF + NPJ] = jnp.where(upper, there, energy[...])
    half[HALF + NPJ :] = jnp.where(upper, energy[...], there)


def pair_kernel(params, table, came, half):
    half[...] = pair_sum(flag(params, 1), table[...], came[...])


def sum_kernel(mine, came, acc, low, high, acc_out):
    total = mine[:HALF] + came[:HALF]
    step = 2 * ROWS
    for q in range(2):
        low[q * step : (q + 1) * step] = total[2 * q * step : (2 * q + 1) * step]
        high[q * step : (q + 1) * step] = total[(2 * q + 1) * step : (2 * q + 2) * step]


def first_sum_kernel(params, mine, came, acc, low, high, acc_out):
    sum_kernel(mine, came, acc, low, high, acc_out)
    second = flag(params, 1)
    for sub, out in ((0, low), (1, high)):
        at = HALF + sub * NPJ
        here, there = mine[at : at + NPJ], came[at : at + NPJ]
        out[THIRD : THIRD + NPJ] = jnp.where(second, here, there)
        out[THIRD + NPJ :] = jnp.where(second, there, here)


def spread_energy(low, high, below, above, energy):
    for q in range(2):
        at = slice(THIRD + q * NPJ, THIRD + (q + 1) * NPJ)
        for r, source in enumerate((below, low, high, above)):
            row = (q * 4 + r) * ROWS
            energy[row : row + ROWS] = jnp.concatenate([source[at]] * ORB, axis=0)


def scale_of(first, params):
    row = 3 if first else 4
    return params[row : row + 1, 0:1]


def total_kernel(first, params, low, high, below, above, acc, energy, out, acc_out, energy_out=None):
    if first:
        spread_energy(low, high, below, above, energy_out)
        energy = energy_out
    step = 2 * ROWS
    scale = params[3 if first else 4 : 4 if first else 5, :]
    for q in range(2):
        at = slice(q * step, (q + 1) * step)
        row = 2 * q * step
        out[row : row + step] = (low[at] + below[at]) * energy[row : row + step] * scale
        row = row + step
        out[row : row + step] = (high[at] + above[at]) * energy[row : row + step] * scale


def first_total_kernel(params, low, high, below, above, acc, out, energy, acc_out):
    total_kernel(True, params, low, high, below, above, acc, None, out, acc_out, energy)


def later_total_kernel(params, low, high, below, above, energy, acc, out, acc_out):
    total_kernel(False, params, low, high, below, above, acc, energy, out, acc_out)


def local_kernel(first, params, half, field, before, pot, own_w, ring_w, out):
    center = params[2:3, 0:1]
    scale = scale_of(first, params)
    diagonal = pot[...] + (3.0 * WEIGHTS[0] * KINETIC - center)

    def step(o):
        value = field[o]
        high, low = split(value)
        across = three(high, low, own_w)
        along = mul(ring_w[0], high) + mul(ring_w[0], low) + mul(ring_w[1], high)
        total = scale * (across + along + diagonal * value)
        out[o] = total if first else total - before[o]

    each(ORB, step)


def halo_kernel(first, params, inner, outer, xl, xh, acc, halo_w, out):
    scale = scale_of(first, params)
    below_inner = flag(params, 1)

    def step(o):
        inside, outside = unpack_edge(inner[o]), unpack_edge(outer[o])
        bottom = jnp.where(below_inner, inside, outside)
        top = jnp.where(below_inner, outside, inside)
        line = jnp.concatenate([unpack_edge(xl[o]), unpack_edge(xh[o]), bottom, top], axis=1)
        high, low = split(line)
        out[o] = acc[o] + scale * three(high, low, halo_w)

    each(ORB, step)


def update_kernel(last, params, index, acc, mine, came, head, tail, *rest):
    if last:
        sent, field, coef_rows, near, far = rest
    else:
        edge, field, xl, xh, inner, outer, coef_rows = rest
    second = flag(params, 1)
    total = jnp.concatenate(
        [jnp.where(second, came[THIRD:], mine[...][:THIRD]), jnp.where(second, mine[...][:THIRD], mine[...][THIRD:]),
         jnp.where(second, mine[...][THIRD:], came[:THIRD])], axis=0
    )
    atoms = atom_hot(index)
    spread = mul(jnp.concatenate(split(total), axis=1), jnp.concatenate([atoms, atoms], axis=0))
    codes = index[2:3, :]
    coefs = jnp.zeros((ROWS, ALL), F32)
    for code in range(CODES):
        coefs = jnp.where(codes == code, spread[code * ROWS : (code + 1) * ROWS], coefs)
    coef_rows[...] = coefs
    sums = []

    def chunk(placed, spot, at, wide):
        hot = column_hot(index, at, wide)
        lines = []
        for o in range(ORB):
            rows = coef_rows[o * NPJ : (o + 1) * NPJ, pl.ds(at, wide)]
            line = rows[0:1] * placed[0, :, pl.ds(spot, wide)]
            for j in range(1, NPJ):
                line = line + rows[j : j + 1] * placed[j, :, pl.ds(spot, wide)]
            lines.append(jnp.concatenate(split(line), axis=1))
        term = mul_t(jnp.concatenate(lines, axis=0), jnp.concatenate([hot, hot], axis=1))
        sums[:] = [sums[0] + term if sums else term]

    chunks(head, tail, chunk)

    def finish(o):
        field[o] = acc[o] + sums[0][o * NZ : (o + 1) * NZ]

    each(ORB, finish, False)
    if not last:
        emit_edges(field, second, edge, xl, xh, inner, outer)
        return
    upper = flag(params, 0)

    def emit(o):
        left, right = field[o, :, :LANES], field[o, :, LANES:]
        for spot, pair in from_columns(jnp.where(upper, left, right), near, far):
            sent[o, :, spot : spot + 2 * NZ] = pair

    each(ORB, emit)


def join_kernel(params, came, b, mine, a, out, density):
    upper = params[0:1, 0:1] == 1.0
    density[...] = a[...] + b[...]

    def step(o):
        out[o] = jnp.where(upper, came[o], mine[o])
        out[ORB + o] = jnp.where(upper, mine[o], came[o])

    each(ORB, step)


def density_kernel(params, field, mine, across, plane, near, far):
    dens = jnp.zeros((NZ, COLS), F32)
    for o in range(ORB):
        dens = dens + params[8 + o : 9 + o, 0:1] * field[o] * field[o]
    left, right = dens[:, :LANES], dens[:, LANES:]
    upper = flag(params, 0)
    second = params[5:6, 0:1] == 1.0
    span = CY * NZ // 2
    for k, value in enumerate((jnp.where(upper, right, left), jnp.where(upper, left, right))):
        for spot, pair in from_columns(value, near, far):
            plane[:, spot : spot + 2 * NZ] = pair
        mine[k] = jnp.where(second, plane[:, span:], plane[:, :span])
        across[k] = jnp.where(second, plane[:, :span], plane[:, span:])


def keep_kernel(params, field, here, kept, near, far):
    upper = flag(params, 0)

    def emit(o):
        mine = jnp.where(upper, field[o, :, LANES:], field[o, :, :LANES])
        for spot, pair in from_columns(mine, near, far):
            kept[o, :, spot : spot + 2 * NZ] = pair

    each(ORB, emit)


def band_kernel(here, came, quarter, going):
    quarter[...] = here[0] + came[0]
    going[...] = here[1] + came[1]


VM = pl.BlockSpec(memory_space=pltpu.VMEM)
ANY = pl.BlockSpec(memory_space=pl.ANY)
SM = pl.BlockSpec(memory_space=pltpu.SMEM)
HB = pl.BlockSpec(memory_space=pltpu.HBM)


def call(kernel, in_specs, shapes, args, scratch=(), flops=10**8, name=None, passed=0, room=48):
    single = isinstance(shapes, tuple)
    outs = [shapes] if single else list(shapes)
    outs = [shape if isinstance(shape[0], tuple) else (shape, F32) for shape in outs]
    plain = len(outs) - passed
    result = pl.pallas_call(
        kernel,
        out_shape=[jax.ShapeDtypeStruct(*out) for out in outs],
        in_specs=in_specs,
        out_specs=[VM] * plain + [ANY] * passed,
        scratch_shapes=list(scratch),
        input_output_aliases={len(args) - passed + k: plain + k for k in range(passed)},
        compiler_params=pltpu.CompilerParams(vmem_limit_bytes=room * 1024 * 1024),
        cost_estimate=pl.CostEstimate(flops=flops, bytes_accessed=4 * 10**6, transcendentals=0),
        name=name,
    )(*args)
    return result[0] if single else result


def send(value, pairs):
    return lax.ppermute(value, "dom", pairs)


def along_z(step):
    return [(d, (d + 16 * step) % 64) for d in range(64)]


def outward(d):
    y = d % 8
    return d // 8 * 8 + ((y - 1) % 8 if y % 2 == 0 else (y + 1) % 8)


SWAP = [(d, d ^ 8) for d in range(64)]
CORES = [(d, d ^ 1) for d in range(64)]
OUTER = [(d, outward(d)) for d in range(64)]


def body(
    orbitals,
    occupation,
    potential,
    projectors,
    energies,
    piece_column,
    piece_shift,
    piece_owner,
    piece_atom,
    lower_edge,
    upper_edge,
):
    own_m, halo_m, ring_m, edge_m = stencil_matrices()
    own_w = jnp.asarray(np.stack(two_parts(own_m)))
    halo_w = jnp.asarray(np.stack(two_parts(halo_m)))
    ring_w = jnp.asarray(np.stack(two_parts(ring_m)))
    edge_w = jnp.asarray(edge_m.astype(np.float32).astype(jnp.bfloat16))

    here = lax.axis_index("dom")
    side = (here // 8 % 2).astype(jnp.int32)
    core = (here % 2).astype(jnp.int32)
    place = jnp.stack([side, core, lax.axis_index("band").astype(jnp.int32)])
    packed = (ORB, PACKED, LANES)
    grid = (ORB, NZ, COLS)
    stage = [pltpu.VMEM((LANES, LANES), F32)] * 2

    raw = orbitals[:, 0]
    message = call(
        pick_kernel,
        [HB] * 2,
        (ORB + 1, CX, CY * NZ),
        (raw, potential),
        [pltpu.SemaphoreType.DMA((2,))],
        flops=10**6,
        name="pick",
    )
    came = send(message, SWAP)
    line = pltpu.VMEM((1, PIECES), jnp.int32)
    keep, params, ints, own_table, note = call(
        begin_kernel,
        [SM] + [HB] * 10,
        [
            (ORB, NZ, LANES),
            (16, LANES),
            ((8, OWN), jnp.int32),
            (TABLE, LANES),
            (NOTE + 24, LANES),
        ],
        (
            place, upper_edge, lower_edge, occupation, piece_column, piece_shift, piece_owner, piece_atom,
            raw, projectors[0], energies[0],
        ),
        [
            line, line, line, line,
            pltpu.VMEM((2 * ORB, CX, CY * NZ), F32),
            pltpu.VMEM((NPJ, PIECES, LANES), F32),
            pltpu.VMEM((NPJ, LANES), F32),
            pltpu.VMEM((2 * ORB, NZ, LANES), F32),
            pltpu.VMEM((2, TABLE, LANES), F32),
            pltpu.VMEM((ORB * NZ, 2 * LANES), BF16),
            pltpu.VMEM((NPJ, NZ, OWN), F32),
            pltpu.VMEM((ROWS, OWN), F32),
            *stage,
            pltpu.SMEM((1,), F32),
            pltpu.SMEM((1,), F32),
            pltpu.SMEM((2 * ORB,), F32),
            pltpu.SemaphoreType.DMA((10,)),
        ],
        name="begin",
        room=ROOM,
    )
    note_came = send(note, SWAP)
    proj = call(gate_kernel, [ANY] * 3, [(NPJ, PIECES, LANES)], (came, note_came, projectors[0]), flops=10**6, name="gate", passed=1)
    proj_came = send(proj[0], SWAP)
    field, pot, xl, xh, inner, outer = call(
        start_kernel,
        [VM] * 5,
        [grid, (NZ, COLS)] + [packed] * 4,
        (params, keep, came, potential, edge_w),
        stage,
        name="start",
    )
    table = call(
        join_table_kernel, [VM] * 2 + [ANY], (TABLE, LANES), (own_table, note_came, field), flops=10**6, name="join_table"
    )
    head = call(own_kernel, [VM] * 2 + [ANY], (NPJ, NZ, HEAD), (ints, projectors[0], table), name="own")
    tail, index = call(
        prepare_kernel,
        [VM] * 4,
        [(NPJ, NZ, ALL - HEAD), ((4, ALL), jnp.int32)],
        (ints, note_came, projectors[0], proj_came),
        name="prepare",
    )

    sums_room = [pltpu.VMEM((ROWS, ALL), F32)]
    before = field
    for level in range(DEG):
        first, last = level == 0, level == DEG - 1
        if not first:
            table = call(
                table_kernel,
                [VM] * 4,
                (TABLE, LANES),
                (index, field, head, tail),
                [pltpu.VMEM((ROWS, ALL), F32), pltpu.VMEM((ORB * NZ, 2 * COLS), BF16)],
                name="table",
            )
        inner_came = send(inner, CORES)
        table_came = send(table, CORES)
        if first:
            half = call(
                first_pair_kernel,
                [VM] * 5,
                (HALF + 8, LANES),
                (params, table, table_came, energies[0], note_came),
                flops=10**6,
                name="pair",
            )
        else:
            half = call(pair_kernel, [VM] * 3, (HALF, LANES), (params, table, table_came), flops=10**6, name="pair")
        half_came = send(half, OUTER)
        xl_came = send(xh, along_z(1))
        xh_came = send(xl, along_z(-1))
        outer_came = send(outer, OUTER)
        acc = call(
            functools.partial(local_kernel, first),
            [VM, ANY] + [VM] * 5,
            grid,
            (params, half, field, before, pot, own_w, ring_w),
            name="local",
        )
        size = (THIRD + 8, LANES) if first else (THIRD, LANES)
        low, high, acc = call(
            first_sum_kernel if first else sum_kernel,
            [VM] * (3 if first else 2) + [ANY],
            [size, size, grid],
            ((params,) if first else ()) + (half, half_came, acc),
            flops=10**6,
            name="sums",
            passed=1,
        )
        below = send(high, along_z(1))
        above = send(low, along_z(-1))
        acc = call(
            functools.partial(halo_kernel, first),
            [VM] * 7,
            grid,
            (params, inner_came, outer_came, xl_came, xh_came, acc, halo_w),
            name="halo",
        )
        if first:
            total, energy, acc = call(
                first_total_kernel,
                [VM] * 5 + [ANY],
                [(HALF, LANES), (HALF, LANES), grid],
                (params, low, high, below, above, acc),
                flops=10**6,
                name="totals",
                passed=1,
            )
        else:
            total, acc = call(
                later_total_kernel,
                [VM] * 6 + [ANY],
                [(HALF, LANES), grid],
                (params, low, high, below, above, energy, acc),
                flops=10**6,
                name="totals",
                passed=1,
            )
        total_came = send(total, CORES)
        args = (params, index, acc, total, total_came, head, tail)
        if not last:
            before, (field, xl, xh, inner, outer) = field, call(
                functools.partial(update_kernel, last),
                [VM] * 8,
                [grid] + [packed] * 4,
                args + (edge_w,),
                sums_room,
                name="update",
            )
        else:
            flat = (ORB, CX, CY * NZ)
            other, result = call(
                functools.partial(update_kernel, last),
                [VM] * 7,
                [flat, grid],
                args,
                sums_room + stage,
                name="finish",
            )
    part = (CX, CY * NZ // 2)
    here_parts, across = call(
        density_kernel,
        [VM] * 2,
        [(2,) + part] * 2,
        (params, result),
        [pltpu.VMEM((CX, CY * NZ), F32)] + stage,
        name="density",
    )
    swapped = send(other, SWAP)
    across_came = lax.ppermute(across, "band", [(0, 1), (1, 0)])
    mine = call(keep_kernel, [VM, VM, ANY], flat, (params, result, across), stage, name="keep")
    quarter, going = call(band_kernel, [VM] * 2, [part] * 2, (here_parts, across_came), flops=10**6, name="band")
    filtered, density = call(
        join_kernel,
        [VM] * 5,
        [(2 * ORB, CX, CY * NZ), part],
        (params, swapped, send(going, SWAP), mine, quarter),
        name="join",
    )
    return filtered[:, None], density[None]


def solution(mesh):
    in_specs = (
        P("band", "dom", None, None),
        P("band"),
        P("dom", None, None),
        P("dom", None, None, None),
        P("dom", None, None),
        P("dom", None),
        P("dom", None),
        P("dom", None),
        P("dom", None),
        P(),
        P(),
    )
    out_specs = (P("band", "dom", None, None), P("dom", None, "band"))
    return jax.shard_map(body, mesh=mesh, in_specs=in_specs, out_specs=out_specs, check_vma=False)
```

```python
import functools

import jax
import jax.numpy as jnp
import numpy as np
from jax import lax
from jax.experimental import pallas as pl
from jax.experimental.pallas import tpu as pltpu
from jax.sharding import PartitionSpec as P

NZ = 192
HALO = 6
DEG = 4
CX = 8
CY = 16
WX = 2 * CX
COLS = WX * CY
ORB = 4
NPJ = 4
PIECES = 448
ALL = 2 * PIECES
PTS = 128
SLOTS = 128
ROWS = ORB * NPJ
PACKED = 144
TAIL = NZ - PACKED
LANES = 128
EDGE = HALO * 16
OWN = 512
HEAD = 384
ROOM = 58
CODES = 12
TABLE = CODES * ROWS
THIRD = TABLE // 3
HALF = 2 * THIRD
NOTE = TABLE

WEIGHTS = (
    -5369.0 / 1800.0,
    12.0 / 7.0,
    -15.0 / 56.0,
    10.0 / 189.0,
    -1.0 / 112.0,
    2.0 / 1925.0,
    -1.0 / 16632.0,
)
KINETIC = -0.5 / 0.16
F32 = jnp.float32
BF16 = jnp.bfloat16


def coupling(steps):
    reach = np.abs(steps)
    near = (reach >= 1) & (reach <= HALO)
    table = np.array(WEIGHTS) * KINETIC
    return np.where(near, table[np.minimum(reach, HALO)], 0.0)


def stencil_matrices():
    col = np.arange(COLS)
    x, y = col // CY, col % CY
    same_x = x[:, None] == x[None, :]
    same_y = y[:, None] == y[None, :]
    own = np.where(same_y, coupling(x[None, :] - x[:, None]), 0.0)
    own = own + np.where(same_x, coupling(y[None, :] - y[:, None]), 0.0)
    lane = np.arange(LANES)
    used = (lane < EDGE)[:, None]
    parts = []
    for start in (-HALO, WX):
        hx, hy = start + lane // CY, lane % CY
        parts.append(np.where(used & (hy[:, None] == y[None, :]), coupling(x[None, :] - hx[:, None]), 0.0))
    for start in (-HALO, CY):
        hy, hx = start + lane // WX, lane % WX
        parts.append(np.where(used & (hx[:, None] == x[None, :]), coupling(y[None, :] - hy[:, None]), 0.0))
    halo = np.concatenate(parts, axis=0)
    depth = np.arange(NZ)
    apart = (depth[None, :] - depth[:, None] + NZ // 2) % NZ - NZ // 2
    ring = coupling(apart)
    picks = []
    for start in (0, CY - HALO):
        hy, hx = start + lane // WX, lane % WX
        picks.append(np.where(used.T & (col[:, None] == (hx * CY + hy)[None, :]), 1.0, 0.0))
    edge = np.concatenate(picks, axis=1)
    return own, halo, ring, edge


def two_parts(matrix):
    high = np.asarray(matrix, np.float32).astype(jnp.bfloat16)
    low = (np.asarray(matrix, np.float64) - high.astype(np.float64)).astype(np.float32).astype(jnp.bfloat16)
    return high, low


def split(value):
    high = value.astype(BF16)
    low = (value - high.astype(F32)).astype(BF16)
    return high, low


def mul(left, right):
    return jnp.dot(left, right, preferred_element_type=F32)


def mul_t(left, right):
    return lax.dot_general(left, right, (((1,), (1,)), ((), ())), preferred_element_type=F32)


def three(high, low, parts):
    return mul(high, parts[0]) + mul(low, parts[0]) + mul(high, parts[1])


def pack_edge(value):
    main = value[:PACKED]
    lane = lax.broadcasted_iota(jnp.int32, (TAIL, LANES), 1)
    rows = []
    for k in range(3):
        tail = pltpu.roll(value[PACKED:], (EDGE - 32 * k) % LANES, 1)
        rows.append(jnp.where(lane < EDGE, main[k * TAIL : (k + 1) * TAIL], tail))
    return jnp.concatenate(rows, axis=0)


def unpack_edge(value):
    lane = lax.broadcasted_iota(jnp.int32, (TAIL, LANES), 1)
    tail = jnp.zeros((TAIL, LANES), F32)
    for k in range(3):
        moved = pltpu.roll(value[k * TAIL : (k + 1) * TAIL], (32 * k - EDGE) % LANES, 1)
        tail = jnp.where((lane >= 32 * k) & (lane < 32 * k + 32), moved, tail)
    return jnp.concatenate([value, tail], axis=0)


def each(count, step, loop=True):
    if not loop:
        for k in range(count):
            step(k)
        return

    def run(k, carry):
        step(k)
        return carry

    lax.fori_loop(0, count, run, 0)


def emit_edges(field, below_inner, edge_ref, xl_ref, xh_ref, inner_ref, outer_ref):
    def step(o):
        value = field[o]
        high, low = split(value)
        picked = mul(high, edge_ref[...]) + mul(low, edge_ref[...])
        xl_ref[o] = pack_edge(value[:, :LANES])
        xh_ref[o] = pack_edge(pltpu.roll(value[:, LANES:], LANES - 32, 1))
        bottom, top = pack_edge(picked[:, :LANES]), pack_edge(picked[:, LANES:])
        inner_ref[o] = jnp.where(below_inner, bottom, top)
        outer_ref[o] = jnp.where(below_inner, top, bottom)

    each(ORB, step, False)


def to_columns(source, near, far):
    for y in range(CY):
        at = y * NZ
        line = source(at)
        near[pl.ds(y, CX, stride=CY), :] = line[:, :LANES]
        tail = line[:, LANES:]
        far[pl.ds(y, CX, stride=CY), :] = jnp.concatenate([tail, jnp.zeros((CX, 2 * LANES - NZ), F32)], axis=1)
    return jnp.concatenate([jnp.transpose(near[...]), jnp.transpose(far[...])[: NZ - LANES]], axis=0)


def from_columns(value, near, far):
    near[...] = jnp.transpose(value[:LANES])
    far[...] = jnp.transpose(jnp.concatenate([value[LANES:], jnp.zeros((2 * LANES - NZ, LANES), F32)], axis=0))
    for y in range(0, CY, 2):
        lines = []
        for at in (y, y + 1):
            lines.append(near[pl.ds(at, CX, stride=CY), :])
            lines.append(far[pl.ds(at, CX, stride=CY), :][:, : NZ - LANES])
        yield y * NZ, jnp.concatenate(lines, axis=1)


def flag(params, row):
    return params[row : row + 1, :] == 1.0


def pick_kernel(raw, potential, out, sems):
    start = (1 - lax.axis_index("dom") // 8 % 2) * ORB
    first = pltpu.make_async_copy(raw.at[pl.ds(start, ORB)], out.at[pl.ds(0, ORB)], sems.at[0])
    second = pltpu.make_async_copy(potential, out.at[pl.ds(ORB, 1)], sems.at[1])
    first.start()
    second.start()
    first.wait()
    second.wait()


def begin_kernel(
    weights_in, column_in, shift_in, owner_in, atom_in, raw_in, proj_in, energy_in,
    keep, params, ints, table, note,
    column, shift, owner, atom, raw, proj, energy, turned, tables, both, placed, partial, near, far, weights, sems,
):
    pairs = (
        (raw_in, raw), (column_in, column), (shift_in, shift), (owner_in, owner),
        (atom_in, atom), (weights_in, weights),
        (proj_in, proj), (energy_in, energy),
    )
    copies = [pltpu.make_async_copy(source, target, sems.at[k]) for k, (source, target) in enumerate(pairs)]
    for copy in copies:
        copy.start()
    for copy in copies[:6]:
        copy.wait()
    here = lax.axis_index("dom")
    side, core = here // 8 % 2, here % 2
    upper = jnp.full((1, LANES), side, jnp.int32) == 1
    params[0:1] = jnp.full((1, LANES), side, jnp.int32).astype(F32)
    params[1:2] = jnp.full((1, LANES), core, jnp.int32).astype(F32)
    params[2:5] = jnp.zeros((3, LANES), F32)
    params[5:6] = jnp.full((1, LANES), lax.axis_index("band"), jnp.int32).astype(F32)
    params[6:8] = jnp.zeros((2, LANES), F32)
    for o in range(ORB):
        params[8 + o : 9 + o] = jnp.full((1, LANES), weights[side * ORB + o], F32)
    params[8 + ORB :] = jnp.zeros((8 - ORB, LANES), F32)
    sub = jnp.full((1, PIECES), side, jnp.int32)
    step_x = (owner[...] >= 3).astype(jnp.int32) + (owner[...] >= 6).astype(jnp.int32)
    row = owner[...] - 3 * step_x
    lines = [
        sub * LANES + column[...],
        shift[...],
        row * 4 + sub + step_x,
        atom[...],
        column[...],
    ]
    gap = jnp.full((1, OWN - PIECES), -1, jnp.int32)
    for k, line in enumerate(lines):
        ints[k : k + 1] = jnp.concatenate([line, gap], axis=1)
    ints[len(lines) :] = jnp.zeros((8 - len(lines), OWN), jnp.int32)
    def turn(o):
        def kept(at):
            return jnp.where(upper[:, :1], raw[ORB + o, :, at : at + NZ], raw[o, :, at : at + NZ])

        def sent(at):
            return jnp.where(upper[:, :1], raw[o, :, at : at + NZ], raw[ORB + o, :, at : at + NZ])

        turned[o] = to_columns(kept, near, far)
        turned[ORB + o] = to_columns(sent, near, far)
        keep[o] = turned[o]

    each(ORB, turn)
    for copy in copies[6:]:
        copy.wait()
    first_tables(ints, turned, tables, both, proj, placed, partial)
    table[...] = tables[0]
    note[:TABLE] = tables[1]
    note[NOTE : NOTE + NPJ] = energy[...]
    note[NOTE + NPJ : NOTE + 8] = jnp.zeros((4, LANES), F32)
    numbers = ints[:4].astype(F32)
    for k in range(OWN // LANES):
        note[NOTE + 8 + 4 * k : NOTE + 12 + 4 * k] = numbers[:, k * LANES : (k + 1) * LANES]


def start_kernel(flags, ends, keep, came, potential, edge, params, field, pot, xl, xh, inner, outer, near, far):
    params[...] = flags[...]
    top, bottom = ends[0:1], ends[1:2]
    half_width = (top - bottom) / 2.0
    params[2:3] = (top + bottom) / 2.0
    params[3:4] = 1.0 / half_width
    params[4:5] = 2.0 / half_width
    upper = flag(params, 0)
    here = to_columns(lambda at: potential[0, :, at : at + NZ], near, far)
    there = to_columns(lambda at: came[ORB, :, at : at + NZ], near, far)
    pot[:, :LANES] = jnp.where(upper, there, here)
    pot[:, LANES:] = jnp.where(upper, here, there)

    def step(o):
        turned = to_columns(lambda at: came[o, :, at : at + NZ], near, far)
        kept = keep[o]
        field[o, :, :LANES] = jnp.where(upper, turned, kept)
        field[o, :, LANES:] = jnp.where(upper, kept, turned)

    each(ORB, step, False)
    emit_edges(field, flag(params, 1), edge, xl, xh, inner, outer)


def gate_kernel(came, note_came, proj, out):
    pass


def own_kernel(ints, own, note, placed):
    for j in range(NPJ):
        for k in range(HEAD // LANES):
            at = slice(k * LANES, (k + 1) * LANES)
            placed[j, :, at] = shifted(own[j, at], ints[1:2, at])


def prepare_kernel(ints, note_came, own, came, placed, index):
    lines = [note_came[NOTE + 8 + 4 * k : NOTE + 12 + 4 * k] for k in range(OWN // LANES)]
    other = jnp.concatenate(lines, axis=1)[:, :PIECES].astype(jnp.int32)
    index[...] = jnp.concatenate([ints[:4, :PIECES], other], axis=1)
    for j in range(NPJ):
        both = jnp.concatenate([own[j, HEAD:], came[j]], axis=0)
        for k in range((ALL - HEAD) // LANES):
            at = slice(k * LANES, (k + 1) * LANES)
            spot = slice(HEAD + k * LANES, HEAD + (k + 1) * LANES)
            placed[j, :, at] = shifted(both[at], index[1:2, spot])


def column_hot(index, at, wide):
    where = lax.broadcasted_iota(jnp.int32, (COLS, wide), 0) == index[0:1, pl.ds(at, wide)]
    return where.astype(F32).astype(BF16)


def chunks(head, tail, step):
    for source, at, base, wide in ((head, 0, 0, 256), (head, 256, 0, 128), (tail, 0, HEAD, 256), (tail, 256, HEAD, 256)):
        step(source, at, base + at, wide)


def atom_hot(index):
    codes = index[3:4, :]
    return (lax.broadcasted_iota(jnp.int32, (SLOTS, codes.shape[1]), 0) == codes).astype(F32).astype(BF16)


def shifted(block, shift):
    block = jnp.concatenate([jnp.transpose(block), jnp.zeros((NZ - PTS, LANES), F32)], axis=0)
    for bit in (64, 32, 16, 8, 4, 2, 1):
        block = jnp.where((shift & bit) != 0, pltpu.roll(block, bit, 0), block)
    return block


def gather_table(index, spread):
    codes = index[2:3, :]
    rows = jnp.concatenate([jnp.where(codes == code, spread, 0.0) for code in range(CODES)], axis=0)
    high, low = split(rows)
    atoms = atom_hot(index)
    return mul_t(high, atoms) + mul_t(low, atoms)


def project(both, hot, placed, partial, spot, at, wide):
    picked = mul(both, jnp.concatenate([hot, hot], axis=0))
    sums = [None] * ROWS
    for z in range(0, NZ, 8):
        lines = [picked[o * NZ + z : o * NZ + z + 8] for o in range(ORB)]
        for j in range(NPJ):
            values = placed[j, z : z + 8, pl.ds(spot, wide)]
            for o in range(ORB):
                term = lines[o] * values
                row = o * NPJ + j
                sums[row] = term if z == 0 else sums[row] + term
    for row in range(ROWS):
        partial[row : row + 1, pl.ds(at, wide)] = jnp.sum(sums[row], axis=0, keepdims=True)


def first_tables(index, turned, tables, both, proj, placed, partial):
    blocks = OWN // LANES

    def place(j):
        for k in range(blocks):
            block = proj[j, k * LANES : min((k + 1) * LANES, PIECES)]
            if k == blocks - 1:
                block = jnp.concatenate([block, jnp.zeros((OWN - PIECES, LANES), F32)], axis=0)
            placed[j, :, k * LANES : (k + 1) * LANES] = shifted(block, index[1:2, k * LANES : (k + 1) * LANES])

    each(NPJ, place)

    def table(s):
        for o in range(ORB):
            both[o * NZ : (o + 1) * NZ, :] = jnp.concatenate(split(turned[s * ORB + o]), axis=1)

        def chunk(k):
            at = k * 256
            where = lax.broadcasted_iota(jnp.int32, (LANES, 256), 0) == index[4:5, pl.ds(at, 256)]
            project(both[...], where.astype(F32).astype(BF16), placed, partial, at, at, 256)

        each(OWN // 256, chunk, False)
        tables[s] = gather_table(index, partial[...])

    each(2, table)


def table_kernel(index, field, head, tail, table, partial, both):
    def gather(o):
        rows = pl.ds(o * NZ, NZ)
        both[rows, :] = jnp.concatenate(split(field[o]), axis=1)

    each(ORB, gather, False)
    def chunk(placed, spot, at, wide):
        project(both[...], column_hot(index, at, wide), placed, partial, spot, at, wide)

    chunks(head, tail, chunk)
    table[...] = gather_table(index, partial[...])


def pair_sum(second, table, came):
    gap = jnp.zeros((THIRD, LANES), F32)
    up = table[THIRD:] + jnp.concatenate([came[HALF:], gap], axis=0)
    down = table[:HALF] + jnp.concatenate([gap, came[:THIRD]], axis=0)
    return jnp.where(second, up, down)


def join_table_kernel(table, note_came, field, out):
    out[...] = table[...] + note_came[:TABLE]


def first_pair_kernel(params, table, came, energy, note_came, half):
    half[:HALF] = pair_sum(flag(params, 1), table[...], came[...])
    upper = flag(params, 0)
    there = note_came[NOTE : NOTE + NPJ]
    half[HALF : HALF + NPJ] = jnp.where(upper, there, energy[...])
    half[HALF + NPJ :] = jnp.where(upper, energy[...], there)


def pair_kernel(params, table, came, half):
    half[...] = pair_sum(flag(params, 1), table[...], came[...])


def sum_kernel(mine, came, acc, low, high, acc_out):
    total = mine[:HALF] + came[:HALF]
    step = 2 * ROWS
    for q in range(2):
        low[q * step : (q + 1) * step] = total[2 * q * step : (2 * q + 1) * step]
        high[q * step : (q + 1) * step] = total[(2 * q + 1) * step : (2 * q + 2) * step]


def first_sum_kernel(params, mine, came, acc, low, high, acc_out):
    sum_kernel(mine, came, acc, low, high, acc_out)
    second = flag(params, 1)
    for sub, out in ((0, low), (1, high)):
        at = HALF + sub * NPJ
        here, there = mine[at : at + NPJ], came[at : at + NPJ]
        out[THIRD : THIRD + NPJ] = jnp.where(second, here, there)
        out[THIRD + NPJ :] = jnp.where(second, there, here)


def spread_energy(low, high, below, above, energy):
    for q in range(2):
        at = slice(THIRD + q * NPJ, THIRD + (q + 1) * NPJ)
        for r, source in enumerate((below, low, high, above)):
            row = (q * 4 + r) * ROWS
            energy[row : row + ROWS] = jnp.concatenate([source[at]] * ORB, axis=0)


def scale_of(first, params):
    row = 3 if first else 4
    return params[row : row + 1, 0:1]


def total_kernel(first, params, low, high, below, above, acc, energy, out, acc_out, energy_out=None):
    if first:
        spread_energy(low, high, below, above, energy_out)
        energy = energy_out
    step = 2 * ROWS
    scale = params[3 if first else 4 : 4 if first else 5, :]
    for q in range(2):
        at = slice(q * step, (q + 1) * step)
        row = 2 * q * step
        out[row : row + step] = (low[at] + below[at]) * energy[row : row + step] * scale
        row = row + step
        out[row : row + step] = (high[at] + above[at]) * energy[row : row + step] * scale


def first_total_kernel(params, low, high, below, above, acc, out, energy, acc_out):
    total_kernel(True, params, low, high, below, above, acc, None, out, acc_out, energy)


def later_total_kernel(params, low, high, below, above, energy, acc, out, acc_out):
    total_kernel(False, params, low, high, below, above, acc, energy, out, acc_out)


def local_kernel(first, params, half, field, before, pot, own_w, ring_w, out):
    center = params[2:3, 0:1]
    scale = scale_of(first, params)
    diagonal = pot[...] + (3.0 * WEIGHTS[0] * KINETIC - center)

    def step(o):
        value = field[o]
        high, low = split(value)
        across = three(high, low, own_w)
        along = mul(ring_w[0], high) + mul(ring_w[0], low) + mul(ring_w[1], high)
        total = scale * (across + along + diagonal * value)
        out[o] = total if first else total - before[o]

    each(ORB, step)


def halo_kernel(first, params, inner, outer, xl, xh, acc, halo_w, out):
    scale = scale_of(first, params)
    below_inner = flag(params, 1)

    def step(o):
        inside, outside = unpack_edge(inner[o]), unpack_edge(outer[o])
        bottom = jnp.where(below_inner, inside, outside)
        top = jnp.where(below_inner, outside, inside)
        line = jnp.concatenate([unpack_edge(xl[o]), unpack_edge(xh[o]), bottom, top], axis=1)
        high, low = split(line)
        out[o] = acc[o] + scale * three(high, low, halo_w)

    each(ORB, step)


def update_kernel(last, params, index, acc, mine, came, head, tail, *rest):
    if last:
        sent, field, coef_rows, near, far = rest
    else:
        edge, field, xl, xh, inner, outer, coef_rows = rest
    second = flag(params, 1)
    total = jnp.concatenate(
        [jnp.where(second, came[THIRD:], mine[...][:THIRD]), jnp.where(second, mine[...][:THIRD], mine[...][THIRD:]),
         jnp.where(second, mine[...][THIRD:], came[:THIRD])], axis=0
    )
    atoms = atom_hot(index)
    spread = mul(jnp.concatenate(split(total), axis=1), jnp.concatenate([atoms, atoms], axis=0))
    codes = index[2:3, :]
    coefs = jnp.zeros((ROWS, ALL), F32)
    for code in range(CODES):
        coefs = jnp.where(codes == code, spread[code * ROWS : (code + 1) * ROWS], coefs)
    coef_rows[...] = coefs
    sums = []

    def chunk(placed, spot, at, wide):
        hot = column_hot(index, at, wide)
        lines = []
        for o in range(ORB):
            rows = coef_rows[o * NPJ : (o + 1) * NPJ, pl.ds(at, wide)]
            line = rows[0:1] * placed[0, :, pl.ds(spot, wide)]
            for j in range(1, NPJ):
                line = line + rows[j : j + 1] * placed[j, :, pl.ds(spot, wide)]
            lines.append(jnp.concatenate(split(line), axis=1))
        term = mul_t(jnp.concatenate(lines, axis=0), jnp.concatenate([hot, hot], axis=1))
        sums[:] = [sums[0] + term if sums else term]

    chunks(head, tail, chunk)

    def finish(o):
        field[o] = acc[o] + sums[0][o * NZ : (o + 1) * NZ]

    each(ORB, finish, False)
    if not last:
        emit_edges(field, second, edge, xl, xh, inner, outer)
        return
    upper = flag(params, 0)

    def emit(o):
        left, right = field[o, :, :LANES], field[o, :, LANES:]
        for spot, pair in from_columns(jnp.where(upper, left, right), near, far):
            sent[o, :, spot : spot + 2 * NZ] = pair

    each(ORB, emit, False)


def join_kernel(params, came, b, mine, a, out, density):
    upper = params[0:1, 0:1] == 1.0
    density[...] = a[...] + b[...]

    def step(o):
        out[o] = jnp.where(upper, came[o], mine[o])
        out[ORB + o] = jnp.where(upper, mine[o], came[o])

    each(ORB, step)


def density_kernel(params, field, mine, across, plane, near, far):
    dens = jnp.zeros((NZ, COLS), F32)
    for o in range(ORB):
        dens = dens + params[8 + o : 9 + o, 0:1] * field[o] * field[o]
    left, right = dens[:, :LANES], dens[:, LANES:]
    upper = flag(params, 0)
    second = params[5:6, 0:1] == 1.0
    span = CY * NZ // 2
    for k, value in enumerate((jnp.where(upper, right, left), jnp.where(upper, left, right))):
        for spot, pair in from_columns(value, near, far):
            plane[:, spot : spot + 2 * NZ] = pair
        mine[k] = jnp.where(second, plane[:, span:], plane[:, :span])
        across[k] = jnp.where(second, plane[:, :span], plane[:, span:])


def keep_kernel(params, field, here, kept, near, far):
    upper = flag(params, 0)

    def emit(o):
        mine = jnp.where(upper, field[o, :, LANES:], field[o, :, :LANES])
        for spot, pair in from_columns(mine, near, far):
            kept[o, :, spot : spot + 2 * NZ] = pair

    each(ORB, emit)


def band_kernel(here, came, quarter, going):
    quarter[...] = here[0] + came[0]
    going[...] = here[1] + came[1]


VM = pl.BlockSpec(memory_space=pltpu.VMEM)
ANY = pl.BlockSpec(memory_space=pl.ANY)
HB = pl.BlockSpec(memory_space=pltpu.HBM)


def call(kernel, in_specs, shapes, args, scratch=(), flops=10**8, name=None, passed=0, room=48):
    single = isinstance(shapes, tuple)
    outs = [shapes] if single else list(shapes)
    outs = [shape if isinstance(shape[0], tuple) else (shape, F32) for shape in outs]
    plain = len(outs) - passed
    result = pl.pallas_call(
        kernel,
        out_shape=[jax.ShapeDtypeStruct(*out) for out in outs],
        in_specs=in_specs,
        out_specs=[VM] * plain + [ANY] * passed,
        scratch_shapes=list(scratch),
        input_output_aliases={len(args) - passed + k: plain + k for k in range(passed)},
        compiler_params=pltpu.CompilerParams(vmem_limit_bytes=room * 1024 * 1024),
        cost_estimate=pl.CostEstimate(flops=flops, bytes_accessed=4 * 10**6, transcendentals=0),
        name=name,
    )(*args)
    return result[0] if single else result


def send(value, pairs):
    return lax.ppermute(value, "dom", pairs)


def along_z(step):
    return [(d, (d + 16 * step) % 64) for d in range(64)]


def outward(d):
    y = d % 8
    return d // 8 * 8 + ((y - 1) % 8 if y % 2 == 0 else (y + 1) % 8)


SWAP = [(d, d ^ 8) for d in range(64)]
CORES = [(d, d ^ 1) for d in range(64)]
OUTER = [(d, outward(d)) for d in range(64)]


def body(
    orbitals,
    occupation,
    potential,
    projectors,
    energies,
    piece_column,
    piece_shift,
    piece_owner,
    piece_atom,
    lower_edge,
    upper_edge,
):
    own_m, halo_m, ring_m, edge_m = stencil_matrices()
    own_w = jnp.asarray(np.stack(two_parts(own_m)))
    halo_w = jnp.asarray(np.stack(two_parts(halo_m)))
    ring_w = jnp.asarray(np.stack(two_parts(ring_m)))
    edge_w = jnp.asarray(edge_m.astype(np.float32).astype(jnp.bfloat16))

    row = lax.broadcasted_iota(jnp.int32, (8, LANES), 0)
    ends = jnp.where(row == 0, upper_edge[0], lower_edge[0])
    packed = (ORB, PACKED, LANES)
    grid = (ORB, NZ, COLS)
    stage = [pltpu.VMEM((LANES, LANES), F32)] * 2

    raw = orbitals[:, 0]
    message = call(
        pick_kernel,
        [HB] * 2,
        (ORB + 1, CX, CY * NZ),
        (raw, potential),
        [pltpu.SemaphoreType.DMA((2,))],
        flops=10**6,
        name="pick",
        room=ROOM,
    )
    came = send(message, SWAP)
    line = pltpu.VMEM((1, PIECES), jnp.int32)
    keep, params, ints, own_table, note = call(
        begin_kernel,
        [HB] * 8,
        [
            (ORB, NZ, LANES),
            (16, LANES),
            ((8, OWN), jnp.int32),
            (TABLE, LANES),
            (NOTE + 24, LANES),
        ],
        (
            occupation, piece_column, piece_shift, piece_owner, piece_atom,
            raw, projectors[0], energies[0],
        ),
        [
            line, line, line, line,
            pltpu.VMEM((2 * ORB, CX, CY * NZ), F32),
            pltpu.VMEM((NPJ, PIECES, LANES), F32),
            pltpu.VMEM((NPJ, LANES), F32),
            pltpu.VMEM((2 * ORB, NZ, LANES), F32),
            pltpu.VMEM((2, TABLE, LANES), F32),
            pltpu.VMEM((ORB * NZ, 2 * LANES), BF16),
            pltpu.VMEM((NPJ, NZ, OWN), F32),
            pltpu.VMEM((ROWS, OWN), F32),
            *stage,
            pltpu.SMEM((2 * ORB,), F32),
            pltpu.SemaphoreType.DMA((8,)),
        ],
        name="begin",
        room=ROOM,
    )
    note_came = send(note, SWAP)
    proj = call(gate_kernel, [ANY] * 3, [(NPJ, PIECES, LANES)], (came, note_came, projectors[0]), flops=10**6, name="gate", passed=1)
    proj_came = send(proj[0], SWAP)
    params, field, pot, xl, xh, inner, outer = call(
        start_kernel,
        [VM] * 6,
        [(16, LANES), grid, (NZ, COLS)] + [packed] * 4,
        (params, ends, keep, came, potential, edge_w),
        stage,
        name="start",
    )
    table = call(
        join_table_kernel, [VM] * 2 + [ANY], (TABLE, LANES), (own_table, note_came, field), flops=10**6, name="join_table"
    )
    head = call(own_kernel, [VM] * 2 + [ANY], (NPJ, NZ, HEAD), (ints, projectors[0], table), name="own")
    tail, index = call(
        prepare_kernel,
        [VM] * 4,
        [(NPJ, NZ, ALL - HEAD), ((4, ALL), jnp.int32)],
        (ints, note_came, projectors[0], proj_came),
        name="prepare",
    )

    sums_room = [pltpu.VMEM((ROWS, ALL), F32)]
    before = field
    for level in range(DEG):
        first, last = level == 0, level == DEG - 1
        if not first:
            table = call(
                table_kernel,
                [VM] * 4,
                (TABLE, LANES),
                (index, field, head, tail),
                [pltpu.VMEM((ROWS, ALL), F32), pltpu.VMEM((ORB * NZ, 2 * COLS), BF16)],
                name="table",
            )
        inner_came = send(inner, CORES)
        table_came = send(table, CORES)
        if first:
            half = call(
                first_pair_kernel,
                [VM] * 5,
                (HALF + 8, LANES),
                (params, table, table_came, energies[0], note_came),
                flops=10**6,
                name="pair",
            )
        else:
            half = call(pair_kernel, [VM] * 3, (HALF, LANES), (params, table, table_came), flops=10**6, name="pair")
        half_came = send(half, OUTER)
        xl_came = send(xh, along_z(1))
        xh_came = send(xl, along_z(-1))
        outer_came = send(outer, OUTER)
        acc = call(
            functools.partial(local_kernel, first),
            [VM, ANY] + [VM] * 5,
            grid,
            (params, half, field, before, pot, own_w, ring_w),
            name="local",
        )
        size = (THIRD + 8, LANES) if first else (THIRD, LANES)
        low, high, acc = call(
            first_sum_kernel if first else sum_kernel,
            [VM] * (3 if first else 2) + [ANY],
            [size, size, grid],
            ((params,) if first else ()) + (half, half_came, acc),
            flops=10**6,
            name="sums",
            passed=1,
        )
        below = send(high, along_z(1))
        above = send(low, along_z(-1))
        acc = call(
            functools.partial(halo_kernel, first),
            [VM] * 7,
            grid,
            (params, inner_came, outer_came, xl_came, xh_came, acc, halo_w),
            name="halo",
        )
        if first:
            total, energy, acc = call(
                first_total_kernel,
                [VM] * 5 + [ANY],
                [(HALF, LANES), (HALF, LANES), grid],
                (params, low, high, below, above, acc),
                flops=10**6,
                name="totals",
                passed=1,
            )
        else:
            total, acc = call(
                later_total_kernel,
                [VM] * 6 + [ANY],
                [(HALF, LANES), grid],
                (params, low, high, below, above, energy, acc),
                flops=10**6,
                name="totals",
                passed=1,
            )
        total_came = send(total, CORES)
        args = (params, index, acc, total, total_came, head, tail)
        if not last:
            before, (field, xl, xh, inner, outer) = field, call(
                functools.partial(update_kernel, last),
                [VM] * 8,
                [grid] + [packed] * 4,
                args + (edge_w,),
                sums_room,
                name="update",
            )
        else:
            flat = (ORB, CX, CY * NZ)
            other, result = call(
                functools.partial(update_kernel, last),
                [VM] * 7,
                [flat, grid],
                args,
                sums_room + stage,
                name="finish",
            )
    part = (CX, CY * NZ // 2)
    here_parts, across = call(
        density_kernel,
        [VM] * 2,
        [(2,) + part] * 2,
        (params, result),
        [pltpu.VMEM((CX, CY * NZ), F32)] + stage,
        name="density",
    )
    swapped = send(other, SWAP)
    across_came = lax.ppermute(across, "band", [(0, 1), (1, 0)])
    mine = call(keep_kernel, [VM, VM, ANY], flat, (params, result, across), stage, name="keep")
    quarter, going = call(band_kernel, [VM] * 2, [part] * 2, (here_parts, across_came), flops=10**6, name="band")
    filtered, density = call(
        join_kernel,
        [VM] * 5,
        [(2 * ORB, CX, CY * NZ), part],
        (params, swapped, send(going, SWAP), mine, quarter),
        name="join",
    )
    return filtered[:, None], density[None]


def solution(mesh):
    in_specs = (
        P("band", "dom", None, None),
        P("band"),
        P("dom", None, None),
        P("dom", None, None, None),
        P("dom", None, None),
        P("dom", None),
        P("dom", None),
        P("dom", None),
        P("dom", None),
        P(),
        P(),
    )
    out_specs = (P("band", "dom", None, None), P("dom", None, "band"))
    return jax.shard_map(body, mesh=mesh, in_specs=in_specs, out_specs=out_specs, check_vma=False)
```

```python
import functools

import jax
import jax.numpy as jnp
import numpy as np
from jax import lax
from jax.experimental import pallas as pl
from jax.experimental.pallas import tpu as pltpu
from jax.sharding import PartitionSpec as P

NZ = 192
HALO = 6
DEG = 4
CX = 8
CY = 16
WX = 2 * CX
COLS = WX * CY
ORB = 4
NPJ = 4
PIECES = 448
ALL = 2 * PIECES
PTS = 128
SLOTS = 128
ROWS = ORB * NPJ
PACKED = 144
TAIL = NZ - PACKED
LANES = 128
EDGE = HALO * 16
OWN = 512
HEAD = 384
ROOM = 58
CODES = 12
TABLE = CODES * ROWS
THIRD = TABLE // 3
HALF = 2 * THIRD
NOTE = TABLE

WEIGHTS = (
    -5369.0 / 1800.0,
    12.0 / 7.0,
    -15.0 / 56.0,
    10.0 / 189.0,
    -1.0 / 112.0,
    2.0 / 1925.0,
    -1.0 / 16632.0,
)
KINETIC = -0.5 / 0.16
F32 = jnp.float32
BF16 = jnp.bfloat16


def coupling(steps):
    reach = np.abs(steps)
    near = (reach >= 1) & (reach <= HALO)
    table = np.array(WEIGHTS) * KINETIC
    return np.where(near, table[np.minimum(reach, HALO)], 0.0)


def stencil_matrices():
    col = np.arange(COLS)
    x, y = col // CY, col % CY
    same_x = x[:, None] == x[None, :]
    same_y = y[:, None] == y[None, :]
    own = np.where(same_y, coupling(x[None, :] - x[:, None]), 0.0)
    own = own + np.where(same_x, coupling(y[None, :] - y[:, None]), 0.0)
    lane = np.arange(LANES)
    used = (lane < EDGE)[:, None]
    parts = []
    for start in (-HALO, WX):
        hx, hy = start + lane // CY, lane % CY
        parts.append(np.where(used & (hy[:, None] == y[None, :]), coupling(x[None, :] - hx[:, None]), 0.0))
    for start in (-HALO, CY):
        hy, hx = start + lane // WX, lane % WX
        parts.append(np.where(used & (hx[:, None] == x[None, :]), coupling(y[None, :] - hy[:, None]), 0.0))
    halo = np.concatenate(parts, axis=0)
    depth = np.arange(NZ)
    apart = (depth[None, :] - depth[:, None] + NZ // 2) % NZ - NZ // 2
    ring = coupling(apart)
    picks = []
    for start in (0, CY - HALO):
        hy, hx = start + lane // WX, lane % WX
        picks.append(np.where(used.T & (col[:, None] == (hx * CY + hy)[None, :]), 1.0, 0.0))
    edge = np.concatenate(picks, axis=1)
    return own, halo, ring, edge


def two_parts(matrix):
    high = np.asarray(matrix, np.float32).astype(jnp.bfloat16)
    low = (np.asarray(matrix, np.float64) - high.astype(np.float64)).astype(np.float32).astype(jnp.bfloat16)
    return high, low


def split(value):
    high = value.astype(BF16)
    low = (value - high.astype(F32)).astype(BF16)
    return high, low


def mul(left, right):
    return jnp.dot(left, right, preferred_element_type=F32)


def mul_t(left, right):
    return lax.dot_general(left, right, (((1,), (1,)), ((), ())), preferred_element_type=F32)


def three(high, low, parts):
    return mul(high, parts[0]) + mul(low, parts[0]) + mul(high, parts[1])


def pack_edge(value):
    main = value[:PACKED]
    lane = lax.broadcasted_iota(jnp.int32, (TAIL, LANES), 1)
    rows = []
    for k in range(3):
        tail = pltpu.roll(value[PACKED:], (EDGE - 32 * k) % LANES, 1)
        rows.append(jnp.where(lane < EDGE, main[k * TAIL : (k + 1) * TAIL], tail))
    return jnp.concatenate(rows, axis=0)


def unpack_edge(value):
    lane = lax.broadcasted_iota(jnp.int32, (TAIL, LANES), 1)
    tail = jnp.zeros((TAIL, LANES), F32)
    for k in range(3):
        moved = pltpu.roll(value[k * TAIL : (k + 1) * TAIL], (32 * k - EDGE) % LANES, 1)
        tail = jnp.where((lane >= 32 * k) & (lane < 32 * k + 32), moved, tail)
    return jnp.concatenate([value, tail], axis=0)


def each(count, step, loop=True):
    if not loop:
        for k in range(count):
            step(k)
        return

    def run(k, carry):
        step(k)
        return carry

    lax.fori_loop(0, count, run, 0)


def emit_edges(field, below_inner, edge_ref, xl_ref, xh_ref, inner_ref, outer_ref):
    def step(o):
        value = field[o]
        high, low = split(value)
        picked = mul(high, edge_ref[...]) + mul(low, edge_ref[...])
        xl_ref[o] = pack_edge(value[:, :LANES])
        xh_ref[o] = pack_edge(pltpu.roll(value[:, LANES:], LANES - 32, 1))
        bottom, top = pack_edge(picked[:, :LANES]), pack_edge(picked[:, LANES:])
        inner_ref[o] = jnp.where(below_inner, bottom, top)
        outer_ref[o] = jnp.where(below_inner, top, bottom)

    each(ORB, step, False)


def to_columns(source, near, far):
    for y in range(CY):
        at = y * NZ
        line = source(at)
        near[pl.ds(y, CX, stride=CY), :] = line[:, :LANES]
        tail = line[:, LANES:]
        far[pl.ds(y, CX, stride=CY), :] = jnp.concatenate([tail, jnp.zeros((CX, 2 * LANES - NZ), F32)], axis=1)
    return jnp.concatenate([jnp.transpose(near[...]), jnp.transpose(far[...])[: NZ - LANES]], axis=0)


def from_columns(value, near, far):
    near[...] = jnp.transpose(value[:LANES])
    far[...] = jnp.transpose(jnp.concatenate([value[LANES:], jnp.zeros((2 * LANES - NZ, LANES), F32)], axis=0))
    for y in range(0, CY, 2):
        lines = []
        for at in (y, y + 1):
            lines.append(near[pl.ds(at, CX, stride=CY), :])
            lines.append(far[pl.ds(at, CX, stride=CY), :][:, : NZ - LANES])
        yield y * NZ, jnp.concatenate(lines, axis=1)


def flag(params, row):
    return params[row : row + 1, :] == 1.0


def pick_kernel(raw, potential, out, sems):
    start = (1 - lax.axis_index("dom") // 8 % 2) * ORB
    first = pltpu.make_async_copy(raw.at[pl.ds(start, ORB)], out.at[pl.ds(0, ORB)], sems.at[0])
    second = pltpu.make_async_copy(potential, out.at[pl.ds(ORB, 1)], sems.at[1])
    first.start()
    second.start()
    first.wait()
    second.wait()


def begin_kernel(
    weights_in, column_in, shift_in, owner_in, atom_in, raw_in, proj_in, energy_in,
    keep, params, ints, table, note,
    column, shift, owner, atom, raw, proj, energy, turned, tables, both, placed, partial, near, far, weights, sems,
):
    pairs = (
        (raw_in, raw), (column_in, column), (shift_in, shift), (owner_in, owner),
        (atom_in, atom), (weights_in, weights),
        (proj_in, proj), (energy_in, energy),
    )
    copies = [pltpu.make_async_copy(source, target, sems.at[k]) for k, (source, target) in enumerate(pairs)]
    for copy in copies:
        copy.start()
    for copy in copies[:6]:
        copy.wait()
    here = lax.axis_index("dom")
    side, core = here // 8 % 2, here % 2
    upper = jnp.full((1, LANES), side, jnp.int32) == 1
    params[0:1] = jnp.full((1, LANES), side, jnp.int32).astype(F32)
    params[1:2] = jnp.full((1, LANES), core, jnp.int32).astype(F32)
    params[2:5] = jnp.zeros((3, LANES), F32)
    params[5:6] = jnp.full((1, LANES), lax.axis_index("band"), jnp.int32).astype(F32)
    params[6:8] = jnp.zeros((2, LANES), F32)
    for o in range(ORB):
        params[8 + o : 9 + o] = jnp.full((1, LANES), weights[side * ORB + o], F32)
    params[8 + ORB :] = jnp.zeros((8 - ORB, LANES), F32)
    sub = jnp.full((1, PIECES), side, jnp.int32)
    step_x = (owner[...] >= 3).astype(jnp.int32) + (owner[...] >= 6).astype(jnp.int32)
    row = owner[...] - 3 * step_x
    lines = [
        sub * LANES + column[...],
        shift[...],
        row * 4 + sub + step_x,
        atom[...],
        column[...],
    ]
    gap = jnp.full((1, OWN - PIECES), -1, jnp.int32)
    for k, line in enumerate(lines):
        ints[k : k + 1] = jnp.concatenate([line, gap], axis=1)
    ints[len(lines) :] = jnp.zeros((8 - len(lines), OWN), jnp.int32)
    def turn(o):
        def kept(at):
            return jnp.where(upper[:, :1], raw[ORB + o, :, at : at + NZ], raw[o, :, at : at + NZ])

        def sent(at):
            return jnp.where(upper[:, :1], raw[o, :, at : at + NZ], raw[ORB + o, :, at : at + NZ])

        turned[o] = to_columns(kept, near, far)
        turned[ORB + o] = to_columns(sent, near, far)
        keep[o] = turned[o]

    each(ORB, turn)
    for copy in copies[6:]:
        copy.wait()
    first_tables(ints, turned, tables, both, proj, placed, partial)
    table[...] = tables[0]
    note[:TABLE] = tables[1]
    note[NOTE : NOTE + NPJ] = energy[...]
    note[NOTE + NPJ : NOTE + 8] = jnp.zeros((4, LANES), F32)
    numbers = ints[:4].astype(F32)
    for k in range(OWN // LANES):
        note[NOTE + 8 + 4 * k : NOTE + 12 + 4 * k] = numbers[:, k * LANES : (k + 1) * LANES]


def start_kernel(flags, ends, keep, came, potential, edge, params, field, pot, xl, xh, inner, outer, near, far):
    params[...] = flags[...]
    top, bottom = ends[0:1], ends[1:2]
    half_width = (top - bottom) / 2.0
    params[2:3] = (top + bottom) / 2.0
    params[3:4] = 1.0 / half_width
    params[4:5] = 2.0 / half_width
    upper = flag(params, 0)
    here = to_columns(lambda at: potential[0, :, at : at + NZ], near, far)
    there = to_columns(lambda at: came[ORB, :, at : at + NZ], near, far)
    pot[:, :LANES] = jnp.where(upper, there, here)
    pot[:, LANES:] = jnp.where(upper, here, there)

    def step(o):
        turned = to_columns(lambda at: came[o, :, at : at + NZ], near, far)
        kept = keep[o]
        field[o, :, :LANES] = jnp.where(upper, turned, kept)
        field[o, :, LANES:] = jnp.where(upper, kept, turned)

    each(ORB, step, False)
    emit_edges(field, flag(params, 1), edge, xl, xh, inner, outer)


def gate_kernel(came, note_came, proj, out):
    pass


def own_kernel(ints, own, note, placed):
    for j in range(NPJ):
        for k in range(HEAD // LANES):
            at = slice(k * LANES, (k + 1) * LANES)
            placed[j, :, at] = shifted(own[j, at], ints[1:2, at])


def prepare_kernel(ints, note_came, own, came, placed, index):
    lines = [note_came[NOTE + 8 + 4 * k : NOTE + 12 + 4 * k] for k in range(OWN // LANES)]
    other = jnp.concatenate(lines, axis=1)[:, :PIECES].astype(jnp.int32)
    index[...] = jnp.concatenate([ints[:4, :PIECES], other], axis=1)
    for j in range(NPJ):
        both = jnp.concatenate([own[j, HEAD:], came[j]], axis=0)
        for k in range((ALL - HEAD) // LANES):
            at = slice(k * LANES, (k + 1) * LANES)
            spot = slice(HEAD + k * LANES, HEAD + (k + 1) * LANES)
            placed[j, :, at] = shifted(both[at], index[1:2, spot])


def column_hot(index, at, wide):
    where = lax.broadcasted_iota(jnp.int32, (COLS, wide), 0) == index[0:1, pl.ds(at, wide)]
    return where.astype(F32).astype(BF16)


def chunks(head, tail, step):
    for source, at, base, wide in ((head, 0, 0, 256), (head, 256, 0, 128), (tail, 0, HEAD, 256), (tail, 256, HEAD, 256)):
        step(source, at, base + at, wide)


def atom_hot(index):
    codes = index[3:4, :]
    return (lax.broadcasted_iota(jnp.int32, (SLOTS, codes.shape[1]), 0) == codes).astype(F32).astype(BF16)


def shifted(block, shift):
    block = jnp.concatenate([jnp.transpose(block), jnp.zeros((NZ - PTS, LANES), F32)], axis=0)
    for bit in (64, 32, 16, 8, 4, 2, 1):
        block = jnp.where((shift & bit) != 0, pltpu.roll(block, bit, 0), block)
    return block


def gather_table(index, spread):
    codes = index[2:3, :]
    rows = jnp.concatenate([jnp.where(codes == code, spread, 0.0) for code in range(CODES)], axis=0)
    high, low = split(rows)
    atoms = atom_hot(index)
    return mul_t(high, atoms) + mul_t(low, atoms)


def project(both, hot, placed, partial, spot, at, wide):
    picked = mul(both, jnp.concatenate([hot, hot], axis=0))
    sums = [None] * ROWS
    for z in range(0, NZ, 8):
        lines = [picked[o * NZ + z : o * NZ + z + 8] for o in range(ORB)]
        for j in range(NPJ):
            values = placed[j, z : z + 8, pl.ds(spot, wide)]
            for o in range(ORB):
                term = lines[o] * values
                row = o * NPJ + j
                sums[row] = term if z == 0 else sums[row] + term
    for row in range(ROWS):
        partial[row : row + 1, pl.ds(at, wide)] = jnp.sum(sums[row], axis=0, keepdims=True)


def first_tables(index, turned, tables, both, proj, placed, partial):
    blocks = OWN // LANES

    def place(j):
        for k in range(blocks):
            block = proj[j, k * LANES : min((k + 1) * LANES, PIECES)]
            if k == blocks - 1:
                block = jnp.concatenate([block, jnp.zeros((OWN - PIECES, LANES), F32)], axis=0)
            placed[j, :, k * LANES : (k + 1) * LANES] = shifted(block, index[1:2, k * LANES : (k + 1) * LANES])

    each(NPJ, place)

    def table(s):
        for o in range(ORB):
            both[o * NZ : (o + 1) * NZ, :] = jnp.concatenate(split(turned[s * ORB + o]), axis=1)

        def chunk(k):
            at = k * 256
            where = lax.broadcasted_iota(jnp.int32, (LANES, 256), 0) == index[4:5, pl.ds(at, 256)]
            project(both[...], where.astype(F32).astype(BF16), placed, partial, at, at, 256)

        each(OWN // 256, chunk, False)
        tables[s] = gather_table(index, partial[...])

    each(2, table)


def table_kernel(index, field, head, tail, table, partial, both):
    def gather(o):
        rows = pl.ds(o * NZ, NZ)
        both[rows, :] = jnp.concatenate(split(field[o]), axis=1)

    each(ORB, gather, False)
    def chunk(placed, spot, at, wide):
        project(both[...], column_hot(index, at, wide), placed, partial, spot, at, wide)

    chunks(head, tail, chunk)
    table[...] = gather_table(index, partial[...])


def pair_sum(second, table, came):
    gap = jnp.zeros((THIRD, LANES), F32)
    up = table[THIRD:] + jnp.concatenate([came[HALF:], gap], axis=0)
    down = table[:HALF] + jnp.concatenate([gap, came[:THIRD]], axis=0)
    return jnp.where(second, up, down)


def join_table_kernel(table, note_came, field, out):
    out[...] = table[...] + note_came[:TABLE]


def first_pair_kernel(params, table, came, energy, note_came, half):
    half[:HALF] = pair_sum(flag(params, 1), table[...], came[...])
    upper = flag(params, 0)
    there = note_came[NOTE : NOTE + NPJ]
    half[HALF : HALF + NPJ] = jnp.where(upper, there, energy[...])
    half[HALF + NPJ :] = jnp.where(upper, energy[...], there)


def pair_kernel(params, table, came, half):
    half[...] = pair_sum(flag(params, 1), table[...], came[...])


def sum_kernel(mine, came, acc, low, high, acc_out):
    total = mine[:HALF] + came[:HALF]
    step = 2 * ROWS
    for q in range(2):
        low[q * step : (q + 1) * step] = total[2 * q * step : (2 * q + 1) * step]
        high[q * step : (q + 1) * step] = total[(2 * q + 1) * step : (2 * q + 2) * step]


def first_sum_kernel(params, mine, came, acc, low, high, acc_out):
    sum_kernel(mine, came, acc, low, high, acc_out)
    second = flag(params, 1)
    for sub, out in ((0, low), (1, high)):
        at = HALF + sub * NPJ
        here, there = mine[at : at + NPJ], came[at : at + NPJ]
        out[THIRD : THIRD + NPJ] = jnp.where(second, here, there)
        out[THIRD + NPJ :] = jnp.where(second, there, here)


def spread_energy(low, high, below, above, energy):
    for q in range(2):
        at = slice(THIRD + q * NPJ, THIRD + (q + 1) * NPJ)
        for r, source in enumerate((below, low, high, above)):
            row = (q * 4 + r) * ROWS
            energy[row : row + ROWS] = jnp.concatenate([source[at]] * ORB, axis=0)


def scale_of(first, params):
    row = 3 if first else 4
    return params[row : row + 1, 0:1]


def total_kernel(first, params, low, high, below, above, acc, energy, out, acc_out, energy_out=None):
    if first:
        spread_energy(low, high, below, above, energy_out)
        energy = energy_out
    step = 2 * ROWS
    scale = params[3 if first else 4 : 4 if first else 5, :]
    for q in range(2):
        at = slice(q * step, (q + 1) * step)
        row = 2 * q * step
        out[row : row + step] = (low[at] + below[at]) * energy[row : row + step] * scale
        row = row + step
        out[row : row + step] = (high[at] + above[at]) * energy[row : row + step] * scale


def first_total_kernel(params, low, high, below, above, acc, out, energy, acc_out):
    total_kernel(True, params, low, high, below, above, acc, None, out, acc_out, energy)


def later_total_kernel(params, low, high, below, above, energy, acc, out, acc_out):
    total_kernel(False, params, low, high, below, above, acc, energy, out, acc_out)


def local_kernel(first, params, half, field, before, pot, own_w, ring_w, out):
    center = params[2:3, 0:1]
    scale = scale_of(first, params)
    diagonal = pot[...] + (3.0 * WEIGHTS[0] * KINETIC - center)

    def step(o):
        value = field[o]
        high, low = split(value)
        across = three(high, low, own_w)
        along = mul(ring_w[0], high) + mul(ring_w[0], low) + mul(ring_w[1], high)
        total = scale * (across + along + diagonal * value)
        out[o] = total if first else total - before[o]

    each(ORB, step)


def halo_kernel(first, params, inner, outer, xl, xh, acc, halo_w, out):
    scale = scale_of(first, params)
    below_inner = flag(params, 1)

    def step(o):
        inside, outside = unpack_edge(inner[o]), unpack_edge(outer[o])
        bottom = jnp.where(below_inner, inside, outside)
        top = jnp.where(below_inner, outside, inside)
        line = jnp.concatenate([unpack_edge(xl[o]), unpack_edge(xh[o]), bottom, top], axis=1)
        high, low = split(line)
        out[o] = acc[o] + scale * three(high, low, halo_w)

    each(ORB, step)


def update_kernel(last, params, index, acc, mine, came, head, tail, *rest):
    if last:
        sent, field, coef_rows, near, far = rest
    else:
        edge, field, xl, xh, inner, outer, coef_rows = rest
    second = flag(params, 1)
    total = jnp.concatenate(
        [jnp.where(second, came[THIRD:], mine[...][:THIRD]), jnp.where(second, mine[...][:THIRD], mine[...][THIRD:]),
         jnp.where(second, mine[...][THIRD:], came[:THIRD])], axis=0
    )
    atoms = atom_hot(index)
    spread = mul(jnp.concatenate(split(total), axis=1), jnp.concatenate([atoms, atoms], axis=0))
    codes = index[2:3, :]
    coefs = jnp.zeros((ROWS, ALL), F32)
    for code in range(CODES):
        coefs = jnp.where(codes == code, spread[code * ROWS : (code + 1) * ROWS], coefs)
    coef_rows[...] = coefs
    sums = []

    def chunk(placed, spot, at, wide):
        hot = column_hot(index, at, wide)
        lines = []
        for o in range(ORB):
            rows = coef_rows[o * NPJ : (o + 1) * NPJ, pl.ds(at, wide)]
            line = rows[0:1] * placed[0, :, pl.ds(spot, wide)]
            for j in range(1, NPJ):
                line = line + rows[j : j + 1] * placed[j, :, pl.ds(spot, wide)]
            lines.append(jnp.concatenate(split(line), axis=1))
        term = mul_t(jnp.concatenate(lines, axis=0), jnp.concatenate([hot, hot], axis=1))
        sums[:] = [sums[0] + term if sums else term]

    chunks(head, tail, chunk)

    def finish(o):
        field[o] = acc[o] + sums[0][o * NZ : (o + 1) * NZ]

    each(ORB, finish, False)
    if not last:
        emit_edges(field, second, edge, xl, xh, inner, outer)
        return
    upper = flag(params, 0)

    def emit(o):
        left, right = field[o, :, :LANES], field[o, :, LANES:]
        for spot, pair in from_columns(jnp.where(upper, left, right), near, far):
            sent[o, :, spot : spot + 2 * NZ] = pair

    each(ORB, emit, False)


def join_kernel(params, came, b, mine, a, out, density):
    upper = params[0:1, 0:1] == 1.0
    density[...] = a[...] + b[...]

    def step(o):
        out[o] = jnp.where(upper, came[o], mine[o])
        out[ORB + o] = jnp.where(upper, mine[o], came[o])

    each(ORB, step, False)


def density_kernel(params, field, mine, across, plane, near, far):
    dens = jnp.zeros((NZ, COLS), F32)
    for o in range(ORB):
        dens = dens + params[8 + o : 9 + o, 0:1] * field[o] * field[o]
    left, right = dens[:, :LANES], dens[:, LANES:]
    upper = flag(params, 0)
    second = params[5:6, 0:1] == 1.0
    span = CY * NZ // 2
    for k, value in enumerate((jnp.where(upper, right, left), jnp.where(upper, left, right))):
        for spot, pair in from_columns(value, near, far):
            plane[:, spot : spot + 2 * NZ] = pair
        mine[k] = jnp.where(second, plane[:, span:], plane[:, :span])
        across[k] = jnp.where(second, plane[:, :span], plane[:, span:])


def keep_kernel(params, field, here, kept, near, far):
    upper = flag(params, 0)

    def emit(o):
        mine = jnp.where(upper, field[o, :, LANES:], field[o, :, :LANES])
        for spot, pair in from_columns(mine, near, far):
            kept[o, :, spot : spot + 2 * NZ] = pair

    each(ORB, emit)


def band_kernel(here, came, quarter, going):
    quarter[...] = here[0] + came[0]
    going[...] = here[1] + came[1]


VM = pl.BlockSpec(memory_space=pltpu.VMEM)
ANY = pl.BlockSpec(memory_space=pl.ANY)
HB = pl.BlockSpec(memory_space=pltpu.HBM)


def call(kernel, in_specs, shapes, args, scratch=(), flops=10**8, name=None, passed=0, room=48):
    single = isinstance(shapes, tuple)
    outs = [shapes] if single else list(shapes)
    outs = [shape if isinstance(shape[0], tuple) else (shape, F32) for shape in outs]
    plain = len(outs) - passed
    result = pl.pallas_call(
        kernel,
        out_shape=[jax.ShapeDtypeStruct(*out) for out in outs],
        in_specs=in_specs,
        out_specs=[VM] * plain + [ANY] * passed,
        scratch_shapes=list(scratch),
        input_output_aliases={len(args) - passed + k: plain + k for k in range(passed)},
        compiler_params=pltpu.CompilerParams(vmem_limit_bytes=room * 1024 * 1024),
        cost_estimate=pl.CostEstimate(flops=flops, bytes_accessed=4 * 10**6, transcendentals=0),
        name=name,
    )(*args)
    return result[0] if single else result


def send(value, pairs):
    return lax.ppermute(value, "dom", pairs)


def along_z(step):
    return [(d, (d + 16 * step) % 64) for d in range(64)]


def outward(d):
    y = d % 8
    return d // 8 * 8 + ((y - 1) % 8 if y % 2 == 0 else (y + 1) % 8)


SWAP = [(d, d ^ 8) for d in range(64)]
CORES = [(d, d ^ 1) for d in range(64)]
OUTER = [(d, outward(d)) for d in range(64)]


def body(
    orbitals,
    occupation,
    potential,
    projectors,
    energies,
    piece_column,
    piece_shift,
    piece_owner,
    piece_atom,
    lower_edge,
    upper_edge,
):
    own_m, halo_m, ring_m, edge_m = stencil_matrices()
    own_w = jnp.asarray(np.stack(two_parts(own_m)))
    halo_w = jnp.asarray(np.stack(two_parts(halo_m)))
    ring_w = jnp.asarray(np.stack(two_parts(ring_m)))
    edge_w = jnp.asarray(edge_m.astype(np.float32).astype(jnp.bfloat16))

    row = lax.broadcasted_iota(jnp.int32, (8, LANES), 0)
    ends = jnp.where(row == 0, upper_edge[0], lower_edge[0])
    packed = (ORB, PACKED, LANES)
    grid = (ORB, NZ, COLS)
    stage = [pltpu.VMEM((LANES, LANES), F32)] * 2

    raw = orbitals[:, 0]
    message = call(
        pick_kernel,
        [HB] * 2,
        (ORB + 1, CX, CY * NZ),
        (raw, potential),
        [pltpu.SemaphoreType.DMA((2,))],
        flops=10**6,
        name="pick",
        room=ROOM,
    )
    came = send(message, SWAP)
    line = pltpu.VMEM((1, PIECES), jnp.int32)
    keep, params, ints, own_table, note = call(
        begin_kernel,
        [HB] * 8,
        [
            (ORB, NZ, LANES),
            (16, LANES),
            ((8, OWN), jnp.int32),
            (TABLE, LANES),
            (NOTE + 24, LANES),
        ],
        (
            occupation, piece_column, piece_shift, piece_owner, piece_atom,
            raw, projectors[0], energies[0],
        ),
        [
            line, line, line, line,
            pltpu.VMEM((2 * ORB, CX, CY * NZ), F32),
            pltpu.VMEM((NPJ, PIECES, LANES), F32),
            pltpu.VMEM((NPJ, LANES), F32),
            pltpu.VMEM((2 * ORB, NZ, LANES), F32),
            pltpu.VMEM((2, TABLE, LANES), F32),
            pltpu.VMEM((ORB * NZ, 2 * LANES), BF16),
            pltpu.VMEM((NPJ, NZ, OWN), F32),
            pltpu.VMEM((ROWS, OWN), F32),
            *stage,
            pltpu.SMEM((2 * ORB,), F32),
            pltpu.SemaphoreType.DMA((8,)),
        ],
        name="begin",
        room=ROOM,
    )
    note_came = send(note, SWAP)
    proj = call(gate_kernel, [ANY] * 3, [(NPJ, PIECES, LANES)], (came, note_came, projectors[0]), flops=10**6, name="gate", passed=1)
    proj_came = send(proj[0], SWAP)
    params, field, pot, xl, xh, inner, outer = call(
        start_kernel,
        [VM] * 6,
        [(16, LANES), grid, (NZ, COLS)] + [packed] * 4,
        (params, ends, keep, came, potential, edge_w),
        stage,
        name="start",
    )
    table = call(
        join_table_kernel, [VM] * 2 + [ANY], (TABLE, LANES), (own_table, note_came, field), flops=10**6, name="join_table"
    )
    head = call(own_kernel, [VM] * 2 + [ANY], (NPJ, NZ, HEAD), (ints, projectors[0], table), name="own")
    tail, index = call(
        prepare_kernel,
        [VM] * 4,
        [(NPJ, NZ, ALL - HEAD), ((4, ALL), jnp.int32)],
        (ints, note_came, projectors[0], proj_came),
        name="prepare",
    )

    sums_room = [pltpu.VMEM((ROWS, ALL), F32)]
    before = field
    for level in range(DEG):
        first, last = level == 0, level == DEG - 1
        if not first:
            table = call(
                table_kernel,
                [VM] * 4,
                (TABLE, LANES),
                (index, field, head, tail),
                [pltpu.VMEM((ROWS, ALL), F32), pltpu.VMEM((ORB * NZ, 2 * COLS), BF16)],
                name="table",
            )
        inner_came = send(inner, CORES)
        table_came = send(table, CORES)
        if first:
            half = call(
                first_pair_kernel,
                [VM] * 5,
                (HALF + 8, LANES),
                (params, table, table_came, energies[0], note_came),
                flops=10**6,
                name="pair",
            )
        else:
            half = call(pair_kernel, [VM] * 3, (HALF, LANES), (params, table, table_came), flops=10**6, name="pair")
        half_came = send(half, OUTER)
        xl_came = send(xh, along_z(1))
        xh_came = send(xl, along_z(-1))
        outer_came = send(outer, OUTER)
        acc = call(
            functools.partial(local_kernel, first),
            [VM, ANY] + [VM] * 5,
            grid,
            (params, half, field, before, pot, own_w, ring_w),
            name="local",
        )
        size = (THIRD + 8, LANES) if first else (THIRD, LANES)
        low, high, acc = call(
            first_sum_kernel if first else sum_kernel,
            [VM] * (3 if first else 2) + [ANY],
            [size, size, grid],
            ((params,) if first else ()) + (half, half_came, acc),
            flops=10**6,
            name="sums",
            passed=1,
        )
        below = send(high, along_z(1))
        above = send(low, along_z(-1))
        acc = call(
            functools.partial(halo_kernel, first),
            [VM] * 7,
            grid,
            (params, inner_came, outer_came, xl_came, xh_came, acc, halo_w),
            name="halo",
        )
        if first:
            total, energy, acc = call(
                first_total_kernel,
                [VM] * 5 + [ANY],
                [(HALF, LANES), (HALF, LANES), grid],
                (params, low, high, below, above, acc),
                flops=10**6,
                name="totals",
                passed=1,
            )
        else:
            total, acc = call(
                later_total_kernel,
                [VM] * 6 + [ANY],
                [(HALF, LANES), grid],
                (params, low, high, below, above, energy, acc),
                flops=10**6,
                name="totals",
                passed=1,
            )
        total_came = send(total, CORES)
        args = (params, index, acc, total, total_came, head, tail)
        if not last:
            before, (field, xl, xh, inner, outer) = field, call(
                functools.partial(update_kernel, last),
                [VM] * 8,
                [grid] + [packed] * 4,
                args + (edge_w,),
                sums_room,
                name="update",
            )
        else:
            flat = (ORB, CX, CY * NZ)
            other, result = call(
                functools.partial(update_kernel, last),
                [VM] * 7,
                [flat, grid],
                args,
                sums_room + stage,
                name="finish",
            )
    part = (CX, CY * NZ // 2)
    here_parts, across = call(
        density_kernel,
        [VM] * 2,
        [(2,) + part] * 2,
        (params, result),
        [pltpu.VMEM((CX, CY * NZ), F32)] + stage,
        name="density",
    )
    swapped = send(other, SWAP)
    across_came = lax.ppermute(across, "band", [(0, 1), (1, 0)])
    mine = call(keep_kernel, [VM, VM, ANY], flat, (params, result, across), stage, name="keep")
    quarter, going = call(band_kernel, [VM] * 2, [part] * 2, (here_parts, across_came), flops=10**6, name="band")
    filtered, density = call(
        join_kernel,
        [VM] * 5,
        [(2 * ORB, CX, CY * NZ), part],
        (params, swapped, send(going, SWAP), mine, quarter),
        name="join",
    )
    return filtered[:, None], density[None]


def solution(mesh):
    in_specs = (
        P("band", "dom", None, None),
        P("band"),
        P("dom", None, None),
        P("dom", None, None, None),
        P("dom", None, None),
        P("dom", None),
        P("dom", None),
        P("dom", None),
        P("dom", None),
        P(),
        P(),
    )
    out_specs = (P("band", "dom", None, None), P("dom", None, "band"))
    return jax.shard_map(body, mesh=mesh, in_specs=in_specs, out_specs=out_specs, check_vma=False)
```
